128 devices in a mesh: pipe: 32 (over y, z, core), cross: 4 (over x).
Axes of the slice: x: 4, y: 4, z: 4, core: 2. Of those that a mesh axis runs over, the one named last changes fastest.
Arguments:
- state: float32 [5, 512, 9216], P(None, 'pipe', 'cross')
- face_diffusion: float32 [512, 9216], P('pipe', 'cross')
- courant: float32 [512, 9216], P('pipe', 'cross'), may hold values from -0.5 to 0.5
- cell_mask: int32 [512, 9216], P('pipe', 'cross'), may hold values from 0 to 1, as said below
- ghost_cell: int32 [16384], P(('pipe', 'cross')), may hold values from 0 to 36863, as said below
- ghost_owner: int32 [16384], P(('pipe', 'cross')), may hold values from 0 to 127, as said below
- ghost_image: int32 [16384], P(('pipe', 'cross')), may hold values from 0 to 255
- image_base: int32 [32768], P(('pipe', 'cross')), may hold values from 0 to 34462, as said below
- image_weight: float32 [8, 32768], P(None, ('pipe', 'cross')), may hold values from 0 to 0.25
Outputs:
- derivative: float32 [5, 512, 9216], P(None, 'pipe', 'cross')
- segment: float32 [5, 512, 9216], P(None, 'pipe', 'cross')
The draws below stay inside these ranges and needn't reach their ends.
Inputs may be any that keep to these rules, and one draw needn't show every extreme that they name: `ghost_cell`: within one device's 128 entries the places are distinct, each a place of that device's block, and cell_mask is 1 at each of them. `ghost_owner`: A device number. Among one device's 128 ghost cells at most 2 name the same owner; one owner, the same for every device, is named by exactly 2 ghost cells of every device. `image_base`: the base row is at most 14, and the base pencil q has q + 97 inside the device's pencils and q + 1 on the same line of 96 pencils. `cell_mask`: 1 marks a solid cell.
All inputs are finite; a program needn't handle non-finite values.
Results may differ from the reference program's by a relative error of at most 0.0003.
Values sent between devices are 32-bit elements; how exact they have to be, the bound alone decides.
A program may use at most 128 MiB of HBM per device.

```python
import math
import jax
import jax.numpy as jnp
from jax import lax

VARS = 5
L_DEV = 16
PEN_DEV = 2304
LINE = 96
G_DEV = 128
IMG_DEV = 256
AXIAL_ROWS = 512
PEN_TOT = 9216
CAP = 2
GHOSTS = 16384
IMAGES = 32768
N_PIPE = 32
N_CROSS = 4


def ghost_layout(key):
    devices = N_PIPE * N_CROSS
    cell_total = L_DEV * PEN_DEV
    places = jnp.arange(cell_total, dtype=jnp.int32)[None, :]
    priority = jax.random.randint(jax.random.fold_in(key, 101), (devices, cell_total), 0, 1 << 14) * cell_total + places
    edge_place = (places == 0) | (places == cell_total - 1)
    priority = jnp.where(edge_place, places - cell_total, priority)
    ordering = jnp.argsort(priority, axis=1)
    return ordering[:, :G_DEV].astype(jnp.int32)


def draw_ghost_cell(key, part):
    chosen = ghost_layout(key)
    return chosen.reshape(-1)


def draw_cell_mask(key, part):
    chosen = ghost_layout(key)
    key = jax.random.fold_in(key, 5)
    devices = N_PIPE * N_CROSS
    solid_cells = (jax.random.randint(key, (devices, L_DEV * PEN_DEV), 0, 8) == 0).astype(jnp.int32)
    solid_cells = solid_cells.at[jnp.arange(devices)[:, None], chosen].set(1)
    return solid_cells.reshape(N_PIPE, N_CROSS, L_DEV, PEN_DEV).transpose(0, 2, 1, 3).reshape(AXIAL_ROWS, PEN_TOT)


def draw_ghost_owner(key, part):
    key = jax.random.fold_in(key, 7)
    random_subkeys = jax.random.split(key, 5)
    devices = N_PIPE * N_CROSS
    busiest = jax.random.randint(random_subkeys[0], (), 0, devices)
    popular = jax.random.randint(random_subkeys[1], (devices,), 0, 4 * devices)
    jitter = jax.random.randint(random_subkeys[2], (devices, devices), 0, 4 * devices)
    candidates = jnp.arange(devices, dtype=jnp.int32)
    priority = (popular[None, :] + jitter) * (2 * devices) + candidates[None, :] + jnp.where(candidates == busiest, 16 * devices * devices, 0)[None, :]
    ordering = jnp.argsort(priority, axis=1)[:, :devices - 1]
    counts = jax.random.randint(random_subkeys[3], (devices, devices - 1), CAP // 2, CAP + 1)
    count_ends = jnp.cumsum(counts, axis=1)
    positions = jnp.arange(G_DEV - CAP, dtype=jnp.int32)
    picked_rank = jax.vmap(lambda ends_row: jnp.searchsorted(ends_row, positions, side='right'))(count_ends)
    remaining = jnp.take_along_axis(ordering, picked_rank, axis=1)
    owners = jnp.concatenate([jnp.broadcast_to(busiest, (devices, CAP)).astype(jnp.int32), remaining.astype(jnp.int32)], axis=1)
    shuffle = jnp.argsort(jax.random.randint(random_subkeys[4], (devices, G_DEV), 0, 1 << 16) * G_DEV + jnp.arange(G_DEV, dtype=jnp.int32)[None, :], axis=1)
    return jnp.take_along_axis(owners, shuffle, axis=1).reshape(-1).astype(jnp.int32)


def draw_image_base(key, part):
    key = jax.random.fold_in(key, 9)
    random_subkeys = jax.random.split(key, 3)
    devices = N_PIPE * N_CROSS
    base_row = jax.random.randint(random_subkeys[0], (devices, IMG_DEV), 0, L_DEV - 1)
    line_number = jax.random.randint(random_subkeys[1], (devices, IMG_DEV), 0, PEN_DEV // LINE - 1)
    line_spot = jax.random.randint(random_subkeys[2], (devices, IMG_DEV), 0, LINE - 1)
    bases = base_row * PEN_DEV + line_number * LINE + line_spot
    slot = jnp.arange(IMG_DEV, dtype=jnp.int32)[None, :]
    highest = (L_DEV - 1) * PEN_DEV - LINE - 2
    bases = jnp.where(slot == 0, 0, jnp.where(slot == 1, highest, bases))
    return bases.reshape(-1).astype(jnp.int32)


def draw_state(key, part):
    key = jax.random.fold_in(key, 11)
    random_subkeys = jax.random.split(key, 1)
    shape = (VARS, AXIAL_ROWS, PEN_TOT)
    return jax.random.normal(random_subkeys[0], shape, jnp.float32)


def draw_face_diffusion(key, part):
    key = jax.random.fold_in(key, 13)
    random_subkeys = jax.random.split(key, 5)
    lowest = L_DEV / 2.0
    highest = AXIAL_ROWS / 2.0
    pencil_rate = jnp.exp(jax.random.uniform(random_subkeys[0], (1, PEN_TOT), jnp.float32, math.log(lowest), math.log(highest)))
    slab_factor = jnp.exp(jax.random.uniform(random_subkeys[1], (N_PIPE, 1, PEN_TOT), jnp.float32, -0.7, 0.7))
    slab_rows = jnp.broadcast_to(slab_factor, (N_PIPE, L_DEV, PEN_TOT)).reshape(AXIAL_ROWS, PEN_TOT)
    roughness = jnp.exp(jax.random.uniform(random_subkeys[2], (AXIAL_ROWS, PEN_TOT), jnp.float32, -0.7, 0.7))
    cluster_positions = jax.random.randint(random_subkeys[3], (4,), 0, AXIAL_ROWS)
    row_location = lax.broadcasted_iota(jnp.int32, (AXIAL_ROWS, 1), 0)
    cluster_rows = jnp.any(row_location == cluster_positions[None, :], axis=1, keepdims=True)
    split_factor = jnp.where(cluster_rows, jnp.exp(jax.random.uniform(random_subkeys[4], (AXIAL_ROWS, 1), jnp.float32, -6.0, -4.0)), 1.0)
    return pencil_rate * pencil_rate * slab_rows * roughness * split_factor


def with_ends(drawn, key, smallest, top_value):
    index_at = [jax.random.randint(jax.random.fold_in(key, axis), (), 0, length) for axis, length in enumerate(drawn.shape)]
    widest = drawn.shape.index(max(drawn.shape))
    next_to = index_at[:widest] + [(index_at[widest] + 1) % drawn.shape[widest]] + index_at[widest + 1:]
    return drawn.at[tuple(index_at)].set(smallest).at[tuple(next_to)].set(top_value)


def shard_levels(rng, dims, pieces, smallest, largest):
    gain = 1.0
    for axis_at, parts in pieces:
        steps = jax.random.uniform(jax.random.fold_in(jax.random.fold_in(rng, 6), axis_at), (parts,), jnp.float32, smallest / len(pieces), largest / len(pieces))
        gain = gain * jnp.repeat(jnp.exp(steps), dims[axis_at] // parts).reshape((-1,) + (1,) * (len(dims) - 1 - axis_at))
    return gain


def setup_inputs(seed: int = 0) -> dict:
    key_of = jax.random.split(jax.random.key(seed), 10)
    return {
        "state": draw_state(jax.random.fold_in(key_of[9], 71), 0),
        "face_diffusion": draw_face_diffusion(jax.random.fold_in(key_of[9], 71), 0),
        "courant": jnp.clip(jax.random.uniform(key_of[2], (AXIAL_ROWS, PEN_TOT), jnp.float32, -0.5, 0.5) * shard_levels(key_of[2], (AXIAL_ROWS, PEN_TOT), ((0, 32), (1, 4)), -0.4, 0.0), -0.5, 0.5),
        "cell_mask": draw_cell_mask(jax.random.fold_in(key_of[9], 71), 0),
        "ghost_cell": draw_ghost_cell(jax.random.fold_in(key_of[9], 71), 0),
        "ghost_owner": draw_ghost_owner(jax.random.fold_in(key_of[9], 71), 0),
        "ghost_image": with_ends(jax.random.randint(key_of[6], (GHOSTS,), 0, IMG_DEV), jax.random.fold_in(key_of[6], 1), 0, IMG_DEV - 1).astype(jnp.int32),
        "image_base": draw_image_base(jax.random.fold_in(key_of[9], 71), 0),
        "image_weight": jnp.clip(0.25 * jax.random.uniform(key_of[8], (8, IMAGES), jnp.float32) ** shard_levels(key_of[8], (8, IMAGES), ((1, 128),), -0.2, 0.2), 0.0, 0.25),
    }


REFLECT = (1.0, -1.0, -1.0, -1.0, 1.0)


def corner_offsets(pencils):
    return jnp.array([0, 1, LINE, LINE + 1, pencils, pencils + 1, pencils + LINE, pencils + LINE + 1], jnp.int32)


def combine(panels, lower_rows, upper_rows, has_lower, has_upper):
    lower_diag = jnp.where(has_lower, lower_rows[1], 1.0)
    upper_diag = jnp.where(has_upper, upper_rows[1], 1.0)
    lower_ratio = panels[0] / lower_diag
    upper_ratio = panels[2] / upper_diag
    new_lower = -lower_ratio * lower_rows[0]
    new_upper = -upper_ratio * upper_rows[2]
    new_margin = panels[3] - lower_ratio * lower_rows[3] - upper_ratio * upper_rows[3]
    new_diag = new_margin - new_lower - new_upper
    new_rhs = panels[4:] - lower_ratio * lower_rows[4:] - upper_ratio * upper_rows[4:]
    return jnp.concatenate([jnp.stack([new_lower, new_diag, new_upper, new_margin]), new_rhs], axis=0)


def shifted_level(panels, stride, row_index, row_total):
    row_count = panels.shape[1]
    zero_rows = jnp.zeros((panels.shape[0], stride, panels.shape[2]), panels.dtype)
    lower_rows = jnp.concatenate([zero_rows, panels[:, :row_count - stride]], axis=1)
    upper_rows = jnp.concatenate([panels[:, stride:], zero_rows], axis=1)
    return combine(panels, lower_rows, upper_rows, row_index >= stride, row_index < row_total - stride)


def pencil_solve(panels):
    row_total = panels.shape[1]
    row_index = lax.broadcasted_iota(jnp.int32, (row_total, 1), 0)
    stride = 1
    while stride < row_total:
        panels = shifted_level(panels, stride, row_index, row_total)
        stride = stride * 2
    return panels[4:] / panels[1]


def explicit_terms(padded, row_index, row_total):
    centre = padded[:, 2:-2]
    minus_one = padded[:, 1:-3]
    plus_one = padded[:, 3:-1]
    minus_two = padded[:, :-4]
    plus_two = padded[:, 4:]
    inner_terms = (7.0 / 9.0) * (plus_one - minus_one) + (1.0 / 36.0) * (plus_two - minus_two)
    near_terms = 0.75 * (plus_one - minus_one)
    first_terms = -1.5 * centre + 2.0 * plus_one - 0.5 * plus_two
    final_terms = 1.5 * centre - 2.0 * minus_one + 0.5 * minus_two
    edge_rows = (row_index == 1) | (row_index == row_total - 2)
    return jnp.where(row_index == 0, first_terms, jnp.where(row_index == row_total - 1, final_terms, jnp.where(edge_rows, near_terms, inner_terms)))


def derivative_panels(row_index, row_total, pencils, stencil_terms):
    edge_rows = (row_index == 1) | (row_index == row_total - 2)
    end_rows = (row_index == 0) | (row_index == row_total - 1)
    side_coef = jnp.where(end_rows, 0.0, jnp.where(edge_rows, 0.25, 1.0 / 3.0)) * jnp.ones((1, pencils), jnp.float32)
    margin = 1.0 + side_coef + side_coef
    return jnp.concatenate([jnp.stack([side_coef, jnp.ones_like(side_coef), side_coef, margin]), stencil_terms], axis=0)


def diffusion_panels(face_low, face_here, row_index, row_total, right_terms):
    lower_side = -face_low
    upper_side = -jnp.where(row_index == row_total - 1, 0.0, face_here)
    margin = jnp.ones_like(face_here)
    diagonal = margin - lower_side - upper_side
    return jnp.concatenate([jnp.stack([lower_side, diagonal, upper_side, margin]), right_terms], axis=0)


def to_blocks(field):
    depth = field.shape[0]
    return field.reshape(depth, N_PIPE, L_DEV, N_CROSS, PEN_DEV).transpose(1, 3, 0, 2, 4).reshape(N_PIPE * N_CROSS, depth, L_DEV * PEN_DEV)


def from_blocks(blocks):
    depth = blocks.shape[1]
    return blocks.reshape(N_PIPE, N_CROSS, depth, L_DEV, PEN_DEV).transpose(2, 0, 3, 1, 4).reshape(depth, AXIAL_ROWS, PEN_DEV * N_CROSS)


def blockwise_solve(panels):
    depth = panels.shape[0]
    grouped_rows = panels.reshape(depth, AXIAL_ROWS, N_CROSS, PEN_DEV).transpose(2, 0, 1, 3)
    solved = lax.map(pencil_solve, grouped_rows)
    return solved.transpose(1, 2, 0, 3).reshape(depth - 4, AXIAL_ROWS, N_CROSS * PEN_DEV)


def image_terms(block_data, corner_cells, corner_weight):
    picked = block_data[:, corner_cells]
    return jnp.sum(picked * corner_weight[None], axis=1)


def fill_block(block_data, solid_flags, cell_list, cell_values):
    cleared = jnp.where(solid_flags[None] == 1, 0.0, block_data)
    return cleared.at[:, cell_list].set(cell_values)


def reference(state, face_diffusion, courant, cell_mask, ghost_cell, ghost_owner, ghost_image, image_base, image_weight):
    devices = N_PIPE * N_CROSS
    blocks = to_blocks(state)
    corners = image_base.reshape(devices, 1, IMG_DEV) + corner_offsets(PEN_DEV)[None, :, None]
    weights = image_weight.reshape(8, devices, IMG_DEV).transpose(1, 0, 2)
    image_values = jax.vmap(image_terms)(blocks, corners, weights)
    all_images = image_values.transpose(1, 0, 2).reshape(VARS, devices * IMG_DEV)
    reflection = jnp.array(REFLECT, jnp.float32)[:, None]
    ghost_values = reflection * all_images[:, ghost_owner * IMG_DEV + ghost_image]
    solid_blocks = to_blocks(cell_mask[None])[:, 0]
    ghost_blocks = ghost_cell.reshape(devices, G_DEV)
    value_blocks = ghost_values.reshape(VARS, devices, G_DEV).transpose(1, 0, 2)
    filled = from_blocks(jax.vmap(fill_block)(blocks, solid_blocks, ghost_blocks, value_blocks))
    row_index = lax.broadcasted_iota(jnp.int32, (AXIAL_ROWS, 1), 0)
    padded = jnp.pad(filled, ((0, 0), (2, 2), (0, 0)))
    stencil_terms = explicit_terms(padded, row_index, AXIAL_ROWS)
    derivative = blockwise_solve(derivative_panels(row_index, AXIAL_ROWS, PEN_DEV * N_CROSS, stencil_terms))
    rhs_two = filled - courant[None] * derivative
    face_low = jnp.pad(face_diffusion, ((1, 0), (0, 0)))[:-1]
    segment = blockwise_solve(diffusion_panels(face_low, face_diffusion, row_index, AXIAL_ROWS, rhs_two))
    return derivative, segment
```

```python
import functools

import jax
import jax.numpy as jnp
import numpy as np
from jax import lax
from jax.experimental import pallas as pl
from jax.experimental.pallas import tpu as pltpu
from jax.sharding import PartitionSpec as P

VARS = 5
ROWS = 16
GHOSTS = 128
IMAGES = 256
UNITS = 3
REFLECT = (1.0, -1.0, -1.0, -1.0, 1.0)
F32 = jnp.float32
I32 = jnp.int32
MESH = pl.DeviceIdType.MESH

T_R = 0
T_S = 17
T_K = 34
T_U = 52
T_V = 68
T_H0 = 84
T_H1 = 87
T_H14 = 91
T_H15 = 95
T_D0, T_D15, T_DL, T_DR = 98, 99, 100, 101


def derivative_constants(slabs):
    n = slabs * ROWS
    side = np.full(n, 1.0 / 3.0)
    side[1] = side[n - 2] = 0.25
    side[0] = side[n - 1] = 0.0
    delta, eps = np.ones(n), np.ones(n)
    for k in range(n - 2, -1, -1):
        delta[k] = 1.0 - side[k] * side[k + 1] / delta[k + 1]
    for k in range(1, n):
        eps[k] = 1.0 - side[k] * side[k - 1] / eps[k - 1]
    r, s, e = -side / delta, -side / eps, 1.0 / (delta + eps - 1.0)

    def at(x, i):
        return x[i] if 0 <= i < n else 0.0

    table = np.zeros((slabs, 128))
    decay_l, decay_r = np.zeros(slabs), np.zeros(slabs)
    for p in range(slabs):
        g = p * ROWS
        row = table[p]
        kappa = {k: 25.0 / 36.0 * at(e, g + k) for k in range(-1, ROWS + 1)}
        for k in range(0, ROWS + 1):
            row[T_R + k] = at(r, g + k)
        for k in range(-1, ROWS):
            row[T_S + k + 1] = at(s, g + k)
        for k in range(-1, ROWS + 1):
            row[T_K + k + 1] = kappa[k]
        u = v = 1.0
        for k in range(ROWS):
            u = u * at(r, g + k) if k else 1.0
            row[T_U + k] = u
        for k in range(ROWS - 1, -1, -1):
            v = v * at(s, g + k) if k < ROWS - 1 else 1.0
            row[T_V + k] = v
        decay_l[p] = u * at(r, g + ROWS)
        decay_r[p] = v * at(s, g - 1)
        row[T_H0 : T_H0 + 3] = (0.0, kappa[0], 0.0)
        row[T_H1 : T_H1 + 4] = (-kappa[1], 0.0, kappa[1], 0.0)
        row[T_H14 : T_H14 + 4] = (0.0, -kappa[14], 0.0, kappa[14])
        row[T_H15 : T_H15 + 3] = (0.0, -kappa[15], 0.0)
        row[T_D0] = row[T_D15] = row[T_DR] = 1.0 / 12.0
        row[T_DL] = -1.0 / 12.0
        if p == 0:
            row[T_H0 : T_H0 + 3] = e[0] * np.array((-1.5, 2.0, -0.5))
            row[T_H1 : T_H1 + 4] = e[1] * np.array((-2.0 / 3.0, 1.0 / 48.0, 2.0 / 3.0, -1.0 / 48.0))
            row[T_D0] = row[T_DL] = 0.0
        if p == slabs - 1:
            row[T_H15 : T_H15 + 3] = e[n - 1] * np.array((0.5, -2.0, 1.5))
            row[T_H14 : T_H14 + 4] = e[n - 2] * np.array((1.0 / 48.0, -2.0 / 3.0, -1.0 / 48.0, 2.0 / 3.0))
            row[T_D15] = row[T_DR] = 0.0
    carry = np.zeros((2 * slabs, slabs))
    for p in range(slabs):
        w = 1.0
        for q in range(p - 1, -1, -1):
            carry[p, q] = w
            w *= decay_l[q]
        w = 1.0
        for q in range(p + 1, slabs):
            carry[slabs + p, q] = w
            w *= decay_r[q]
    return table.astype(np.float32), carry.astype(np.float32)


def image_kernel(tiles, base_s, base_v, state, wts, table, xbuf, win, stage):
    tp = tiles + 1
    magic = -(-65536 // tiles)

    def al(x):
        return pl.multiple_of(x, 8)

    for r in range(ROWS):
        xbuf[pl.ds((r * tp + tiles) * 8, 8), :] = jnp.zeros((8, 128), F32)
    for rt in range(2):
        for lt in range(tiles):
            for v in range(VARS):
                xbuf[pl.ds((rt * 8 * tp + lt) * 8 + v, 8, stride=tp * 8), :] = state[
                    v, pl.ds(rt * 8, 8), pl.ds(lt * 128, 128)
                ]

    lane = lax.broadcasted_iota(I32, (8, 128), 1)
    spot = jnp.broadcast_to((base_v[...] & 127).astype(F32), (8, IMAGES)).T
    cols8 = wts[...].T
    for g in range(IMAGES // 8):
        here = spot[g * 8 : g * 8 + 8, 0:1].astype(I32)
        rel = (lane - here) & 127
        w = [jnp.broadcast_to(cols8[g * 8 : g * 8 + 8, k : k + 1], (8, 128)) for k in range(8)]
        for row in range(2):
            m = jnp.zeros((8, 128), F32)
            for k, off in enumerate((0, 1, 96, 97)):
                m = jnp.where(rel == off, w[row * 4 + k], m)
            win[pl.ds(row * IMAGES + g * 8, 8), :] = m

    def image_group(g, _):
        m0 = win[pl.ds(al(g * 8), 8), :]
        m1 = win[pl.ds(al(IMAGES + g * 8), 8), :]
        for k in range(8):
            b = base_s[0, g * 8 + k]
            x = b >> 7
            r = (x * magic) >> 16
            off = al((r * tp + x - r * tiles) * 8)
            inside = lane >= (b & 127)
            z0 = jnp.where(inside, xbuf[pl.ds(off, 8), :], xbuf[pl.ds(al(off + 8), 8), :])
            z1 = jnp.where(
                inside, xbuf[pl.ds(al(off + tp * 8), 8), :], xbuf[pl.ds(al(off + tp * 8 + 8), 8), :]
            )
            stage[pl.ds(al((g * 8 + k) * 8), 8), :] = z0 * m0[k : k + 1, :] + z1 * m1[k : k + 1, :]
        return 0

    lax.fori_loop(0, IMAGES // 8, image_group, 0)

    def half_sum(h, _):
        def node(level, i):
            if level == 0:
                return stage[pl.ds(al((h * 128 + i) * 8), 8), :]
            a = node(level - 1, i)
            b = node(level - 1, i + (128 >> level))
            bit = level - 1
            low = ((lane >> bit) & 1) == 0
            return jnp.where(low, a, b) + pltpu.roll(jnp.where(low, b, a), 128 - (1 << bit), axis=1)

        table[pl.ds(al(h * 8), 8), :] = node(7, 0)
        return 0

    lax.fori_loop(0, 2, half_sum, 0)


def kernel(
    slabs, cross, tiles,
    tab, lam, table, state, phi, cour, mask, gcell, gown, gimg,
    der, seg,
    tabs, req, pick_out, pick_in, gmap, fbuf, xrow, srow, crow, arow,
    coef_out, coef_in, fac, dat_out, dat_in, ret_out, ret_in, halo_out, halo_in,
    send_sem, recv_sem,
):
    p = lax.axis_index("pipe")
    c = lax.axis_index("cross")
    yz, core = p // 2, p % 2
    planes = slabs // 2
    slot = c * 2 + core
    slots = cross * 2
    magic = -(-65536 // tiles)
    groups = tiles // 3
    solvers = -(-(VARS * tiles) // UNITS)
    is_solver = p < solvers

    def send(src, dst, sem, dev):
        pltpu.make_async_remote_copy(
            src_ref=src,
            dst_ref=dst,
            send_sem=send_sem.at[sem],
            recv_sem=recv_sem.at[sem],
            device_id=dev,
            device_id_type=MESH,
        ).start()

    def wait(sems, sem, ref, rows):
        part = ref.at[pl.ds(0, rows), :]
        pltpu.make_async_copy(part, part, sems.at[sem]).wait()

    def al(x):
        return pl.multiple_of(x, 8)

    barrier = pltpu.get_barrier_semaphore()

    def greet(i, _):
        pl.semaphore_signal(barrier, inc=1, device_id=(lax.rem(p + i, slabs), c), device_id_type=MESH)
        return 0

    lax.fori_loop(1, slabs, greet, 0)
    for dc in range(1, cross):
        for k in range(2):
            pl.semaphore_signal(
                barrier, inc=1, device_id=(yz * 2 + k, lax.rem(c + dc, cross)), device_id_type=MESH
            )

    for rt in range(2):
        for lt in range(tiles):
            cols = pl.ds(lt * 128, 128)
            rows = pl.ds(rt * 8, 8)
            solid = mask[rows, cols] == 1
            place = (lt % 3) * 8 + lt // 3
            for v in range(VARS):
                nat = state[v, rows, cols]
                fbuf[pl.ds((v * ROWS + rt * 8) * 24 + place, 8, stride=24), :] = jnp.where(solid, 0.0, nat)
            crow[pl.ds(rt * 8 * 24 + place, 8, stride=24), :] = cour[rows, cols]
            arow[pl.ds(rt * 8 * 24 + place, 8, stride=24), :] = phi[rows, cols]

    tabs[pl.ds(al(slot * 16), 16), :] = table[...]

    req[pl.ds(al(yz * 8), 8), :] = jnp.concatenate(
        [gown[...], gimg[...], jnp.zeros((6, GHOSTS), I32)], axis=0
    )

    pl.semaphore_wait(barrier, slabs - 1 + (cross - 1) * 2)

    for dc in range(cross):
        for dk in range(2):
            if dc or dk:
                send(
                    tabs.at[pl.ds(al(slot * 16), 16), :],
                    tabs.at[pl.ds(al(slot * 16), 16), :],
                    0,
                    (yz * 2 + lax.rem(core + dk, 2), lax.rem(c + dc, cross)),
                )

    def send_req(i, _):
        mine = pl.ds(al(yz * 8), 8)
        send(req.at[mine, :], req.at[mine, :], 1, (lax.rem(yz + i, planes) * 2 + core, c))
        return 0

    lax.fori_loop(1, planes, send_req, 0)

    cell = gcell[...]
    x = cell >> 7
    r = (x * magic) >> 16
    t = x - r * tiles
    t3 = (t * 21846) >> 16
    at_row = r * 24 + (t - t3 * 3) * 8 + t3
    ghost_no = (lax.broadcasted_iota(I32, (1, GHOSTS), 1) + 1).astype(F32)
    row_no = lax.broadcasted_iota(I32, (ROWS * 24, GHOSTS), 0)
    left = jnp.where(row_no == at_row, ghost_no, 0.0).astype(jnp.bfloat16)
    lane_no = lax.broadcasted_iota(I32, (128, GHOSTS), 0)
    right = jnp.where(lane_no == (cell & 127), 1.0, 0.0).astype(jnp.bfloat16)
    numbers = lax.dot_general(left, right, (((1,), (1,)), ((), ())), preferred_element_type=F32)
    gmap[...] = (numbers + 0.5).astype(I32) - 1

    def rowof(ref, i):
        return ref[pl.ds(i * 24, 24), :]

    def put(ref, i, val):
        ref[pl.ds(i * 24, 24), :] = val

    E, H, RD, WL, WR, C = 0, 16, 32, 48, 64, 80
    top = jnp.where(p == slabs - 1, 0.0, 1.0)
    h = rowof(arow, 0)
    m = jnp.ones_like(h)
    m_l = jnp.ones_like(h)
    faces = arow
    for k in range(1, ROWS):
        face = rowof(faces, k)
        if k == ROWS - 1:
            face = face * top
        rd = 1.0 / (h + face + m)
        e = face * rd
        hh = h * rd
        put(arow, 16 + E + k, e)
        put(arow, 16 + H + k, hh)
        put(arow, 16 + RD + k, rd)
        m_l = m_l + m * hh
        h = h * e
        m = 1.0 + m * e
    w_l = jnp.zeros_like(h)
    w_r = jnp.ones_like(h)
    cols = [jnp.zeros_like(h) for _ in range(4)]
    for k in range(ROWS - 1, 0, -1):
        e = rowof(arow, 16 + E + k)
        w_l = rowof(arow, 16 + H + k) + e * w_l
        w_r = e * w_r
        put(arow, 16 + WL + k, w_l)
        put(arow, 16 + WR + k, w_r)
        ck = rowof(crow, k)
        cl, cr = w_l * ck, w_r * ck
        u, v = tab[p, T_U + k], tab[p, T_V + k]
        cols = [cols[0] - u * cl, cols[1] - u * cr, cols[2] - v * cl, cols[3] - v * cr]
        if k == ROWS - 1:
            k1, k2 = -tab[p, T_DR] * cl, -tab[p, T_DR] * cr
    c0 = rowof(crow, 0)
    cols[0] = cols[0] - tab[p, T_U] * c0
    cols[2] = cols[2] - tab[p, T_V] * c0
    fields = [h, m_l, m - 1.0, *cols, -tab[p, T_DL] * c0, k1, k2]
    for k, val in enumerate(fields):
        for b in range(3):
            coef_out[pl.ds(b * 16 + k, 8, stride=48), :] = val[b * 8 : b * 8 + 8, :]

    def first_tile(d):
        return (UNITS * d) // VARS

    def send_coef(i, _):
        d = lax.rem(p + i, slabs)

        @pl.when(d < solvers)
        def _():
            send(
                coef_out.at[pl.ds(al(first_tile(d) * 16), 32), :],
                coef_in.at[pl.ds(al(p * 32), 32), :],
                2,
                (d, c),
            )

        return 0

    lax.fori_loop(1, slabs, send_coef, 0)

    @pl.when(is_solver)
    def _():
        coef_in[pl.ds(al(p * 32), 32), :] = coef_out[pl.ds(al(first_tile(p) * 16), 32), :]

    wait(recv_sem, 0, tabs, (slots - 1) * 16)
    wait(recv_sem, 1, req, (planes - 1) * 8)
    owner = req[pl.ds(0, planes, stride=8), :]
    image = req[pl.ds(1, planes, stride=8), :]
    o_c = lax.rem(owner, cross)
    o_p = lax.div(owner, cross)
    which = jnp.where(
        (o_p >> 1) == yz, (o_c * 2 + (o_p & 1)) * 2 + (image >> 7), jnp.full_like(owner, -1)
    )
    spot7 = jnp.zeros_like(image)
    for bit in range(7):
        spot7 = spot7 | (((image >> bit) & 1) << (6 - bit))
    for n in range(planes):
        idx = jnp.broadcast_to(spot7[n : n + 1, :], (8, 128))
        wh = jnp.broadcast_to(which[n : n + 1, :], (8, 128))
        acc = jnp.zeros((8, 128), F32)
        for k in range(slots * 2):
            got = jnp.take_along_axis(tabs[pl.ds(k * 8, 8), :], idx, axis=1, mode="promise_in_bounds")
            acc = jnp.where(wh == k, got, acc)
        pick_out[pl.ds(n * 8, 8), :] = acc

    def send_pick(i, _):
        n = lax.rem(yz + i, planes)
        send(pick_out.at[pl.ds(al(n * 8), 8), :], pick_in.at[pl.ds(al(yz * 8), 8), :], 3, (n * 2 + core, c))
        return 0

    lax.fori_loop(1, planes, send_pick, 0)
    pick_in[pl.ds(al(yz * 8), 8), :] = pick_out[pl.ds(al(yz * 8), 8), :]

    @pl.when(is_solver)
    def _():
        wait(recv_sem, 2, coef_in, (slabs - 1) * 32)
        for j in range(2):

            def field(k):
                return coef_in[pl.ds(j * 16 + k, slabs, stride=32), :]

            gu = field(0)
            gl = pltpu.roll(gu, 1, axis=0)
            mm = field(1) + pltpu.roll(field(2), 1, axis=0)
            step, s = 0, 1
            while s < slabs:
                rd = 1.0 / (mm + gl + gu)
                pf = gl * pltpu.roll(rd, s, axis=0)
                tf = gu * pltpu.roll(rd, slabs - s, axis=0)
                at0 = ((j * 6 + step) * 2) * slabs
                fac[pl.ds(at0, slabs), :] = pf
                fac[pl.ds(at0 + slabs, slabs), :] = tf
                mm = mm + pf * pltpu.roll(mm, s, axis=0) + tf * pltpu.roll(mm, slabs - s, axis=0)
                gl = pf * pltpu.roll(gl, s, axis=0)
                gu = tf * pltpu.roll(gu, slabs - s, axis=0)
                step, s = step + 1, s * 2
            fac[pl.ds((j * 6 + 5) * 2 * slabs, slabs), :] = 1.0 / (mm + gl + gu)

    wait(recv_sem, 3, pick_in, (planes - 1) * 8)
    ghost = pick_in[pl.ds(0, 8), :]
    for n in range(1, planes):
        ghost = ghost + pick_in[pl.ds(n * 8, 8), :]
    ghost = [jnp.broadcast_to(REFLECT[v] * ghost[v : v + 1, :], (8, 128)) for v in range(VARS)]

    def tv(i):
        return tab[p, i]

    def local(b, _):
        def at(row):
            return pl.ds(al(row * 24 + b * 8), 8)

        def filled(i):
            gi = gmap[at(i), :]
            has = gi >= 0
            idx = jnp.maximum(gi, 0)
            out = []
            for v in range(VARS):
                got = jnp.take_along_axis(ghost[v], idx, axis=1, mode="promise_in_bounds")
                val = jnp.where(has, got, fbuf[at(v * ROWS + i), :])
                fbuf[at(v * ROWS + i), :] = val
                out.append(val)
            return out

        f = [filled(i) for i in range(ROWS)]
        for v in range(VARS):
            fv = [f[i][v] for i in range(ROWS)]
            up = tv(T_K) * fv[0]
            for i in range(ROWS):
                if i == 0:
                    hi = tv(T_H0) * fv[0] + tv(T_H0 + 1) * fv[1] + tv(T_H0 + 2) * fv[2]
                elif i == 1:
                    hi = sum(tv(T_H1 + k) * fv[k] for k in range(4))
                elif i == ROWS - 2:
                    hi = sum(tv(T_H14 + k) * fv[12 + k] for k in range(4))
                elif i == ROWS - 1:
                    hi = sum(tv(T_H15 + k) * fv[13 + k] for k in range(3))
                else:
                    hi = tv(T_K + 1 + i) * (fv[i + 1] - fv[i - 1])
                up = tv(T_R + i) * up + hi
                xrow[at(v * ROWS + i), :] = up
                srow[at(v * ROWS + i), :] = hi
            end = tv(T_K + 1 + ROWS) * fv[ROWS - 1]
            z_l = tv(T_R + ROWS) * up - end
            down = -end
            s_l = s_r = None
            for i in range(ROWS - 1, -1, -1):
                down = tv(T_S + 1 + i) * down
                xi = xrow[at(v * ROWS + i), :] + down
                if i == 0:
                    xi = xi + tv(T_D0) * fv[1]
                elif i == ROWS - 1:
                    xi = xi - tv(T_D15) * fv[ROWS - 2]
                else:
                    xi = xi + (1.0 / 12.0) * (fv[i + 1] - fv[i - 1])
                xrow[at(v * ROWS + i), :] = xi
                down = down + srow[at(v * ROWS + i), :]
                rhs = fv[i] - crow[at(i), :] * xi
                if i:
                    wl, wr = arow[at(16 + WL + i), :], arow[at(16 + WR + i), :]
                    s_l = wl * rhs if s_l is None else s_l + wl * rhs
                    s_r = wr * rhs if s_r is None else s_r + wr * rhs
                else:
                    s_l = s_l + rhs
            z_r = tv(T_S) * down + tv(T_K) * fv[0]
            for k, val in enumerate((z_l, z_r, s_l, s_r, fv[0], fv[ROWS - 1])):
                dat_out[pl.ds((5 * b + v) * 8 + k, 8, stride=120), :] = val
            halo_out[pl.ds(al(v * 24 + b * 8), 8), :] = fv[0]
            halo_out[pl.ds(al(120 + v * 24 + b * 8), 8), :] = fv[ROWS - 1]
        return 0

    lax.fori_loop(0, 3, local, 0)

    def send_dat(i, _):
        d = lax.rem(p + i, slabs)

        @pl.when(d < solvers)
        def _():
            send(
                dat_out.at[pl.ds(al(d * 24), 24), :],
                dat_in.at[pl.ds(al(p * 24), 24), :],
                4,
                (d, c),
            )

        return 0

    lax.fori_loop(1, slabs, send_dat, 0)
    send(halo_out.at[pl.ds(0, 120), :], halo_in.at[pl.ds(0, 120), :], 5, (lax.rem(p + slabs - 1, slabs), c))
    send(halo_out.at[pl.ds(120, 120), :], halo_in.at[pl.ds(120, 120), :], 6, (lax.rem(p + 1, slabs), c))

    @pl.when(is_solver)
    def _():
        dat_in[pl.ds(al(p * 24), 24), :] = dat_out[pl.ds(al(p * 24), 24), :]
        wait(recv_sem, 4, dat_in, (slabs - 1) * 24)

        def data(u, k):
            return dat_in[pl.ds(u * 8 + k, slabs, stride=24), :]

        z_l = jnp.concatenate([data(u, 0) for u in range(UNITS)], axis=1)
        z_r = jnp.concatenate([data(u, 1) for u in range(UNITS)], axis=1)
        hi = lax.Precision.HIGHEST
        c_l = jnp.dot(lam[pl.ds(0, slabs), :], z_l, precision=hi, preferred_element_type=F32)
        c_r = jnp.dot(lam[pl.ds(slabs, slabs), :], z_r, precision=hi, preferred_element_type=F32)
        for u in range(UNITS):
            j = (UNITS * p + u) // VARS - first_tile(p)

            def field(k):
                return coef_in[pl.ds(j * 16 + k, slabs, stride=32), :]

            cl, cr = c_l[:, u * 128 : u * 128 + 128], c_r[:, u * 128 : u * 128 + 128]
            f_up = pltpu.roll(data(u, 4), slabs - 1, axis=0)
            f_dn = pltpu.roll(data(u, 5), 1, axis=0)
            q = data(u, 3) + field(4) * cl + field(6) * cr + field(9) * f_up
            d = data(u, 2) + field(3) * cl + field(5) * cr + field(7) * f_dn + field(8) * f_up
            d = d + pltpu.roll(q, 1, axis=0)
            step, s = 0, 1
            while s < slabs:
                at0 = ((j * 6 + step) * 2) * slabs
                pf = fac[pl.ds(al(at0), slabs), :]
                tf = fac[pl.ds(al(at0 + slabs), slabs), :]
                d = d + pf * pltpu.roll(d, s, axis=0) + tf * pltpu.roll(d, slabs - s, axis=0)
                step, s = step + 1, s * 2
            x = d * fac[pl.ds(al((j * 6 + 5) * 2 * slabs), slabs), :]
            for k, val in enumerate((cl, cr, x, pltpu.roll(x, slabs - 1, axis=0))):
                ret_out[pl.ds(u * 4 + k, slabs, stride=16), :] = val

        def send_ret(i, _):
            d = lax.rem(p + i, slabs)
            send(ret_out.at[pl.ds(al(d * 16), 16), :], ret_in.at[pl.ds(al(p * 16), 16), :], 7, (d, c))
            return 0

        lax.fori_loop(1, slabs, send_ret, 0)
        ret_in[pl.ds(al(p * 16), 16), :] = ret_out[pl.ds(al(p * 16), 16), :]
        wait(recv_sem, 7, ret_in, (solvers - 1) * 16)

    @pl.when(jnp.logical_not(is_solver))
    def _():
        wait(recv_sem, 7, ret_in, solvers * 16)

    wait(recv_sem, 5, halo_in, 120)
    wait(recv_sem, 6, halo_in, 120)

    def finish(b, _):
        def at(row):
            return pl.ds(al(row * 24 + b * 8), 8)

        for v in range(VARS):
            w = 5 * b + v

            def back(k):
                return ret_in[pl.ds((w // 3) * 16 + (w % 3) * 4 + k, 8, stride=80), :]

            left_c, right_c, t0, t1 = back(0), back(1), back(2), back(3)
            above = halo_in[at(v), :]
            below = halo_in[at(5 + v), :]
            run = None
            for i in range(ROWS):
                xi = xrow[at(v * ROWS + i), :] + tv(T_U + i) * left_c + tv(T_V + i) * right_c
                if i == 0:
                    xi = xi + tv(T_DL) * below
                if i == ROWS - 1:
                    xi = xi + tv(T_DR) * above
                xrow[at(v * ROWS + i), :] = xi
                if i:
                    rhs = fbuf[at(v * ROWS + i), :] - crow[at(i), :] * xi
                    run = rhs if run is None else rhs + arow[at(16 + E + i - 1), :] * run
                    srow[at(v * ROWS + i), :] = (
                        arow[at(16 + RD + i), :] * run + arow[at(16 + H + i), :] * t0
                    )
            y = t1
            for i in range(ROWS - 1, 0, -1):
                y = srow[at(v * ROWS + i), :] + arow[at(16 + E + i), :] * y
                srow[at(v * ROWS + i), :] = y
            srow[at(v * ROWS), :] = t0
        return 0

    lax.fori_loop(0, 3, finish, 0)
    for v in range(VARS):
        for rt in range(2):
            for lt in range(tiles):
                src = pl.ds((v * ROWS + rt * 8) * 24 + (lt % 3) * 8 + lt // 3, 8, stride=24)
                der[v, pl.ds(rt * 8, 8), pl.ds(lt * 128, 128)] = xrow[src, :]
                seg[v, pl.ds(rt * 8, 8), pl.ds(lt * 128, 128)] = srow[src, :]

    wait(send_sem, 0, tabs, (slots - 1) * 16)
    wait(send_sem, 1, req, (planes - 1) * 8)
    wait(send_sem, 3, pick_in, (planes - 1) * 8)
    wait(send_sem, 5, halo_in, 120)
    wait(send_sem, 6, halo_in, 120)

    @pl.when(is_solver)
    def _():
        wait(send_sem, 2, coef_in, (solvers - 1) * 32)
        wait(send_sem, 4, dat_in, (solvers - 1) * 24)
        wait(send_sem, 7, ret_out, (slabs - 1) * 16)

    @pl.when(jnp.logical_not(is_solver))
    def _():
        wait(send_sem, 2, coef_in, solvers * 32)
        wait(send_sem, 4, dat_in, solvers * 24)


def solution(mesh):
    slabs, cross = mesh.shape["pipe"], mesh.shape["cross"]
    table, carry = derivative_constants(slabs)

    def local(state, face, courant, cell_mask, ghost_cell, ghost_owner, ghost_image, base, weight):
        pencils = state.shape[2]
        tiles = pencils // 128
        solvers = -(-(VARS * tiles) // UNITS)
        vm = pl.BlockSpec(memory_space=pltpu.VMEM)
        sm = pl.BlockSpec(memory_space=pltpu.SMEM)
        out = jax.ShapeDtypeStruct(state.shape, F32)
        planes, slots = slabs // 2, cross * 2
        span = VARS * ROWS * 24

        def buf(rows, dtype=F32):
            return pltpu.VMEM((rows, 128), dtype)

        base = base.reshape(1, -1)
        images = pl.pallas_call(
            functools.partial(image_kernel, tiles),
            out_shape=jax.ShapeDtypeStruct((16, 128), F32),
            in_specs=[sm, vm, vm, vm],
            out_specs=vm,
            scratch_shapes=[
                buf(ROWS * (tiles + 1) * 8),
                buf(2 * IMAGES),
                buf(IMAGES * 8),
            ],
            compiler_params=pltpu.CompilerParams(vmem_limit_bytes=24 * 1024 * 1024),
        )(base, base, state, weight)
        return pl.pallas_call(
            functools.partial(kernel, slabs, cross, tiles),
            out_shape=(out, out),
            in_specs=[sm] + [vm] * 9,
            out_specs=(vm, vm),
            scratch_shapes=[
                buf(slots * 16),
                buf(planes * 8, I32),
                buf(planes * 8),
                buf(planes * 8),
                buf(ROWS * 24, I32),
                buf(span),
                buf(span),
                buf(span),
                buf(ROWS * 24),
                buf(ROWS * 24 * 6),
                buf(384),
                buf(slabs * 32),
                buf(24 * slabs),
                buf(960),
                buf(slabs * 24),
                buf(slabs * 16),
                buf(max(640, solvers * 16)),
                buf(240),
                buf(240),
                pltpu.SemaphoreType.DMA((8,)),
                pltpu.SemaphoreType.DMA((8,)),
            ],
            compiler_params=pltpu.CompilerParams(
                collective_id=0, has_side_effects=True, vmem_limit_bytes=40 * 1024 * 1024
            ),
        )(
            jnp.asarray(table), jnp.asarray(carry), images,
            state, face, courant, cell_mask,
            ghost_cell.reshape(1, -1), ghost_owner.reshape(1, -1), ghost_image.reshape(1, -1),
        )

    flat = P(("pipe", "cross"))
    slab = P("pipe", "cross")
    whole = P(None, "pipe", "cross")
    return jax.shard_map(
        local,
        mesh=mesh,
        in_specs=(whole, slab, slab, slab, flat, flat, flat, flat, P(None, ("pipe", "cross"))),
        out_specs=(whole, whole),
        check_vma=False,
    )
```

```python
import functools

import jax
import jax.numpy as jnp
import numpy as np
from jax import lax
from jax.experimental import pallas as pl
from jax.experimental.pallas import tpu as pltpu
from jax.sharding import PartitionSpec as P

VARS = 5
ROWS = 16
GHOSTS = 128
IMAGES = 256
UNITS = 3
REFLECT = (1.0, -1.0, -1.0, -1.0, 1.0)
F32 = jnp.float32
I32 = jnp.int32
MESH = pl.DeviceIdType.MESH

T_R = 0
T_S = 17
T_K = 34
T_U = 52
T_V = 68
T_H0 = 84
T_H1 = 87
T_H14 = 91
T_H15 = 95
T_D0, T_D15, T_DL, T_DR = 98, 99, 100, 101


def derivative_constants(slabs):
    n = slabs * ROWS
    side = np.full(n, 1.0 / 3.0)
    side[1] = side[n - 2] = 0.25
    side[0] = side[n - 1] = 0.0
    delta, eps = np.ones(n), np.ones(n)
    for k in range(n - 2, -1, -1):
        delta[k] = 1.0 - side[k] * side[k + 1] / delta[k + 1]
    for k in range(1, n):
        eps[k] = 1.0 - side[k] * side[k - 1] / eps[k - 1]
    r, s, e = -side / delta, -side / eps, 1.0 / (delta + eps - 1.0)

    def at(x, i):
        return x[i] if 0 <= i < n else 0.0

    table = np.zeros((slabs, 128))
    decay_l, decay_r = np.zeros(slabs), np.zeros(slabs)
    for p in range(slabs):
        g = p * ROWS
        row = table[p]
        kappa = {k: 25.0 / 36.0 * at(e, g + k) for k in range(-1, ROWS + 1)}
        for k in range(0, ROWS + 1):
            row[T_R + k] = at(r, g + k)
        for k in range(-1, ROWS):
            row[T_S + k + 1] = at(s, g + k)
        for k in range(-1, ROWS + 1):
            row[T_K + k + 1] = kappa[k]
        u = v = 1.0
        for k in range(ROWS):
            u = u * at(r, g + k) if k else 1.0
            row[T_U + k] = u
        for k in range(ROWS - 1, -1, -1):
            v = v * at(s, g + k) if k < ROWS - 1 else 1.0
            row[T_V + k] = v
        decay_l[p] = u * at(r, g + ROWS)
        decay_r[p] = v * at(s, g - 1)
        row[T_H0 : T_H0 + 3] = (0.0, kappa[0], 0.0)
        row[T_H1 : T_H1 + 4] = (-kappa[1], 0.0, kappa[1], 0.0)
        row[T_H14 : T_H14 + 4] = (0.0, -kappa[14], 0.0, kappa[14])
        row[T_H15 : T_H15 + 3] = (0.0, -kappa[15], 0.0)
        row[T_D0] = row[T_D15] = row[T_DR] = 1.0 / 12.0
        row[T_DL] = -1.0 / 12.0
        if p == 0:
            row[T_H0 : T_H0 + 3] = e[0] * np.array((-1.5, 2.0, -0.5))
            row[T_H1 : T_H1 + 4] = e[1] * np.array((-2.0 / 3.0, 1.0 / 48.0, 2.0 / 3.0, -1.0 / 48.0))
            row[T_D0] = row[T_DL] = 0.0
        if p == slabs - 1:
            row[T_H15 : T_H15 + 3] = e[n - 1] * np.array((0.5, -2.0, 1.5))
            row[T_H14 : T_H14 + 4] = e[n - 2] * np.array((1.0 / 48.0, -2.0 / 3.0, -1.0 / 48.0, 2.0 / 3.0))
            row[T_D15] = row[T_DR] = 0.0
    carry = np.zeros((2 * slabs, slabs))
    for p in range(slabs):
        w = 1.0
        for q in range(p - 1, -1, -1):
            carry[p, q] = w
            w *= decay_l[q]
        w = 1.0
        for q in range(p + 1, slabs):
            carry[slabs + p, q] = w
            w *= decay_r[q]
    return table.astype(np.float32), carry.astype(np.float32)


def kernel(
    slabs, cross, tiles,
    tab_hbm, lam_hbm, base_hbm, state_hbm, phi_hbm, cour_hbm, mask_hbm, gcell_hbm, gown_hbm, gimg_hbm, wts_hbm,
    der, seg,
    tab, base_s, lam, base_v, state, phi, cour, mask, gcell, gown, gimg, wts,
    xbuf, win, stage, tabs, req, pick_out, pick_in, gmap, fbuf, xrow, srow, crow, arow,
    coef_out, coef_in, fac, side_out, side_in, dat_out, dat_in, ret_out, ret_in, halo_out, halo_in,
    in_sem, send_sem, recv_sem,
):
    p = lax.axis_index("pipe")
    c = lax.axis_index("cross")
    yz, core = p // 2, p % 2
    planes = slabs // 2
    slot = c * 2 + core
    slots = cross * 2
    tp = tiles + 1
    magic = -(-65536 // tiles)
    solvers = -(-(VARS * tiles) // UNITS)
    is_solver = p < solvers
    before, after = lax.rem(p + slabs - 1, slabs), lax.rem(p + 1, slabs)

    def fetch(k, src, dst):
        copy = pltpu.make_async_copy(src, dst, in_sem.at[k])
        copy.start()
        return copy

    got_state = fetch(0, state_hbm, state)
    got_base = fetch(1, base_hbm, base_v)
    got_base_s = fetch(2, base_hbm, base_s)
    got_wts = fetch(3, wts_hbm, wts)
    got_rest = [
        fetch(4, mask_hbm, mask),
        fetch(5, phi_hbm, phi),
        fetch(6, cour_hbm, cour),
        fetch(7, gcell_hbm, gcell),
        fetch(8, gown_hbm, gown),
        fetch(9, gimg_hbm, gimg),
        fetch(10, tab_hbm.at[p], tab),
        fetch(11, lam_hbm, lam),
    ]

    def send(src, dst, sem, dev):
        pltpu.make_async_remote_copy(
            src_ref=src,
            dst_ref=dst,
            send_sem=send_sem.at[sem],
            recv_sem=recv_sem.at[sem],
            device_id=dev,
            device_id_type=MESH,
        ).start()

    def wait(sems, sem, ref, rows):
        part = ref.at[pl.ds(0, rows), :]
        pltpu.make_async_copy(part, part, sems.at[sem]).wait()

    def al(x):
        return pl.multiple_of(x, 8)

    barrier = pltpu.get_barrier_semaphore()

    def greet(i, _):
        pl.semaphore_signal(barrier, inc=1, device_id=(lax.rem(p + i, slabs), c), device_id_type=MESH)
        return 0

    lax.fori_loop(1, slabs, greet, 0)
    for dc in range(1, cross):
        for k in range(2):
            pl.semaphore_signal(
                barrier, inc=1, device_id=(yz * 2 + k, lax.rem(c + dc, cross)), device_id_type=MESH
            )

    lane = lax.broadcasted_iota(I32, (8, 128), 1)
    got_base.wait()
    got_wts.wait()
    spot = jnp.broadcast_to((base_v[...] & 127).astype(F32), (8, IMAGES)).T
    cols8 = wts[...].T
    for g in range(IMAGES // 8):
        here = spot[g * 8 : g * 8 + 8, 0:1].astype(I32)
        rel = (lane - here) & 127
        w = [jnp.broadcast_to(cols8[g * 8 : g * 8 + 8, k : k + 1], (8, 128)) for k in range(8)]
        for row in range(2):
            m = jnp.zeros((8, 128), F32)
            for k, off in enumerate((0, 1, 96, 97)):
                m = jnp.where(rel == off, w[row * 4 + k], m)
            win[pl.ds(row * IMAGES + g * 8, 8), :] = m

    for r in range(ROWS):
        xbuf[pl.ds((r * tp + tiles) * 8, 8), :] = jnp.zeros((8, 128), F32)
    got_state.wait()
    for rt in range(2):
        for lt in range(tiles):
            for v in range(VARS):
                nat = state[v, pl.ds(rt * 8, 8), pl.ds(lt * 128, 128)]
                xbuf[pl.ds((rt * 8 * tp + lt) * 8 + v, 8, stride=tp * 8), :] = nat
    got_base_s.wait()
    blocks = xbuf.reshape(ROWS * tp, 8, 128)

    def image_group(g, _):
        m0 = win[pl.ds(al(g * 8), 8), :]
        m1 = win[pl.ds(al(IMAGES + g * 8), 8), :]
        for k in range(8):
            b = base_s[0, g * 8 + k]
            x = b >> 7
            r = (x * magic) >> 16
            off = x + r
            inside = lane >= (b & 127)
            z0 = jnp.where(inside, blocks[off], blocks[off + 1])
            z1 = jnp.where(inside, blocks[off + tp], blocks[off + tp + 1])
            stage[pl.ds(al((g * 8 + k) * 8), 8), :] = z0 * m0[k : k + 1, :] + z1 * m1[k : k + 1, :]
        return 0

    lax.fori_loop(0, IMAGES // 8, image_group, 0)

    def half_sum(h, _):
        def node(level, i):
            if level == 0:
                return stage[pl.ds(al((h * 128 + i) * 8), 8), :]
            a = node(level - 1, i)
            b = node(level - 1, i + (128 >> level))
            bit = level - 1
            low = ((lane >> bit) & 1) == 0
            return jnp.where(low, a, b) + pltpu.roll(jnp.where(low, b, a), 128 - (1 << bit), axis=1)

        tabs[pl.ds(al((slot * 2 + h) * 8), 8), :] = node(7, 0)
        return 0

    lax.fori_loop(0, 2, half_sum, 0)

    for copy in got_rest:
        copy.wait()
    req[pl.ds(al(yz * 8), 8), :] = jnp.concatenate(
        [gown[...], gimg[...], jnp.zeros((6, GHOSTS), I32)], axis=0
    )

    pl.semaphore_wait(barrier, slabs - 1 + (cross - 1) * 2)

    for dc in range(cross):
        for dk in range(2):
            if dc or dk:
                send(
                    tabs.at[pl.ds(al(slot * 16), 16), :],
                    tabs.at[pl.ds(al(slot * 16), 16), :],
                    0,
                    (yz * 2 + lax.rem(core + dk, 2), lax.rem(c + dc, cross)),
                )

    def send_req(i, _):
        mine = pl.ds(al(yz * 8), 8)
        send(req.at[mine, :], req.at[mine, :], 1, (lax.rem(yz + i, planes) * 2 + core, c))
        return 0

    lax.fori_loop(1, planes, send_req, 0)

    for rt in range(2):
        for lt in range(tiles):
            cols = pl.ds(lt * 128, 128)
            rows = pl.ds(rt * 8, 8)
            solid = mask[rows, cols] == 1
            place = (lt % 3) * 8 + lt // 3
            for v in range(VARS):
                fbuf[pl.ds((v * ROWS + rt * 8) * 24 + place, 8, stride=24), :] = jnp.where(
                    solid, 0.0, state[v, rows, cols]
                )
            crow[pl.ds(rt * 8 * 24 + place, 8, stride=24), :] = cour[rows, cols]
            arow[pl.ds(rt * 8 * 24 + place, 8, stride=24), :] = phi[rows, cols]

    cell = gcell[...]
    x = cell >> 7
    r = (x * magic) >> 16
    t = x - r * tiles
    t3 = (t * 21846) >> 16
    at_row = r * 24 + (t - t3 * 3) * 8 + t3
    ghost_no = (lax.broadcasted_iota(I32, (1, GHOSTS), 1) + 1).astype(F32)
    row_no = lax.broadcasted_iota(I32, (ROWS * 24, GHOSTS), 0)
    left = jnp.where(row_no == at_row, ghost_no, 0.0).astype(jnp.bfloat16)
    lane_no = lax.broadcasted_iota(I32, (128, GHOSTS), 0)
    right = jnp.where(lane_no == (cell & 127), 1.0, 0.0).astype(jnp.bfloat16)
    numbers = lax.dot_general(left, right, (((1,), (1,)), ((), ())), preferred_element_type=F32)
    gmap[...] = (numbers + 0.5).astype(I32) - 1

    def rowof(ref, i):
        return ref[pl.ds(i * 24, 24), :]

    def put(ref, i, val):
        ref[pl.ds(i * 24, 24), :] = val

    E, H, RD, WL, WR, C = 0, 16, 32, 48, 64, 80
    top = jnp.where(p == slabs - 1, 0.0, 1.0)
    h = rowof(arow, 0)
    m = jnp.ones_like(h)
    m_l = jnp.ones_like(h)
    faces = arow
    for k in range(1, ROWS):
        face = rowof(faces, k)
        if k == ROWS - 1:
            face = face * top
        rd = 1.0 / (h + face + m)
        e = face * rd
        hh = h * rd
        put(arow, 16 + E + k, e)
        put(arow, 16 + H + k, hh)
        put(arow, 16 + RD + k, rd)
        m_l = m_l + m * hh
        h = h * e
        m = 1.0 + m * e
    w_l = jnp.zeros_like(h)
    w_r = jnp.ones_like(h)
    cols = [jnp.zeros_like(h) for _ in range(4)]
    for k in range(ROWS - 1, 0, -1):
        e = rowof(arow, 16 + E + k)
        w_l = rowof(arow, 16 + H + k) + e * w_l
        w_r = e * w_r
        put(arow, 16 + WL + k, w_l)
        put(arow, 16 + WR + k, w_r)
        ck = rowof(crow, k)
        cl, cr = w_l * ck, w_r * ck
        u, v = tab[0, T_U + k], tab[0, T_V + k]
        cols = [cols[0] - u * cl, cols[1] - u * cr, cols[2] - v * cl, cols[3] - v * cr]
        if k == ROWS - 1:
            k1, k2 = -tab[0, T_DR] * cl, -tab[0, T_DR] * cr
    c0 = rowof(crow, 0)
    cols[0] = cols[0] - tab[0, T_U] * c0
    cols[2] = cols[2] - tab[0, T_V] * c0
    for k, val in enumerate((h, m_l, m - 1.0, *cols)):
        for b in range(3):
            coef_out[pl.ds(b * 8 + k, 8, stride=24), :] = val[b * 8 : b * 8 + 8, :]
    for k, val in enumerate((-tab[0, T_DL] * c0, k1, k2)):
        side_out[pl.ds(k * 24, 24), :] = val

    def first_tile(d):
        return (UNITS * d) // VARS

    def has_two(d):
        return jnp.logical_and(d < solvers, lax.rem(UNITS * d, VARS) > VARS - UNITS)

    n_two = sum((UNITS * d) % VARS > VARS - UNITS for d in range(solvers))

    wait(recv_sem, 0, tabs, (slots - 1) * 16)
    wait(recv_sem, 1, req, (planes - 1) * 8)
    owner = req[pl.ds(0, planes, stride=8), :]
    image = req[pl.ds(1, planes, stride=8), :]
    o_c = lax.rem(owner, cross)
    o_p = lax.div(owner, cross)
    which = jnp.where(
        (o_p >> 1) == yz, (o_c * 2 + (o_p & 1)) * 2 + (image >> 7), jnp.full_like(owner, -1)
    )
    spot7 = jnp.zeros_like(image)
    for bit in range(7):
        spot7 = spot7 | (((image >> bit) & 1) << (6 - bit))
    for n in range(planes):
        idx = jnp.broadcast_to(spot7[n : n + 1, :], (8, 128))
        wh = jnp.broadcast_to(which[n : n + 1, :], (8, 128))
        acc = jnp.zeros((8, 128), F32)
        for k in range(slots * 2):
            got = jnp.take_along_axis(tabs[pl.ds(k * 8, 8), :], idx, axis=1, mode="promise_in_bounds")
            acc = jnp.where(wh == k, got, acc)
        pick_out[pl.ds(n * 8, 8), :] = acc

    def send_pick(i, _):
        n = lax.rem(yz + i, planes)
        send(pick_out.at[pl.ds(al(n * 8), 8), :], pick_in.at[pl.ds(al(yz * 8), 8), :], 3, (n * 2 + core, c))
        return 0

    lax.fori_loop(1, planes, send_pick, 0)
    pick_in[pl.ds(al(yz * 8), 8), :] = pick_out[pl.ds(al(yz * 8), 8), :]

    def send_coef(i, _):
        d = lax.rem(p + i, slabs)

        @pl.when(d < solvers)
        def _():
            send(
                coef_out.at[pl.ds(al(first_tile(d) * 8), 8), :],
                coef_in.at[pl.ds(al(p * 16), 8), :],
                2,
                (d, c),
            )

        @pl.when(has_two(d))
        def _():
            send(
                coef_out.at[pl.ds(al(first_tile(d) * 8 + 8), 8), :],
                coef_in.at[pl.ds(al(p * 16 + 8), 8), :],
                8,
                (d, c),
            )

        return 0

    send(side_out.at[pl.ds(0, 24), :], side_in.at[pl.ds(0, 24), :], 9, (before, c))
    send(side_out.at[pl.ds(24, 48), :], side_in.at[pl.ds(24, 48), :], 10, (after, c))
    lax.fori_loop(1, slabs, send_coef, 0)

    @pl.when(is_solver)
    def _():
        coef_in[pl.ds(al(p * 16), 16), :] = coef_out[pl.ds(al(first_tile(p) * 8), 16), :]

    wait(recv_sem, 3, pick_in, (planes - 1) * 8)
    ghost = pick_in[pl.ds(0, 8), :]
    for n in range(1, planes):
        ghost = ghost + pick_in[pl.ds(n * 8, 8), :]
    ghost = [jnp.broadcast_to(REFLECT[v] * ghost[v : v + 1, :], (8, 128)) for v in range(VARS)]

    def tv(i):
        return tab[0, i]

    wait(recv_sem, 9, side_in, 24)
    wait(recv_sem, 10, side_in, 48)

    def send_class(k):
        def one(i, _):
            d = 5 * lax.rem(p + i, tiles // 3) + k

            @pl.when(d != p)
            def _():
                send(
                    dat_out.at[pl.ds(al(d * 16), 16), :],
                    dat_in.at[pl.ds(al(p * 16), 16), :],
                    4,
                    (d, c),
                )

            return 0

        lax.fori_loop(0, tiles // 3, one, 0)

    def local(b, _):
        def at(row):
            return pl.ds(al(row * 24 + b * 8), 8)

        def filled(i):
            gi = gmap[at(i), :]
            has = gi >= 0
            idx = jnp.maximum(gi, 0)
            out = []
            for v in range(VARS):
                got = jnp.take_along_axis(ghost[v], idx, axis=1, mode="promise_in_bounds")
                val = jnp.where(has, got, fbuf[at(v * ROWS + i), :])
                fbuf[at(v * ROWS + i), :] = val
                out.append(val)
            return out

        f = [filled(i) for i in range(ROWS)]
        for v in range(VARS):
            fv = [f[i][v] for i in range(ROWS)]
            up = tv(T_K) * fv[0]
            for i in range(ROWS):
                if i == 0:
                    hi = tv(T_H0) * fv[0] + tv(T_H0 + 1) * fv[1] + tv(T_H0 + 2) * fv[2]
                elif i == 1:
                    hi = sum(tv(T_H1 + k) * fv[k] for k in range(4))
                elif i == ROWS - 2:
                    hi = sum(tv(T_H14 + k) * fv[12 + k] for k in range(4))
                elif i == ROWS - 1:
                    hi = sum(tv(T_H15 + k) * fv[13 + k] for k in range(3))
                else:
                    hi = tv(T_K + 1 + i) * (fv[i + 1] - fv[i - 1])
                up = tv(T_R + i) * up + hi
                xrow[at(v * ROWS + i), :] = up
                srow[at(v * ROWS + i), :] = hi
            end = tv(T_K + 1 + ROWS) * fv[ROWS - 1]
            z_l = tv(T_R + ROWS) * up - end
            down = -end
            s_l = s_r = None
            for i in range(ROWS - 1, -1, -1):
                down = tv(T_S + 1 + i) * down
                xi = xrow[at(v * ROWS + i), :] + down
                if i == 0:
                    xi = xi + tv(T_D0) * fv[1]
                elif i == ROWS - 1:
                    xi = xi - tv(T_D15) * fv[ROWS - 2]
                else:
                    xi = xi + (1.0 / 12.0) * (fv[i + 1] - fv[i - 1])
                xrow[at(v * ROWS + i), :] = xi
                down = down + srow[at(v * ROWS + i), :]
                rhs = fv[i] - crow[at(i), :] * xi
                if i:
                    wl, wr = arow[at(16 + WL + i), :], arow[at(16 + WR + i), :]
                    s_l = wl * rhs if s_l is None else s_l + wl * rhs
                    s_r = wr * rhs if s_r is None else s_r + wr * rhs
                else:
                    s_l = s_l + rhs
            z_r = tv(T_S) * down + tv(T_K) * fv[0]
            s_r = s_r + side_in[at(0), :] * fv[ROWS - 1]
            s_b = side_in[at(1), :] * fv[0]
            s_l = s_l + side_in[at(2), :] * fv[0]
            w = 5 * b + v
            for k, val in enumerate((z_l, z_r, s_l, s_r, s_b)):
                dat_out[pl.ds((w // 3) * 16 + (w % 3) * 5 + k, 8, stride=80), :] = val
            halo_out[pl.ds(al(v * 24 + b * 8), 8), :] = fv[0]
            halo_out[pl.ds(al(120 + v * 24 + b * 8), 8), :] = fv[ROWS - 1]
        send_class(2 * b)

        @pl.when(b > 0)
        def _():
            send_class(2 * b - 1)

        return 0

    lax.fori_loop(0, 3, local, 0)

    send(halo_out.at[pl.ds(0, 120), :], halo_in.at[pl.ds(0, 120), :], 5, (before, c))
    send(halo_out.at[pl.ds(120, 120), :], halo_in.at[pl.ds(120, 120), :], 6, (after, c))

    @pl.when(is_solver)
    def _():
        wait(recv_sem, 2, coef_in, (slabs - 1) * 8)

        @pl.when(has_two(p))
        def _():
            wait(recv_sem, 8, coef_in, (slabs - 1) * 8)

        for j in range(2):

            def field(k):
                return coef_in[pl.ds(j * 8 + k, slabs, stride=16), :]

            gu = field(0)
            gl = pltpu.roll(gu, 1, axis=0)
            mm = field(1) + pltpu.roll(field(2), 1, axis=0)
            step, s = 0, 1
            while s < slabs:
                rd = 1.0 / (mm + gl + gu)
                pf = gl * pltpu.roll(rd, s, axis=0)
                tf = gu * pltpu.roll(rd, slabs - s, axis=0)
                at0 = ((j * 6 + step) * 2) * slabs
                fac[pl.ds(at0, slabs), :] = pf
                fac[pl.ds(at0 + slabs, slabs), :] = tf
                mm = mm + pf * pltpu.roll(mm, s, axis=0) + tf * pltpu.roll(mm, slabs - s, axis=0)
                gl = pf * pltpu.roll(gl, s, axis=0)
                gu = tf * pltpu.roll(gu, slabs - s, axis=0)
                step, s = step + 1, s * 2
            fac[pl.ds((j * 6 + 5) * 2 * slabs, slabs), :] = 1.0 / (mm + gl + gu)

    @pl.when(is_solver)
    def _():
        dat_in[pl.ds(al(p * 16), 16), :] = dat_out[pl.ds(al(p * 16), 16), :]
        wait(recv_sem, 4, dat_in, (slabs - 1) * 16)

        def data(u, k):
            return dat_in[pl.ds(u * 5 + k, slabs, stride=16), :]

        z_l = jnp.concatenate([data(u, 0) for u in range(UNITS)], axis=1)
        z_r = jnp.concatenate([data(u, 1) for u in range(UNITS)], axis=1)
        hi = lax.Precision.HIGHEST
        c_l = jnp.dot(lam[pl.ds(0, slabs), :], z_l, precision=hi, preferred_element_type=F32)
        c_r = jnp.dot(lam[pl.ds(slabs, slabs), :], z_r, precision=hi, preferred_element_type=F32)
        for u in range(UNITS):
            j = (UNITS * p + u) // VARS - first_tile(p)

            def field(k):
                return coef_in[pl.ds(j * 8 + k, slabs, stride=16), :]

            cl, cr = c_l[:, u * 128 : u * 128 + 128], c_r[:, u * 128 : u * 128 + 128]
            q = data(u, 3) + field(4) * cl + field(6) * cr
            d = data(u, 2) + field(3) * cl + field(5) * cr + pltpu.roll(data(u, 4), slabs - 1, axis=0)
            d = d + pltpu.roll(q, 1, axis=0)
            step, s = 0, 1
            while s < slabs:
                at0 = ((j * 6 + step) * 2) * slabs
                pf = fac[pl.ds(al(at0), slabs), :]
                tf = fac[pl.ds(al(at0 + slabs), slabs), :]
                d = d + pf * pltpu.roll(d, s, axis=0) + tf * pltpu.roll(d, slabs - s, axis=0)
                step, s = step + 1, s * 2
            x = d * fac[pl.ds(al((j * 6 + 5) * 2 * slabs), slabs), :]
            for k, val in enumerate((cl, cr, x, pltpu.roll(x, slabs - 1, axis=0))):
                ret_out[pl.ds(u * 4 + k, slabs, stride=16), :] = val

        def send_ret(i, _):
            d = lax.rem(p + i, slabs)
            send(ret_out.at[pl.ds(al(d * 16), 16), :], ret_in.at[pl.ds(al(p * 16), 16), :], 7, (d, c))
            return 0

        lax.fori_loop(1, slabs, send_ret, 0)
        ret_in[pl.ds(al(p * 16), 16), :] = ret_out[pl.ds(al(p * 16), 16), :]
        wait(recv_sem, 7, ret_in, (solvers - 1) * 16)

    @pl.when(jnp.logical_not(is_solver))
    def _():
        wait(recv_sem, 7, ret_in, solvers * 16)

    wait(recv_sem, 5, halo_in, 120)
    wait(recv_sem, 6, halo_in, 120)

    def finish(b, _):
        def at(row):
            return pl.ds(al(row * 24 + b * 8), 8)

        for v in range(VARS):
            w = 5 * b + v

            def back(k):
                return ret_in[pl.ds((w // 3) * 16 + (w % 3) * 4 + k, 8, stride=80), :]

            left_c, right_c, t0, t1 = back(0), back(1), back(2), back(3)
            above = halo_in[at(v), :]
            below = halo_in[at(5 + v), :]
            run = None
            for i in range(ROWS):
                xi = xrow[at(v * ROWS + i), :] + tv(T_U + i) * left_c + tv(T_V + i) * right_c
                if i == 0:
                    xi = xi + tv(T_DL) * below
                if i == ROWS - 1:
                    xi = xi + tv(T_DR) * above
                xrow[at(v * ROWS + i), :] = xi
                if i:
                    rhs = fbuf[at(v * ROWS + i), :] - crow[at(i), :] * xi
                    run = rhs if run is None else rhs + arow[at(16 + E + i - 1), :] * run
                    srow[at(v * ROWS + i), :] = (
                        arow[at(16 + RD + i), :] * run + arow[at(16 + H + i), :] * t0
                    )
            y = t1
            for i in range(ROWS - 1, 0, -1):
                y = srow[at(v * ROWS + i), :] + arow[at(16 + E + i), :] * y
                srow[at(v * ROWS + i), :] = y
            srow[at(v * ROWS), :] = t0
        return 0

    lax.fori_loop(0, 3, finish, 0)
    for v in range(VARS):
        for rt in range(2):
            for lt in range(tiles):
                src = pl.ds((v * ROWS + rt * 8) * 24 + (lt % 3) * 8 + lt // 3, 8, stride=24)
                der[v, pl.ds(rt * 8, 8), pl.ds(lt * 128, 128)] = xrow[src, :]
                seg[v, pl.ds(rt * 8, 8), pl.ds(lt * 128, 128)] = srow[src, :]

    wait(send_sem, 0, tabs, (slots - 1) * 16)
    wait(send_sem, 1, req, (planes - 1) * 8)
    wait(send_sem, 3, pick_in, (planes - 1) * 8)
    wait(send_sem, 5, halo_in, 120)
    wait(send_sem, 6, halo_in, 120)
    wait(send_sem, 9, side_in, 24)
    wait(send_sem, 10, side_in, 48)

    @pl.when(is_solver)
    def _():
        wait(send_sem, 2, coef_in, (solvers - 1) * 8)
        wait(send_sem, 4, dat_in, (solvers - 1) * 16)
        wait(send_sem, 7, ret_out, (slabs - 1) * 16)

    @pl.when(jnp.logical_not(is_solver))
    def _():
        wait(send_sem, 2, coef_in, solvers * 8)
        wait(send_sem, 4, dat_in, solvers * 16)

    @pl.when(has_two(p))
    def _():
        wait(send_sem, 8, coef_in, (n_two - 1) * 8)

    @pl.when(jnp.logical_not(has_two(p)))
    def _():
        wait(send_sem, 8, coef_in, n_two * 8)


def solution(mesh):
    slabs, cross = mesh.shape["pipe"], mesh.shape["cross"]
    table, carry = derivative_constants(slabs)

    def local(state, face, courant, cell_mask, ghost_cell, ghost_owner, ghost_image, base, weight):
        pencils = state.shape[2]
        tiles = pencils // 128
        solvers = -(-(VARS * tiles) // UNITS)
        planes, slots = slabs // 2, cross * 2
        span = VARS * ROWS * 24

        def buf(rows, dtype=F32):
            return pltpu.VMEM((rows, 128), dtype)

        return pl.pallas_call(
            functools.partial(kernel, slabs, cross, tiles),
            out_shape=(pltpu.VMEM(state.shape, F32),) * 2,
            in_specs=[pl.BlockSpec(memory_space=pl.ANY)] * 11,
            out_specs=(pl.BlockSpec(memory_space=pltpu.VMEM),) * 2,
            scratch_shapes=[
                pltpu.SMEM((1, 128), F32),
                pltpu.SMEM((1, IMAGES), I32),
                pltpu.VMEM((2 * slabs, slabs), F32),
                pltpu.VMEM((1, IMAGES), I32),
                pltpu.VMEM(state.shape, F32),
                pltpu.VMEM(face.shape, F32),
                pltpu.VMEM(face.shape, F32),
                pltpu.VMEM(face.shape, I32),
                pltpu.VMEM((1, GHOSTS), I32),
                pltpu.VMEM((1, GHOSTS), I32),
                pltpu.VMEM((1, GHOSTS), I32),
                pltpu.VMEM((8, IMAGES), F32),
                buf(ROWS * (tiles + 1) * 8),
                buf(2 * IMAGES),
                buf(IMAGES * 8),
                buf(slots * 16),
                buf(planes * 8, I32),
                buf(planes * 8),
                buf(planes * 8),
                buf(ROWS * 24, I32),
                buf(span),
                buf(span),
                buf(span),
                buf(ROWS * 24),
                buf(ROWS * 24 * 6),
                buf(192),
                buf(slabs * 16),
                buf(24 * slabs),
                buf(72),
                buf(72),
                buf(640),
                buf(slabs * 16),
                buf(slabs * 16),
                buf(max(640, solvers * 16)),
                buf(240),
                buf(240),
                pltpu.SemaphoreType.DMA((12,)),
                pltpu.SemaphoreType.DMA((11,)),
                pltpu.SemaphoreType.DMA((11,)),
            ],
            compiler_params=pltpu.CompilerParams(
                collective_id=0, has_side_effects=True, vmem_limit_bytes=62 * 1024 * 1024
            ),
        )(
            jnp.asarray(table).reshape(slabs, 1, 128), jnp.asarray(carry), base.reshape(1, -1),
            state, face, courant, cell_mask,
            ghost_cell.reshape(1, -1), ghost_owner.reshape(1, -1), ghost_image.reshape(1, -1), weight,
        )

    flat = P(("pipe", "cross"))
    slab = P("pipe", "cross")
    whole = P(None, "pipe", "cross")
    return jax.shard_map(
        local,
        mesh=mesh,
        in_specs=(whole, slab, slab, slab, flat, flat, flat, flat, P(None, ("pipe", "cross"))),
        out_specs=(whole, whole),
        check_vma=False,
    )
```

```python
import functools

import jax
import jax.numpy as jnp
import numpy as np
from jax import lax
from jax.experimental import pallas as pl
from jax.experimental.pallas import tpu as pltpu
from jax.sharding import PartitionSpec as P

VARS = 5
ROWS = 16
GHOSTS = 128
IMAGES = 256
UNITS = 3
IMAGE_BITS = (2, 1, 0, 6, 5, 4, 3)
REFLECT = (1.0, -1.0, -1.0, -1.0, 1.0)
F32 = jnp.float32
I32 = jnp.int32
MESH = pl.DeviceIdType.MESH

T_R = 0
T_S = 17
T_K = 34
T_U = 52
T_V = 68
T_H0 = 84
T_H1 = 87
T_H14 = 91
T_H15 = 95
T_D0, T_D15, T_DL, T_DR = 98, 99, 100, 101


def derivative_constants(slabs):
    n = slabs * ROWS
    side = np.full(n, 1.0 / 3.0)
    side[1] = side[n - 2] = 0.25
    side[0] = side[n - 1] = 0.0
    delta, eps = np.ones(n), np.ones(n)
    for k in range(n - 2, -1, -1):
        delta[k] = 1.0 - side[k] * side[k + 1] / delta[k + 1]
    for k in range(1, n):
        eps[k] = 1.0 - side[k] * side[k - 1] / eps[k - 1]
    r, s, e = -side / delta, -side / eps, 1.0 / (delta + eps - 1.0)

    def at(x, i):
        return x[i] if 0 <= i < n else 0.0

    table = np.zeros((slabs, 128))
    decay_l, decay_r = np.zeros(slabs), np.zeros(slabs)
    for p in range(slabs):
        g = p * ROWS
        row = table[p]
        kappa = {k: 25.0 / 36.0 * at(e, g + k) for k in range(-1, ROWS + 1)}
        for k in range(0, ROWS + 1):
            row[T_R + k] = at(r, g + k)
        for k in range(-1, ROWS):
            row[T_S + k + 1] = at(s, g + k)
        for k in range(-1, ROWS + 1):
            row[T_K + k + 1] = kappa[k]
        u = v = 1.0
        for k in range(ROWS):
            u = u * at(r, g + k) if k else 1.0
            row[T_U + k] = u
        for k in range(ROWS - 1, -1, -1):
            v = v * at(s, g + k) if k < ROWS - 1 else 1.0
            row[T_V + k] = v
        decay_l[p] = u * at(r, g + ROWS)
        decay_r[p] = v * at(s, g - 1)
        row[T_H0 : T_H0 + 3] = (0.0, kappa[0], 0.0)
        row[T_H1 : T_H1 + 4] = (-kappa[1], 0.0, kappa[1], 0.0)
        row[T_H14 : T_H14 + 4] = (0.0, -kappa[14], 0.0, kappa[14])
        row[T_H15 : T_H15 + 3] = (0.0, -kappa[15], 0.0)
        row[T_D0] = row[T_D15] = row[T_DR] = 1.0 / 12.0
        row[T_DL] = -1.0 / 12.0
        if p == 0:
            row[T_H0 : T_H0 + 3] = e[0] * np.array((-1.5, 2.0, -0.5))
            row[T_H1 : T_H1 + 4] = e[1] * np.array((-2.0 / 3.0, 1.0 / 48.0, 2.0 / 3.0, -1.0 / 48.0))
            row[T_D0] = row[T_DL] = 0.0
        if p == slabs - 1:
            row[T_H15 : T_H15 + 3] = e[n - 1] * np.array((0.5, -2.0, 1.5))
            row[T_H14 : T_H14 + 4] = e[n - 2] * np.array((1.0 / 48.0, -2.0 / 3.0, -1.0 / 48.0, 2.0 / 3.0))
            row[T_D15] = row[T_DR] = 0.0
    carry = np.zeros((2 * slabs, slabs))
    for p in range(slabs):
        w = 1.0
        for q in range(p - 1, -1, -1):
            carry[p, q] = w
            w *= decay_l[q]
        w = 1.0
        for q in range(p + 1, slabs):
            carry[slabs + p, q] = w
            w *= decay_r[q]
    return table.astype(np.float32), carry.astype(np.float32)


def kernel(
    slabs, cross, tiles,
    tab_hbm, lam_hbm, base_hbm, state_hbm, phi_hbm, cour_hbm, mask_hbm, gcell_hbm, gown_hbm, gimg_hbm, wts_hbm,
    out,
    tab, base_s, lam, base_v, state, phi, cour, mask, gcell, gown, gimg, wts,
    xbuf, win, stage, tabs, req, pick_out, pick_in, gmap, fbuf, xrow, srow, crow, arow,
    coef_out, coef_in, fac, side_out, side_in, dat_out, dat_in, ret_out, ret_in, halo_out, halo_in,
    in_sem, send_sem, recv_sem,
):
    p = lax.axis_index("pipe")
    c = lax.axis_index("cross")
    yz, core = p // 2, p % 2
    planes = slabs // 2
    slot = c * 2 + core
    slots = cross * 2
    tp = tiles + 1
    magic = -(-65536 // tiles)
    solvers = -(-(VARS * tiles) // UNITS)
    is_solver = p < solvers
    before, after = lax.rem(p + slabs - 1, slabs), lax.rem(p + 1, slabs)

    def fetch(k, src, dst):
        copy = pltpu.make_async_copy(src, dst, in_sem.at[k])
        copy.start()
        return copy

    got_base = fetch(1, base_hbm, base_v)
    got_wts = fetch(3, wts_hbm, wts)
    got_state = [fetch(0, state_hbm, state)]
    got_base_s = fetch(2, base_hbm, base_s)
    barrier = pltpu.get_barrier_semaphore()

    def greet(i, _):
        pl.semaphore_signal(barrier, inc=1, device_id=(lax.rem(p + i, slabs), c), device_id_type=MESH)
        return 0

    lax.fori_loop(1, slabs, greet, 0)
    for dc in range(1, cross):
        for k in range(2):
            pl.semaphore_signal(
                barrier, inc=1, device_id=(yz * 2 + k, lax.rem(c + dc, cross)), device_id_type=MESH
            )

    got_rest = [
        fetch(4, mask_hbm, mask),
        fetch(5, phi_hbm, phi),
        fetch(6, cour_hbm, cour),
        fetch(7, gcell_hbm, gcell),
        fetch(8, gown_hbm, gown),
        fetch(9, gimg_hbm, gimg),
        fetch(10, tab_hbm.at[p], tab),
        fetch(11, lam_hbm, lam),
    ]

    def send(src, dst, sem, dev):
        pltpu.make_async_remote_copy(
            src_ref=src,
            dst_ref=dst,
            send_sem=send_sem.at[sem],
            recv_sem=recv_sem.at[sem],
            device_id=dev,
            device_id_type=MESH,
        ).start()

    def wait(sems, sem, ref, rows):
        part = ref.at[pl.ds(0, rows), :]
        pltpu.make_async_copy(part, part, sems.at[sem]).wait()

    def al(x):
        return pl.multiple_of(x, 8)

    lane = lax.broadcasted_iota(I32, (8, 128), 1)
    got_base.wait()
    got_wts.wait()
    spot = jnp.broadcast_to((base_v[...] & 127).astype(F32), (8, IMAGES)).T
    cols8 = wts[...].T
    for g in range(IMAGES // 8):
        here = spot[g * 8 : g * 8 + 8, 0:1].astype(I32)
        rel = (lane - here) & 127
        w = [jnp.broadcast_to(cols8[g * 8 : g * 8 + 8, k : k + 1], (8, 128)) for k in range(8)]
        for row in range(2):
            m = jnp.zeros((8, 128), F32)
            for k, off in enumerate((0, 1, 96, 97)):
                m = jnp.where(rel == off, w[row * 4 + k], m)
            win[pl.ds(row * IMAGES + g * 8, 8), :] = m

    for r in range(ROWS):
        xbuf[pl.ds((r * tp + tiles) * 8, 8), :] = jnp.zeros((8, 128), F32)
    for copy in got_state:
        copy.wait()
    for rt in range(2):
        for lt in range(tiles):
            for v in range(VARS):
                nat = state[v, pl.ds(rt * 8, 8), pl.ds(lt * 128, 128)]
                xbuf[pl.ds((rt * 8 * tp + lt) * 8 + v, 8, stride=tp * 8), :] = nat
    got_base_s.wait()
    blocks = xbuf.reshape(ROWS * tp, 8, 128)

    def merge(bit, a, b):
        low = ((lane >> bit) & 1) == 0
        return jnp.where(low, a, b) + pltpu.roll(jnp.where(low, b, a), 128 - (1 << bit), axis=1)

    def halves(bit, vals):
        n = len(vals) // 2
        return [merge(bit, vals[i], vals[i + n]) for i in range(n)]

    def image_group(g, _):
        m0 = win[pl.ds(al(g * 8), 8), :]
        m1 = win[pl.ds(al(IMAGES + g * 8), 8), :]
        vals = []
        for k in range(8):
            b = base_s[0, g * 8 + k]
            x = b >> 7
            r = (x * magic) >> 16
            off = x + r
            inside = lane >= (b & 127)
            z0 = jnp.where(inside, blocks[off], blocks[off + 1])
            z1 = jnp.where(inside, blocks[off + tp], blocks[off + tp + 1])
            stage[pl.ds(al(g * 64 + k * 8), 8), :] = z0 * m0[k : k + 1, :] + z1 * m1[k : k + 1, :]
        return 0

    lax.fori_loop(0, IMAGES // 8, image_group, 0, unroll=4)
    both = [[], []]
    for g in range(IMAGES // 8):
        vals = [stage[pl.ds(g * 64 + k * 8, 8), :] for k in range(8)]
        for bit in range(3):
            vals = halves(bit, vals)
        both[g // 16].append(vals[0])
    for bit in range(3, 7):
        both = [halves(bit, vals) for vals in both]
    sub = lax.broadcasted_iota(I32, (8, 128), 0)
    second = pltpu.roll(both[1][0], VARS, axis=0)
    tabs[pl.ds(al(yz * 16), 8), :] = jnp.where(sub < VARS, both[0][0], second)
    tabs[pl.ds(al(yz * 16 + 8), 8), :] = second

    for copy in got_rest:
        copy.wait()
    req[pl.ds(al(slot * 8), 8), :] = jnp.concatenate(
        [gown[...], gimg[...], jnp.zeros((6, GHOSTS), I32)], axis=0
    )

    pl.semaphore_wait(barrier, slabs - 1 + (cross - 1) * 2)

    def send_table(j, _):
        half = planes // 2
        d = lax.rem(yz + jnp.where(j < half, half + j, planes - 1 - j), planes)
        mine = pl.ds(al(yz * 16), 2 * VARS)
        send(tabs.at[mine, :], tabs.at[mine, :], 0, (d * 2 + core, c))
        return 0

    lax.fori_loop(0, planes - 1, send_table, 0)
    row_peers = [
        (yz * 2 + lax.rem(core + dk, 2), lax.rem(c + dc, cross))
        for dc in range(cross)
        for dk in range(2)
        if dc or dk
    ]
    for dev in row_peers:
        mine = pl.ds(al(slot * 8), 2)
        send(req.at[mine, :], req.at[mine, :], 1, dev)

    for rt in range(2):
        for lt in range(tiles):
            cols = pl.ds(lt * 128, 128)
            rows = pl.ds(rt * 8, 8)
            solid = mask[rows, cols] == 1
            place = (lt % 3) * 8 + lt // 3
            for v in range(VARS):
                fbuf[pl.ds((v * ROWS + rt * 8) * 24 + place, 8, stride=24), :] = jnp.where(
                    solid, 0.0, state[v, rows, cols]
                )
            crow[pl.ds(rt * 8 * 24 + place, 8, stride=24), :] = cour[rows, cols]
            arow[pl.ds(rt * 8 * 24 + place, 8, stride=24), :] = phi[rows, cols]

    cell = gcell[...]
    x = cell >> 7
    r = (x * magic) >> 16
    t = x - r * tiles
    t3 = (t * 21846) >> 16
    at_row = r * 24 + (t - t3 * 3) * 8 + t3
    ghost_no = (lax.broadcasted_iota(I32, (1, GHOSTS), 1) + 1).astype(F32)
    row_no = lax.broadcasted_iota(I32, (ROWS * 24, GHOSTS), 0)
    left = jnp.where(row_no == at_row, ghost_no, 0.0).astype(jnp.bfloat16)
    lane_no = lax.broadcasted_iota(I32, (128, GHOSTS), 0)
    right = jnp.where(lane_no == (cell & 127), 1.0, 0.0).astype(jnp.bfloat16)
    numbers = lax.dot_general(left, right, (((1,), (1,)), ((), ())), preferred_element_type=F32)
    gmap[...] = (numbers + 0.5).astype(I32) - 1

    def rowof(ref, i):
        return ref[pl.ds(i * 24, 24), :]

    def put(ref, i, val):
        ref[pl.ds(i * 24, 24), :] = val

    E, H, RD, WL, WR, C = 0, 16, 32, 48, 64, 80
    top = jnp.where(p == slabs - 1, 0.0, 1.0)
    h = rowof(arow, 0)
    m = jnp.ones_like(h)
    m_l = jnp.ones_like(h)
    faces = arow
    for k in range(1, ROWS):
        face = rowof(faces, k)
        if k == ROWS - 1:
            face = face * top
        rd = 1.0 / (h + face + m)
        e = face * rd
        hh = h * rd
        put(arow, 16 + E + k, e)
        put(arow, 16 + H + k, hh)
        put(arow, 16 + RD + k, rd)
        m_l = m_l + m * hh
        h = h * e
        m = 1.0 + m * e
    w_l = jnp.zeros_like(h)
    w_r = jnp.ones_like(h)
    cols = [jnp.zeros_like(h) for _ in range(4)]
    for k in range(ROWS - 1, 0, -1):
        e = rowof(arow, 16 + E + k)
        w_l = rowof(arow, 16 + H + k) + e * w_l
        w_r = e * w_r
        put(arow, 16 + WL + k, w_l)
        put(arow, 16 + WR + k, w_r)
        ck = rowof(crow, k)
        cl, cr = w_l * ck, w_r * ck
        u, v = tab[0, T_U + k], tab[0, T_V + k]
        cols = [cols[0] - u * cl, cols[1] - u * cr, cols[2] - v * cl, cols[3] - v * cr]
        if k == ROWS - 1:
            k1, k2 = -tab[0, T_DR] * cl, -tab[0, T_DR] * cr
    c0 = rowof(crow, 0)
    cols[0] = cols[0] - tab[0, T_U] * c0
    cols[2] = cols[2] - tab[0, T_V] * c0
    for k, val in enumerate((h, m_l, m - 1.0, *cols)):
        for b in range(3):
            coef_out[pl.ds(b * 8 + k, 8, stride=24), :] = val[b * 8 : b * 8 + 8, :]
    for k, val in enumerate((-tab[0, T_DL] * c0, k1, k2)):
        side_out[pl.ds(k * 24, 24), :] = val

    def first_tile(d):
        return (UNITS * d) // VARS

    def has_two(d):
        return jnp.logical_and(d < solvers, lax.rem(UNITS * d, VARS) > VARS - UNITS)

    n_two = sum((UNITS * d) % VARS > VARS - UNITS for d in range(solvers))

    def send_coef(i, _):
        d = lax.rem(p + i, slabs)

        @pl.when(d < solvers)
        def _():
            send(
                coef_out.at[pl.ds(al(first_tile(d) * 8), 8), :],
                coef_in.at[pl.ds(al(p * 16), 8), :],
                2,
                (d, c),
            )

        @pl.when(has_two(d))
        def _():
            send(
                coef_out.at[pl.ds(al(first_tile(d) * 8 + 8), 8), :],
                coef_in.at[pl.ds(al(p * 16 + 8), 8), :],
                8,
                (d, c),
            )

        return 0

    wait(recv_sem, 0, tabs, (planes - 1) * 2 * VARS)
    wait(recv_sem, 1, req, (slots - 1) * 2)
    owner = req[pl.ds(0, slots, stride=8), :]
    image = req[pl.ds(1, slots, stride=8), :]
    o_c = lax.rem(owner, cross)
    o_p = lax.div(owner, cross)
    held = jnp.logical_and(o_c == c, (o_p & 1) == core)
    which = jnp.where(held, (o_p >> 1) * 2 + (image >> 7), jnp.full_like(owner, -1))
    spot7 = jnp.zeros_like(image)
    for bit in range(7):
        spot7 = spot7 | (((image >> bit) & 1) << IMAGE_BITS[bit])
    tables = []
    for k in range(planes):
        first, second = tabs[pl.ds(k * 16, 8), :], tabs[pl.ds(k * 16 + 8, 8), :]
        back = 8 - VARS
        tables += [
            first,
            jnp.where(sub < back, pltpu.roll(first, back, axis=0), pltpu.roll(second, back, axis=0)),
        ]
    for n in range(slots):
        idx = jnp.broadcast_to(spot7[n : n + 1, :], (8, 128))
        wh = jnp.broadcast_to(which[n : n + 1, :], (8, 128))
        acc = jnp.zeros((8, 128), F32)
        for k in range(planes * 2):
            got = jnp.take_along_axis(tables[k], idx, axis=1, mode="promise_in_bounds")
            acc = jnp.where(wh == k, got, acc)
        pick_out[pl.ds(n * 8, 8), :] = acc

    for dev in row_peers:
        send(
            pick_out.at[pl.ds(al((dev[1] * 2 + lax.rem(dev[0], 2)) * 8), VARS), :],
            pick_in.at[pl.ds(al(slot * 8), VARS), :],
            3,
            dev,
        )
    pick_in[pl.ds(al(slot * 8), 8), :] = pick_out[pl.ds(al(slot * 8), 8), :]

    send(side_out.at[pl.ds(0, 24), :], side_in.at[pl.ds(0, 24), :], 9, (before, c))
    send(side_out.at[pl.ds(24, 48), :], side_in.at[pl.ds(24, 48), :], 10, (after, c))
    lax.fori_loop(1, slabs, send_coef, 0)

    @pl.when(is_solver)
    def _():
        coef_in[pl.ds(al(p * 16), 16), :] = coef_out[pl.ds(al(first_tile(p) * 8), 16), :]

    wait(recv_sem, 3, pick_in, (slots - 1) * VARS)
    ghost = pick_in[pl.ds(0, 8), :]
    for n in range(1, slots):
        ghost = ghost + pick_in[pl.ds(n * 8, 8), :]
    ghost = [jnp.broadcast_to(REFLECT[v] * ghost[v : v + 1, :], (8, 128)) for v in range(VARS)]

    def tv(i):
        return tab[0, i]

    wait(recv_sem, 9, side_in, 24)
    wait(recv_sem, 10, side_in, 48)

    def send_class(k):
        def one(i, _):
            d = 5 * lax.rem(p + i, tiles // 3) + k

            @pl.when(d != p)
            def _():
                send(
                    dat_out.at[pl.ds(al(d * 16), 16), :],
                    dat_in.at[pl.ds(al(p * 16), 16), :],
                    4,
                    (d, c),
                )

            return 0

        lax.fori_loop(0, tiles // 3, one, 0)

    def local(b, _):
        def at(row):
            return pl.ds(al(row * 24 + b * 8), 8)

        def filled(i):
            gi = gmap[at(i), :]
            has = gi >= 0
            idx = jnp.maximum(gi, 0)
            out = []
            for v in range(VARS):
                got = jnp.take_along_axis(ghost[v], idx, axis=1, mode="promise_in_bounds")
                val = jnp.where(has, got, fbuf[at(v * ROWS + i), :])
                fbuf[at(v * ROWS + i), :] = val
                out.append(val)
            return out

        f = [filled(i) for i in range(ROWS)]
        for v in range(VARS):
            fv = [f[i][v] for i in range(ROWS)]
            up = tv(T_K) * fv[0]
            for i in range(ROWS):
                if i == 0:
                    hi = tv(T_H0) * fv[0] + tv(T_H0 + 1) * fv[1] + tv(T_H0 + 2) * fv[2]
                elif i == 1:
                    hi = sum(tv(T_H1 + k) * fv[k] for k in range(4))
                elif i == ROWS - 2:
                    hi = sum(tv(T_H14 + k) * fv[12 + k] for k in range(4))
                elif i == ROWS - 1:
                    hi = sum(tv(T_H15 + k) * fv[13 + k] for k in range(3))
                else:
                    hi = tv(T_K + 1 + i) * (fv[i + 1] - fv[i - 1])
                up = tv(T_R + i) * up + hi
                xrow[at(v * ROWS + i), :] = up
                srow[at(v * ROWS + i), :] = hi
            end = tv(T_K + 1 + ROWS) * fv[ROWS - 1]
            z_l = tv(T_R + ROWS) * up - end
            down = -end
            s_l = s_r = None
            for i in range(ROWS - 1, -1, -1):
                down = tv(T_S + 1 + i) * down
                xi = xrow[at(v * ROWS + i), :] + down
                if i == 0:
                    xi = xi + tv(T_D0) * fv[1]
                elif i == ROWS - 1:
                    xi = xi - tv(T_D15) * fv[ROWS - 2]
                else:
                    xi = xi + (1.0 / 12.0) * (fv[i + 1] - fv[i - 1])
                xrow[at(v * ROWS + i), :] = xi
                down = down + srow[at(v * ROWS + i), :]
                rhs = fv[i] - crow[at(i), :] * xi
                if i:
                    wl, wr = arow[at(16 + WL + i), :], arow[at(16 + WR + i), :]
                    s_l = wl * rhs if s_l is None else s_l + wl * rhs
                    s_r = wr * rhs if s_r is None else s_r + wr * rhs
                else:
                    s_l = s_l + rhs
            z_r = tv(T_S) * down + tv(T_K) * fv[0]
            s_r = s_r + side_in[at(0), :] * fv[ROWS - 1]
            s_b = side_in[at(1), :] * fv[0]
            s_l = s_l + side_in[at(2), :] * fv[0]
            w = 5 * b + v
            for k, val in enumerate((z_l, z_r, s_l, s_r, s_b)):
                dat_out[pl.ds((w // 3) * 16 + (w % 3) * 5 + k, 8, stride=80), :] = val
            halo_out[pl.ds(al(v * 24 + b * 8), 8), :] = fv[0]
            halo_out[pl.ds(al(120 + v * 24 + b * 8), 8), :] = fv[ROWS - 1]
        send_class(2 * b)

        @pl.when(b > 0)
        def _():
            send_class(2 * b - 1)

        return 0

    lax.fori_loop(0, 3, local, 0)

    send(halo_out.at[pl.ds(0, 120), :], halo_in.at[pl.ds(0, 120), :], 5, (before, c))
    send(halo_out.at[pl.ds(120, 120), :], halo_in.at[pl.ds(120, 120), :], 6, (after, c))

    @pl.when(is_solver)
    def _():
        wait(recv_sem, 2, coef_in, (slabs - 1) * 8)

        @pl.when(has_two(p))
        def _():
            wait(recv_sem, 8, coef_in, (slabs - 1) * 8)

        for j in range(2):

            def field(k):
                return coef_in[pl.ds(j * 8 + k, slabs, stride=16), :]

            gu = field(0)
            gl = pltpu.roll(gu, 1, axis=0)
            mm = field(1) + pltpu.roll(field(2), 1, axis=0)
            step, s = 0, 1
            while s < slabs:
                rd = 1.0 / (mm + gl + gu)
                pf = gl * pltpu.roll(rd, s, axis=0)
                tf = gu * pltpu.roll(rd, slabs - s, axis=0)
                at0 = ((j * 6 + step) * 2) * slabs
                fac[pl.ds(at0, slabs), :] = pf
                fac[pl.ds(at0 + slabs, slabs), :] = tf
                mm = mm + pf * pltpu.roll(mm, s, axis=0) + tf * pltpu.roll(mm, slabs - s, axis=0)
                gl = pf * pltpu.roll(gl, s, axis=0)
                gu = tf * pltpu.roll(gu, slabs - s, axis=0)
                step, s = step + 1, s * 2
            fac[pl.ds((j * 6 + 5) * 2 * slabs, slabs), :] = 1.0 / (mm + gl + gu)

    @pl.when(is_solver)
    def _():
        dat_in[pl.ds(al(p * 16), 16), :] = dat_out[pl.ds(al(p * 16), 16), :]
        wait(recv_sem, 4, dat_in, (slabs - 1) * 16)

        def data(u, k):
            return dat_in[pl.ds(u * 5 + k, slabs, stride=16), :]

        z_l = jnp.concatenate([data(u, 0) for u in range(UNITS)], axis=1)
        z_r = jnp.concatenate([data(u, 1) for u in range(UNITS)], axis=1)
        hi = lax.Precision.HIGHEST
        c_l = jnp.dot(lam[pl.ds(0, slabs), :], z_l, precision=hi, preferred_element_type=F32)
        c_r = jnp.dot(lam[pl.ds(slabs, slabs), :], z_r, precision=hi, preferred_element_type=F32)
        for u in range(UNITS):
            j = (UNITS * p + u) // VARS - first_tile(p)

            def field(k):
                return coef_in[pl.ds(j * 8 + k, slabs, stride=16), :]

            cl, cr = c_l[:, u * 128 : u * 128 + 128], c_r[:, u * 128 : u * 128 + 128]
            q = data(u, 3) + field(4) * cl + field(6) * cr
            d = data(u, 2) + field(3) * cl + field(5) * cr + pltpu.roll(data(u, 4), slabs - 1, axis=0)
            d = d + pltpu.roll(q, 1, axis=0)
            step, s = 0, 1
            while s < slabs:
                at0 = ((j * 6 + step) * 2) * slabs
                pf = fac[pl.ds(al(at0), slabs), :]
                tf = fac[pl.ds(al(at0 + slabs), slabs), :]
                d = d + pf * pltpu.roll(d, s, axis=0) + tf * pltpu.roll(d, slabs - s, axis=0)
                step, s = step + 1, s * 2
            x = d * fac[pl.ds(al((j * 6 + 5) * 2 * slabs), slabs), :]
            for k, val in enumerate((cl, cr, x, pltpu.roll(x, slabs - 1, axis=0))):
                ret_out[pl.ds(u * 4 + k, slabs, stride=16), :] = val

        def send_ret(i, _):
            d = lax.rem(p + i, slabs)
            send(ret_out.at[pl.ds(al(d * 16), 12), :], ret_in.at[pl.ds(al(p * 16), 12), :], 7, (d, c))
            return 0

        lax.fori_loop(1, slabs, send_ret, 0)
        ret_in[pl.ds(al(p * 16), 16), :] = ret_out[pl.ds(al(p * 16), 16), :]
        wait(recv_sem, 7, ret_in, (solvers - 1) * 12)

    @pl.when(jnp.logical_not(is_solver))
    def _():
        wait(recv_sem, 7, ret_in, solvers * 12)

    wait(recv_sem, 5, halo_in, 120)
    wait(recv_sem, 6, halo_in, 120)

    def finish(b, _):
        def at(row):
            return pl.ds(al(row * 24 + b * 8), 8)

        for v in range(VARS):
            w = 5 * b + v

            def back(k):
                return ret_in[pl.ds((w // 3) * 16 + (w % 3) * 4 + k, 8, stride=80), :]

            left_c, right_c, t0, t1 = back(0), back(1), back(2), back(3)
            above = halo_in[at(v), :]
            below = halo_in[at(5 + v), :]
            run = None
            for i in range(ROWS):
                xi = xrow[at(v * ROWS + i), :] + tv(T_U + i) * left_c + tv(T_V + i) * right_c
                if i == 0:
                    xi = xi + tv(T_DL) * below
                if i == ROWS - 1:
                    xi = xi + tv(T_DR) * above
                xrow[at(v * ROWS + i), :] = xi
                if i:
                    rhs = fbuf[at(v * ROWS + i), :] - crow[at(i), :] * xi
                    run = rhs if run is None else rhs + arow[at(16 + E + i - 1), :] * run
                    srow[at(v * ROWS + i), :] = (
                        arow[at(16 + RD + i), :] * run + arow[at(16 + H + i), :] * t0
                    )
            y = t1
            for i in range(ROWS - 1, 0, -1):
                y = srow[at(v * ROWS + i), :] + arow[at(16 + E + i), :] * y
                srow[at(v * ROWS + i), :] = y
            srow[at(v * ROWS), :] = t0
        return 0

    lax.fori_loop(0, 3, finish, 0)
    for v in range(VARS):
        for rt in range(2):
            for lt in range(tiles):
                src = pl.ds((v * ROWS + rt * 8) * 24 + (lt % 3) * 8 + lt // 3, 8, stride=24)
                out[0, v, pl.ds(rt * 8, 8), pl.ds(lt * 128, 128)] = xrow[src, :]
                out[1, v, pl.ds(rt * 8, 8), pl.ds(lt * 128, 128)] = srow[src, :]

    wait(send_sem, 0, tabs, (planes - 1) * 2 * VARS)
    wait(send_sem, 1, req, (slots - 1) * 2)
    wait(send_sem, 3, pick_in, (slots - 1) * VARS)
    wait(send_sem, 5, halo_in, 120)
    wait(send_sem, 6, halo_in, 120)
    wait(send_sem, 9, side_in, 24)
    wait(send_sem, 10, side_in, 48)

    @pl.when(is_solver)
    def _():
        wait(send_sem, 2, coef_in, (solvers - 1) * 8)
        wait(send_sem, 4, dat_in, (solvers - 1) * 16)
        wait(send_sem, 7, ret_out, (slabs - 1) * 12)

    @pl.when(jnp.logical_not(is_solver))
    def _():
        wait(send_sem, 2, coef_in, solvers * 8)
        wait(send_sem, 4, dat_in, solvers * 16)

    @pl.when(has_two(p))
    def _():
        wait(send_sem, 8, coef_in, (n_two - 1) * 8)

    @pl.when(jnp.logical_not(has_two(p)))
    def _():
        wait(send_sem, 8, coef_in, n_two * 8)


def solution(mesh):
    slabs, cross = mesh.shape["pipe"], mesh.shape["cross"]
    table, carry = derivative_constants(slabs)

    def local(state, face, courant, cell_mask, ghost_cell, ghost_owner, ghost_image, base, weight):
        pencils = state.shape[2]
        tiles = pencils // 128
        solvers = -(-(VARS * tiles) // UNITS)
        planes, slots = slabs // 2, cross * 2
        span = VARS * ROWS * 24

        def buf(rows, dtype=F32):
            return pltpu.VMEM((rows, 128), dtype)

        out = pl.pallas_call(
            functools.partial(kernel, slabs, cross, tiles),
            out_shape=pltpu.VMEM((2, *state.shape), F32),
            in_specs=[pl.BlockSpec(memory_space=pl.ANY)] * 11,
            out_specs=pl.BlockSpec(memory_space=pltpu.VMEM),
            scratch_shapes=[
                pltpu.SMEM((1, 128), F32),
                pltpu.SMEM((1, IMAGES), I32),
                pltpu.VMEM((2 * slabs, slabs), F32),
                pltpu.VMEM((1, IMAGES), I32),
                pltpu.VMEM(state.shape, F32),
                pltpu.VMEM(face.shape, F32),
                pltpu.VMEM(face.shape, F32),
                pltpu.VMEM(face.shape, I32),
                pltpu.VMEM((1, GHOSTS), I32),
                pltpu.VMEM((1, GHOSTS), I32),
                pltpu.VMEM((1, GHOSTS), I32),
                pltpu.VMEM((8, IMAGES), F32),
                buf(ROWS * (tiles + 1) * 8),
                buf(2 * IMAGES),
                buf(IMAGES * 8),
                buf(planes * 16),
                buf(slots * 8, I32),
                buf(slots * 8),
                buf(slots * 8),
                buf(ROWS * 24, I32),
                buf(span),
                buf(span),
                buf(span),
                buf(ROWS * 24),
                buf(ROWS * 24 * 6),
                buf(192),
                buf(slabs * 16),
                buf(24 * slabs),
                buf(72),
                buf(72),
                buf(640),
                buf(slabs * 16),
                buf(slabs * 16),
                buf(max(640, solvers * 16)),
                buf(240),
                buf(240),
                pltpu.SemaphoreType.DMA((16,)),
                pltpu.SemaphoreType.DMA((11,)),
                pltpu.SemaphoreType.DMA((11,)),
            ],
            compiler_params=pltpu.CompilerParams(
                collective_id=0, has_side_effects=True, vmem_limit_bytes=62 * 1024 * 1024
            ),
        )(
            jnp.asarray(table).reshape(slabs, 1, 128), jnp.asarray(carry), base.reshape(1, -1),
            state, face, courant, cell_mask,
            ghost_cell.reshape(1, -1), ghost_owner.reshape(1, -1), ghost_image.reshape(1, -1), weight,
        )
        return out[0], out[1]

    flat = P(("pipe", "cross"))
    slab = P("pipe", "cross")
    whole = P(None, "pipe", "cross")
    return jax.shard_map(
        local,
        mesh=mesh,
        in_specs=(whole, slab, slab, slab, flat, flat, flat, flat, P(None, ("pipe", "cross"))),
        out_specs=(whole, whole),
        check_vma=False,
    )
```

```python
import functools

import jax
import jax.numpy as jnp
import numpy as np
from jax import lax
from jax.experimental import pallas as pl
from jax.experimental.pallas import tpu as pltpu
from jax.sharding import PartitionSpec as P

VARS = 5
ROWS = 16
GHOSTS = 128
IMAGES = 256
UNITS = 3
IMAGE_BITS = (2, 1, 0, 6, 5, 4, 3)
REFLECT = (1.0, -1.0, -1.0, -1.0, 1.0)
F32 = jnp.float32
I32 = jnp.int32
MESH = pl.DeviceIdType.MESH

T_R = 0
T_S = 17
T_K = 34
T_U = 52
T_V = 68
T_H0 = 84
T_H1 = 87
T_H14 = 91
T_H15 = 95
T_D0, T_D15, T_DL, T_DR = 98, 99, 100, 101


def derivative_constants(slabs):
    n = slabs * ROWS
    side = np.full(n, 1.0 / 3.0)
    side[1] = side[n - 2] = 0.25
    side[0] = side[n - 1] = 0.0
    delta, eps = np.ones(n), np.ones(n)
    for k in range(n - 2, -1, -1):
        delta[k] = 1.0 - side[k] * side[k + 1] / delta[k + 1]
    for k in range(1, n):
        eps[k] = 1.0 - side[k] * side[k - 1] / eps[k - 1]
    r, s, e = -side / delta, -side / eps, 1.0 / (delta + eps - 1.0)

    def at(x, i):
        return x[i] if 0 <= i < n else 0.0

    table = np.zeros((slabs, 128))
    decay_l, decay_r = np.zeros(slabs), np.zeros(slabs)
    for p in range(slabs):
        g = p * ROWS
        row = table[p]
        kappa = {k: 25.0 / 36.0 * at(e, g + k) for k in range(-1, ROWS + 1)}
        for k in range(0, ROWS + 1):
            row[T_R + k] = at(r, g + k)
        for k in range(-1, ROWS):
            row[T_S + k + 1] = at(s, g + k)
        for k in range(-1, ROWS + 1):
            row[T_K + k + 1] = kappa[k]
        u = v = 1.0
        for k in range(ROWS):
            u = u * at(r, g + k) if k else 1.0
            row[T_U + k] = u
        for k in range(ROWS - 1, -1, -1):
            v = v * at(s, g + k) if k < ROWS - 1 else 1.0
            row[T_V + k] = v
        decay_l[p] = u * at(r, g + ROWS)
        decay_r[p] = v * at(s, g - 1)
        row[T_H0 : T_H0 + 3] = (0.0, kappa[0], 0.0)
        row[T_H1 : T_H1 + 4] = (-kappa[1], 0.0, kappa[1], 0.0)
        row[T_H14 : T_H14 + 4] = (0.0, -kappa[14], 0.0, kappa[14])
        row[T_H15 : T_H15 + 3] = (0.0, -kappa[15], 0.0)
        row[T_D0] = row[T_D15] = row[T_DR] = 1.0 / 12.0
        row[T_DL] = -1.0 / 12.0
        if p == 0:
            row[T_H0 : T_H0 + 3] = e[0] * np.array((-1.5, 2.0, -0.5))
            row[T_H1 : T_H1 + 4] = e[1] * np.array((-2.0 / 3.0, 1.0 / 48.0, 2.0 / 3.0, -1.0 / 48.0))
            row[T_D0] = row[T_DL] = 0.0
        if p == slabs - 1:
            row[T_H15 : T_H15 + 3] = e[n - 1] * np.array((0.5, -2.0, 1.5))
            row[T_H14 : T_H14 + 4] = e[n - 2] * np.array((1.0 / 48.0, -2.0 / 3.0, -1.0 / 48.0, 2.0 / 3.0))
            row[T_D15] = row[T_DR] = 0.0
    carry = np.zeros((2 * slabs, slabs))
    for p in range(slabs):
        w = 1.0
        for q in range(p - 1, -1, -1):
            carry[p, q] = w
            w *= decay_l[q]
        w = 1.0
        for q in range(p + 1, slabs):
            carry[slabs + p, q] = w
            w *= decay_r[q]
    return table.astype(np.float32), carry.astype(np.float32)


def kernel(
    slabs, cross, tiles,
    tab_hbm, lam_hbm, base_hbm, state_hbm, phi_hbm, cour_hbm, mask_hbm, gcell_hbm, gown_hbm, gimg_hbm, wts_hbm,
    out,
    tab, base_s, lam, base_v, state, phi, cour, mask, gcell, gown, gimg, wts,
    xbuf, win, stage, tabs, req, pick_out, pick_in, gmap, fbuf, xrow, srow, crow, arow,
    coef_out, coef_in, fac, side_out, side_in, dat_out, dat_in, ret_out, ret_in, halo_out, halo_in,
    in_sem, send_sem, recv_sem,
):
    p = lax.axis_index("pipe")
    c = lax.axis_index("cross")
    yz, core = p // 2, p % 2
    planes = slabs // 2
    slot = c * 2 + core
    slots = cross * 2
    tp = tiles + 1
    magic = -(-65536 // tiles)
    solvers = -(-(VARS * tiles) // UNITS)
    is_solver = p < solvers
    before, after = lax.rem(p + slabs - 1, slabs), lax.rem(p + 1, slabs)

    def fetch(k, src, dst):
        copy = pltpu.make_async_copy(src, dst, in_sem.at[k])
        copy.start()
        return copy

    got_base = fetch(1, base_hbm, base_v)
    got_wts = fetch(3, wts_hbm, wts)
    got_state = [fetch(0, state_hbm, state)]
    got_base_s = fetch(2, base_hbm, base_s)
    barrier = pltpu.get_barrier_semaphore()

    def greet(i, _):
        pl.semaphore_signal(barrier, inc=1, device_id=(lax.rem(p + i, slabs), c), device_id_type=MESH)
        return 0

    lax.fori_loop(1, slabs, greet, 0)
    for dc in range(1, cross):
        for k in range(2):
            pl.semaphore_signal(
                barrier, inc=1, device_id=(yz * 2 + k, lax.rem(c + dc, cross)), device_id_type=MESH
            )

    got_rest = [
        fetch(4, mask_hbm, mask),
        fetch(5, phi_hbm, phi),
        fetch(6, cour_hbm, cour),
        fetch(7, gcell_hbm, gcell),
        fetch(8, gown_hbm, gown),
        fetch(9, gimg_hbm, gimg),
        fetch(10, tab_hbm.at[p], tab),
        fetch(11, lam_hbm, lam),
    ]

    def send(src, dst, sem, dev):
        pltpu.make_async_remote_copy(
            src_ref=src,
            dst_ref=dst,
            send_sem=send_sem.at[sem],
            recv_sem=recv_sem.at[sem],
            device_id=dev,
            device_id_type=MESH,
        ).start()

    def wait(sems, sem, ref, rows):
        part = ref.at[pl.ds(0, rows), :]
        pltpu.make_async_copy(part, part, sems.at[sem]).wait()

    def al(x):
        return pl.multiple_of(x, 8)

    lane = lax.broadcasted_iota(I32, (8, 128), 1)
    got_base.wait()
    got_wts.wait()
    spot = jnp.broadcast_to((base_v[...] & 127).astype(F32), (8, IMAGES)).T
    cols8 = wts[...].T
    for g in range(IMAGES // 8):
        here = spot[g * 8 : g * 8 + 8, 0:1].astype(I32)
        rel = (lane - here) & 127
        w = [jnp.broadcast_to(cols8[g * 8 : g * 8 + 8, k : k + 1], (8, 128)) for k in range(8)]
        for row in range(2):
            m = jnp.zeros((8, 128), F32)
            for k, off in enumerate((0, 1, 96, 97)):
                m = jnp.where(rel == off, w[row * 4 + k], m)
            win[pl.ds(row * IMAGES + g * 8, 8), :] = m

    for r in range(ROWS):
        xbuf[pl.ds((r * tp + tiles) * 8, 8), :] = jnp.zeros((8, 128), F32)
    for copy in got_state:
        copy.wait()
    for rt in range(2):
        for lt in range(tiles):
            for v in range(VARS):
                nat = state[v, pl.ds(rt * 8, 8), pl.ds(lt * 128, 128)]
                xbuf[pl.ds((rt * 8 * tp + lt) * 8 + v, 8, stride=tp * 8), :] = nat
    got_base_s.wait()
    blocks = xbuf.reshape(ROWS * tp, 8, 128)

    def merge(bit, a, b):
        low = ((lane >> bit) & 1) == 0
        return jnp.where(low, a, b) + pltpu.roll(jnp.where(low, b, a), 128 - (1 << bit), axis=1)

    def halves(bit, vals):
        n = len(vals) // 2
        return [merge(bit, vals[i], vals[i + n]) for i in range(n)]

    def image_group(g, _):
        m0 = win[pl.ds(al(g * 8), 8), :]
        m1 = win[pl.ds(al(IMAGES + g * 8), 8), :]
        vals = []
        for k in range(8):
            b = base_s[0, g * 8 + k]
            x = b >> 7
            r = (x * magic) >> 16
            off = x + r
            inside = lane >= (b & 127)
            z0 = jnp.where(inside, blocks[off], blocks[off + 1])
            z1 = jnp.where(inside, blocks[off + tp], blocks[off + tp + 1])
            stage[pl.ds(al(g * 64 + k * 8), 8), :] = z0 * m0[k : k + 1, :] + z1 * m1[k : k + 1, :]
        return 0

    lax.fori_loop(0, IMAGES // 8, image_group, 0, unroll=4)
    both = [[], []]
    for g in range(IMAGES // 8):
        vals = [stage[pl.ds(g * 64 + k * 8, 8), :] for k in range(8)]
        for bit in range(3):
            vals = halves(bit, vals)
        both[g // 16].append(vals[0])
    for bit in range(3, 7):
        both = [halves(bit, vals) for vals in both]
    sub = lax.broadcasted_iota(I32, (8, 128), 0)
    second = pltpu.roll(both[1][0], VARS, axis=0)
    tabs[pl.ds(al(yz * 16), 8), :] = jnp.where(sub < VARS, both[0][0], second)
    tabs[pl.ds(al(yz * 16 + 8), 8), :] = second

    for copy in got_rest:
        copy.wait()
    req[pl.ds(al(slot * 8), 8), :] = jnp.concatenate(
        [gown[...], gimg[...], jnp.zeros((6, GHOSTS), I32)], axis=0
    )

    pl.semaphore_wait(barrier, slabs - 1 + (cross - 1) * 2)

    def send_table(j, _):
        half = planes // 2
        d = lax.rem(yz + jnp.where(j < half, half + j, planes - 1 - j), planes)
        mine = pl.ds(al(yz * 16), 2 * VARS)
        send(tabs.at[mine, :], tabs.at[mine, :], 0, (d * 2 + core, c))
        return 0

    lax.fori_loop(0, planes - 1, send_table, 0)
    row_peers = [
        (yz * 2 + lax.rem(core + dk, 2), lax.rem(c + dc, cross))
        for dc in range(cross)
        for dk in range(2)
        if dc or dk
    ]
    for dev in row_peers:
        mine = pl.ds(al(slot * 8), 2)
        send(req.at[mine, :], req.at[mine, :], 1, dev)

    for rt in range(2):
        for lt in range(tiles):
            cols = pl.ds(lt * 128, 128)
            rows = pl.ds(rt * 8, 8)
            solid = mask[rows, cols] == 1
            place = (lt % 3) * 8 + lt // 3
            for v in range(VARS):
                fbuf[pl.ds((v * ROWS + rt * 8) * 24 + place, 8, stride=24), :] = jnp.where(
                    solid, 0.0, state[v, rows, cols]
                )
            crow[pl.ds(rt * 8 * 24 + place, 8, stride=24), :] = cour[rows, cols]
            arow[pl.ds(rt * 8 * 24 + place, 8, stride=24), :] = phi[rows, cols]

    cell = gcell[...]
    x = cell >> 7
    r = (x * magic) >> 16
    t = x - r * tiles
    t3 = (t * 21846) >> 16
    at_row = r * 24 + (t - t3 * 3) * 8 + t3
    ghost_no = (lax.broadcasted_iota(I32, (1, GHOSTS), 1) + 1).astype(F32)
    row_no = lax.broadcasted_iota(I32, (ROWS * 24, GHOSTS), 0)
    left = jnp.where(row_no == at_row, ghost_no, 0.0).astype(jnp.bfloat16)
    lane_no = lax.broadcasted_iota(I32, (128, GHOSTS), 0)
    right = jnp.where(lane_no == (cell & 127), 1.0, 0.0).astype(jnp.bfloat16)
    numbers = lax.dot_general(left, right, (((1,), (1,)), ((), ())), preferred_element_type=F32)
    gmap[...] = (numbers + 0.5).astype(I32) - 1

    def rowof(ref, i):
        return ref[pl.ds(i * 24, 24), :]

    def put(ref, i, val):
        ref[pl.ds(i * 24, 24), :] = val

    E, H, RD, WL, WR, C = 0, 16, 32, 48, 64, 80
    top = jnp.where(p == slabs - 1, 0.0, 1.0)
    h = rowof(arow, 0)
    m = jnp.ones_like(h)
    m_l = jnp.ones_like(h)
    faces = arow
    for k in range(1, ROWS):
        face = rowof(faces, k)
        if k == ROWS - 1:
            face = face * top
        rd = 1.0 / (h + face + m)
        e = face * rd
        hh = h * rd
        put(arow, 16 + E + k, e)
        put(arow, 16 + H + k, hh)
        put(arow, 16 + RD + k, rd)
        m_l = m_l + m * hh
        h = h * e
        m = 1.0 + m * e
    w_l = jnp.zeros_like(h)
    w_r = jnp.ones_like(h)
    cols = [jnp.zeros_like(h) for _ in range(4)]
    for k in range(ROWS - 1, 0, -1):
        e = rowof(arow, 16 + E + k)
        w_l = rowof(arow, 16 + H + k) + e * w_l
        w_r = e * w_r
        put(arow, 16 + WL + k, w_l)
        put(arow, 16 + WR + k, w_r)
        ck = rowof(crow, k)
        cl, cr = w_l * ck, w_r * ck
        u, v = tab[0, T_U + k], tab[0, T_V + k]
        cols = [cols[0] - u * cl, cols[1] - u * cr, cols[2] - v * cl, cols[3] - v * cr]
        if k == ROWS - 1:
            k1, k2 = -tab[0, T_DR] * cl, -tab[0, T_DR] * cr
    c0 = rowof(crow, 0)
    cols[0] = cols[0] - tab[0, T_U] * c0
    cols[2] = cols[2] - tab[0, T_V] * c0
    for k, val in enumerate((h, m_l, m - 1.0, *cols)):
        for b in range(3):
            coef_out[pl.ds(b * 8 + k, 8, stride=24), :] = val[b * 8 : b * 8 + 8, :]
    for k, val in enumerate((-tab[0, T_DL] * c0, k1, k2)):
        side_out[pl.ds(k * 24, 24), :] = val

    def first_tile(d):
        return (UNITS * d) // VARS

    def has_two(d):
        return jnp.logical_and(d < solvers, lax.rem(UNITS * d, VARS) > VARS - UNITS)

    n_two = sum((UNITS * d) % VARS > VARS - UNITS for d in range(solvers))

    def send_coef(i, _):
        d = lax.rem(p + i, slabs)

        @pl.when(d < solvers)
        def _():
            send(
                coef_out.at[pl.ds(al(first_tile(d) * 8), 8), :],
                coef_in.at[pl.ds(al(p * 16), 8), :],
                2,
                (d, c),
            )

        @pl.when(has_two(d))
        def _():
            send(
                coef_out.at[pl.ds(al(first_tile(d) * 8 + 8), 8), :],
                coef_in.at[pl.ds(al(p * 16 + 8), 8), :],
                8,
                (d, c),
            )

        return 0

    wait(recv_sem, 0, tabs, (planes - 1) * 2 * VARS)
    wait(recv_sem, 1, req, (slots - 1) * 2)
    owner = req[pl.ds(0, slots, stride=8), :]
    image = req[pl.ds(1, slots, stride=8), :]
    o_c = lax.rem(owner, cross)
    o_p = lax.div(owner, cross)
    held = jnp.logical_and(o_c == c, (o_p & 1) == core)
    which = jnp.where(held, (o_p >> 1) * 2 + (image >> 7), jnp.full_like(owner, -1))
    spot7 = jnp.zeros_like(image)
    for bit in range(7):
        spot7 = spot7 | (((image >> bit) & 1) << IMAGE_BITS[bit])
    tables = []
    for k in range(planes):
        first, second = tabs[pl.ds(k * 16, 8), :], tabs[pl.ds(k * 16 + 8, 8), :]
        back = 8 - VARS
        tables += [
            first,
            jnp.where(sub < back, pltpu.roll(first, back, axis=0), pltpu.roll(second, back, axis=0)),
        ]
    for n in range(slots):
        idx = jnp.broadcast_to(spot7[n : n + 1, :], (8, 128))
        wh = jnp.broadcast_to(which[n : n + 1, :], (8, 128))
        acc = jnp.zeros((8, 128), F32)
        for k in range(planes * 2):
            got = jnp.take_along_axis(tables[k], idx, axis=1, mode="promise_in_bounds")
            acc = jnp.where(wh == k, got, acc)
        pick_out[pl.ds(n * 8, 8), :] = acc

    for dev in row_peers:
        send(
            pick_out.at[pl.ds(al((dev[1] * 2 + lax.rem(dev[0], 2)) * 8), VARS), :],
            pick_in.at[pl.ds(al(slot * 8), VARS), :],
            3,
            dev,
        )
    pick_in[pl.ds(al(slot * 8), 8), :] = pick_out[pl.ds(al(slot * 8), 8), :]

    send(side_out.at[pl.ds(0, 24), :], side_in.at[pl.ds(0, 24), :], 9, (before, c))
    send(side_out.at[pl.ds(24, 48), :], side_in.at[pl.ds(24, 48), :], 10, (after, c))
    lax.fori_loop(1, slabs, send_coef, 0)

    @pl.when(is_solver)
    def _():
        coef_in[pl.ds(al(p * 16), 16), :] = coef_out[pl.ds(al(first_tile(p) * 8), 16), :]

    wait(recv_sem, 3, pick_in, (slots - 1) * VARS)
    ghost = pick_in[pl.ds(0, 8), :]
    for n in range(1, slots):
        ghost = ghost + pick_in[pl.ds(n * 8, 8), :]
    ghost = [jnp.broadcast_to(REFLECT[v] * ghost[v : v + 1, :], (8, 128)) for v in range(VARS)]

    def tv(i):
        return tab[0, i]

    wait(recv_sem, 9, side_in, 24)
    wait(recv_sem, 10, side_in, 48)

    def send_class(k):
        def one(i, _):
            d = 5 * lax.rem(p + i, tiles // 3) + k

            @pl.when(d != p)
            def _():
                send(
                    dat_out.at[pl.ds(al(d * 16), 16), :],
                    dat_in.at[pl.ds(al(p * 16), 16), :],
                    4,
                    (d, c),
                )

            return 0

        lax.fori_loop(0, tiles // 3, one, 0)

    def local(b, _):
        def at(row):
            return pl.ds(al(row * 24 + b * 8), 8)

        def filled(i):
            gi = gmap[at(i), :]
            has = gi >= 0
            idx = jnp.maximum(gi, 0)
            out = []
            for v in range(VARS):
                got = jnp.take_along_axis(ghost[v], idx, axis=1, mode="promise_in_bounds")
                val = jnp.where(has, got, fbuf[at(v * ROWS + i), :])
                fbuf[at(v * ROWS + i), :] = val
                out.append(val)
            return out

        f = [filled(i) for i in range(ROWS)]
        for v in range(VARS):
            fv = [f[i][v] for i in range(ROWS)]
            up = tv(T_K) * fv[0]
            for i in range(ROWS):
                if i == 0:
                    hi = tv(T_H0) * fv[0] + tv(T_H0 + 1) * fv[1] + tv(T_H0 + 2) * fv[2]
                elif i == 1:
                    hi = sum(tv(T_H1 + k) * fv[k] for k in range(4))
                elif i == ROWS - 2:
                    hi = sum(tv(T_H14 + k) * fv[12 + k] for k in range(4))
                elif i == ROWS - 1:
                    hi = sum(tv(T_H15 + k) * fv[13 + k] for k in range(3))
                else:
                    hi = tv(T_K + 1 + i) * (fv[i + 1] - fv[i - 1])
                up = tv(T_R + i) * up + hi
                xrow[at(v * ROWS + i), :] = up
                srow[at(v * ROWS + i), :] = hi
            end = tv(T_K + 1 + ROWS) * fv[ROWS - 1]
            z_l = tv(T_R + ROWS) * up - end
            down = -end
            s_l = s_r = None
            for i in range(ROWS - 1, -1, -1):
                down = tv(T_S + 1 + i) * down
                xi = xrow[at(v * ROWS + i), :] + down
                if i == 0:
                    xi = xi + tv(T_D0) * fv[1]
                elif i == ROWS - 1:
                    xi = xi - tv(T_D15) * fv[ROWS - 2]
                else:
                    xi = xi + (1.0 / 12.0) * (fv[i + 1] - fv[i - 1])
                xrow[at(v * ROWS + i), :] = xi
                down = down + srow[at(v * ROWS + i), :]
                rhs = fv[i] - crow[at(i), :] * xi
                if i:
                    wl, wr = arow[at(16 + WL + i), :], arow[at(16 + WR + i), :]
                    s_l = wl * rhs if s_l is None else s_l + wl * rhs
                    s_r = wr * rhs if s_r is None else s_r + wr * rhs
                else:
                    s_l = s_l + rhs
            z_r = tv(T_S) * down + tv(T_K) * fv[0]
            s_r = s_r + side_in[at(0), :] * fv[ROWS - 1]
            s_b = side_in[at(1), :] * fv[0]
            s_l = s_l + side_in[at(2), :] * fv[0]
            w = 5 * b + v
            for k, val in enumerate((z_l, z_r, s_l, s_r, s_b)):
                dat_out[pl.ds((w // 3) * 16 + (w % 3) * 5 + k, 8, stride=80), :] = val
            halo_out[pl.ds(al(v * 24 + b * 8), 8), :] = fv[0]
            halo_out[pl.ds(al(120 + v * 24 + b * 8), 8), :] = fv[ROWS - 1]
        send_class(2 * b)

        @pl.when(b > 0)
        def _():
            send_class(2 * b - 1)

        return 0

    lax.fori_loop(0, 3, local, 0)

    @pl.when(is_solver)
    def _():
        wait(recv_sem, 2, coef_in, (slabs - 1) * 8)

        @pl.when(has_two(p))
        def _():
            wait(recv_sem, 8, coef_in, (slabs - 1) * 8)

        for j in range(2):

            def field(k):
                return coef_in[pl.ds(j * 8 + k, slabs, stride=16), :]

            gu = field(0)
            gl = pltpu.roll(gu, 1, axis=0)
            mm = field(1) + pltpu.roll(field(2), 1, axis=0)
            step, s = 0, 1
            while s < slabs:
                rd = 1.0 / (mm + gl + gu)
                pf = gl * pltpu.roll(rd, s, axis=0)
                tf = gu * pltpu.roll(rd, slabs - s, axis=0)
                at0 = ((j * 6 + step) * 2) * slabs
                fac[pl.ds(at0, slabs), :] = pf
                fac[pl.ds(at0 + slabs, slabs), :] = tf
                mm = mm + pf * pltpu.roll(mm, s, axis=0) + tf * pltpu.roll(mm, slabs - s, axis=0)
                gl = pf * pltpu.roll(gl, s, axis=0)
                gu = tf * pltpu.roll(gu, slabs - s, axis=0)
                step, s = step + 1, s * 2
            fac[pl.ds((j * 6 + 5) * 2 * slabs, slabs), :] = 1.0 / (mm + gl + gu)

    send(halo_out.at[pl.ds(0, 120), :], halo_in.at[pl.ds(0, 120), :], 5, (before, c))
    send(halo_out.at[pl.ds(120, 120), :], halo_in.at[pl.ds(120, 120), :], 6, (after, c))

    @pl.when(is_solver)
    def _():
        dat_in[pl.ds(al(p * 16), 16), :] = dat_out[pl.ds(al(p * 16), 16), :]
        wait(recv_sem, 4, dat_in, (slabs - 1) * 16)

        def data(u, k):
            return dat_in[pl.ds(u * 5 + k, slabs, stride=16), :]

        z_l = jnp.concatenate([data(u, 0) for u in range(UNITS)], axis=1)
        z_r = jnp.concatenate([data(u, 1) for u in range(UNITS)], axis=1)
        hi = lax.Precision.HIGHEST
        c_l = jnp.dot(lam[pl.ds(0, slabs), :], z_l, precision=hi, preferred_element_type=F32)
        c_r = jnp.dot(lam[pl.ds(slabs, slabs), :], z_r, precision=hi, preferred_element_type=F32)
        for u in range(UNITS):
            j = (UNITS * p + u) // VARS - first_tile(p)

            def field(k):
                return coef_in[pl.ds(j * 8 + k, slabs, stride=16), :]

            cl, cr = c_l[:, u * 128 : u * 128 + 128], c_r[:, u * 128 : u * 128 + 128]
            q = data(u, 3) + field(4) * cl + field(6) * cr
            d = data(u, 2) + field(3) * cl + field(5) * cr + pltpu.roll(data(u, 4), slabs - 1, axis=0)
            d = d + pltpu.roll(q, 1, axis=0)
            step, s = 0, 1
            while s < slabs:
                at0 = ((j * 6 + step) * 2) * slabs
                pf = fac[pl.ds(al(at0), slabs), :]
                tf = fac[pl.ds(al(at0 + slabs), slabs), :]
                d = d + pf * pltpu.roll(d, s, axis=0) + tf * pltpu.roll(d, slabs - s, axis=0)
                step, s = step + 1, s * 2
            x = d * fac[pl.ds(al((j * 6 + 5) * 2 * slabs), slabs), :]
            for k, val in enumerate((cl, cr, x, pltpu.roll(x, slabs - 1, axis=0))):
                ret_out[pl.ds(u * 4 + k, slabs, stride=16), :] = val

        def send_ret(i, _):
            d = lax.rem(p + i, slabs)
            send(ret_out.at[pl.ds(al(d * 16), 12), :], ret_in.at[pl.ds(al(p * 16), 12), :], 7, (d, c))
            return 0

        lax.fori_loop(1, slabs, send_ret, 0)
        ret_in[pl.ds(al(p * 16), 16), :] = ret_out[pl.ds(al(p * 16), 16), :]
        wait(recv_sem, 7, ret_in, (solvers - 1) * 12)

    @pl.when(jnp.logical_not(is_solver))
    def _():
        wait(recv_sem, 7, ret_in, solvers * 12)

    wait(recv_sem, 5, halo_in, 120)
    wait(recv_sem, 6, halo_in, 120)

    def finish(b, _):
        def at(row):
            return pl.ds(al(row * 24 + b * 8), 8)

        def natural(which, v, i):
            return pl.ds((((which * VARS + v) * 2 + i // 8) * tiles + b) * 8 + i % 8, tiles // 3, stride=24)

        for v in range(VARS):
            w = 5 * b + v

            def back(k):
                return ret_in[pl.ds((w // 3) * 16 + (w % 3) * 4 + k, 8, stride=80), :]

            left_c, right_c, t0, t1 = back(0), back(1), back(2), back(3)
            above = halo_in[at(v), :]
            below = halo_in[at(5 + v), :]
            run = None
            for i in range(ROWS):
                xi = xrow[at(v * ROWS + i), :] + tv(T_U + i) * left_c + tv(T_V + i) * right_c
                if i == 0:
                    xi = xi + tv(T_DL) * below
                if i == ROWS - 1:
                    xi = xi + tv(T_DR) * above
                out[natural(0, v, i), :] = xi[: tiles // 3]
                if i:
                    rhs = fbuf[at(v * ROWS + i), :] - crow[at(i), :] * xi
                    run = rhs if run is None else rhs + arow[at(16 + E + i - 1), :] * run
                    srow[at(v * ROWS + i), :] = (
                        arow[at(16 + RD + i), :] * run + arow[at(16 + H + i), :] * t0
                    )
            y = t1
            for i in range(ROWS - 1, 0, -1):
                y = srow[at(v * ROWS + i), :] + arow[at(16 + E + i), :] * y
                out[natural(1, v, i), :] = y[: tiles // 3]
            out[natural(1, v, 0), :] = t0[: tiles // 3]
        return 0

    lax.fori_loop(0, 3, finish, 0)
    wait(send_sem, 0, tabs, (planes - 1) * 2 * VARS)
    wait(send_sem, 1, req, (slots - 1) * 2)
    wait(send_sem, 3, pick_in, (slots - 1) * VARS)
    wait(send_sem, 5, halo_in, 120)
    wait(send_sem, 6, halo_in, 120)
    wait(send_sem, 9, side_in, 24)
    wait(send_sem, 10, side_in, 48)

    @pl.when(is_solver)
    def _():
        wait(send_sem, 2, coef_in, (solvers - 1) * 8)
        wait(send_sem, 4, dat_in, (solvers - 1) * 16)
        wait(send_sem, 7, ret_out, (slabs - 1) * 12)

    @pl.when(jnp.logical_not(is_solver))
    def _():
        wait(send_sem, 2, coef_in, solvers * 8)
        wait(send_sem, 4, dat_in, solvers * 16)

    @pl.when(has_two(p))
    def _():
        wait(send_sem, 8, coef_in, (n_two - 1) * 8)

    @pl.when(jnp.logical_not(has_two(p)))
    def _():
        wait(send_sem, 8, coef_in, n_two * 8)


def solution(mesh):
    slabs, cross = mesh.shape["pipe"], mesh.shape["cross"]
    table, carry = derivative_constants(slabs)

    def local(state, face, courant, cell_mask, ghost_cell, ghost_owner, ghost_image, base, weight):
        pencils = state.shape[2]
        tiles = pencils // 128
        solvers = -(-(VARS * tiles) // UNITS)
        planes, slots = slabs // 2, cross * 2
        span = VARS * ROWS * 24

        def buf(rows, dtype=F32):
            return pltpu.VMEM((rows, 128), dtype)

        out = pl.pallas_call(
            functools.partial(kernel, slabs, cross, tiles),
            out_shape=pltpu.VMEM((2 * VARS * ROWS * tiles, 128), F32),
            in_specs=[pl.BlockSpec(memory_space=pl.ANY)] * 11,
            out_specs=pl.BlockSpec(memory_space=pltpu.VMEM),
            scratch_shapes=[
                pltpu.SMEM((1, 128), F32),
                pltpu.SMEM((1, IMAGES), I32),
                pltpu.VMEM((2 * slabs, slabs), F32),
                pltpu.VMEM((1, IMAGES), I32),
                pltpu.VMEM(state.shape, F32),
                pltpu.VMEM(face.shape, F32),
                pltpu.VMEM(face.shape, F32),
                pltpu.VMEM(face.shape, I32),
                pltpu.VMEM((1, GHOSTS), I32),
                pltpu.VMEM((1, GHOSTS), I32),
                pltpu.VMEM((1, GHOSTS), I32),
                pltpu.VMEM((8, IMAGES), F32),
                buf(ROWS * (tiles + 1) * 8),
                buf(2 * IMAGES),
                buf(IMAGES * 8),
                buf(planes * 16),
                buf(slots * 8, I32),
                buf(slots * 8),
                buf(slots * 8),
                buf(ROWS * 24, I32),
                buf(span),
                buf(span),
                buf(span),
                buf(ROWS * 24),
                buf(ROWS * 24 * 6),
                buf(192),
                buf(slabs * 16),
                buf(24 * slabs),
                buf(72),
                buf(72),
                buf(640),
                buf(slabs * 16),
                buf(slabs * 16),
                buf(max(640, solvers * 16)),
                buf(240),
                buf(240),
                pltpu.SemaphoreType.DMA((16,)),
                pltpu.SemaphoreType.DMA((11,)),
                pltpu.SemaphoreType.DMA((11,)),
            ],
            compiler_params=pltpu.CompilerParams(
                collective_id=0, has_side_effects=True, vmem_limit_bytes=62 * 1024 * 1024
            ),
        )(
            jnp.asarray(table).reshape(slabs, 1, 128), jnp.asarray(carry), base.reshape(1, -1),
            state, face, courant, cell_mask,
            ghost_cell.reshape(1, -1), ghost_owner.reshape(1, -1), ghost_image.reshape(1, -1), weight,
        )
        out = out.reshape(2, VARS, 2, tiles, 8, 128).transpose(0, 1, 2, 4, 3, 5).reshape(2, *state.shape)
        return out[0], out[1]

    flat = P(("pipe", "cross"))
    slab = P("pipe", "cross")
    whole = P(None, "pipe", "cross")
    return jax.shard_map(
        local,
        mesh=mesh,
        in_specs=(whole, slab, slab, slab, flat, flat, flat, flat, P(None, ("pipe", "cross"))),
        out_specs=(whole, whole),
        check_vma=False,
    )
```

```python
import functools

import jax
import jax.numpy as jnp
import numpy as np
from jax import lax
from jax.experimental import pallas as pl
from jax.experimental.pallas import tpu as pltpu
from jax.sharding import PartitionSpec as P

VARS = 5
ROWS = 16
GHOSTS = 128
IMAGES = 256
UNITS = 3
IMAGE_BITS = (2, 1, 0, 6, 5, 4, 3)
REFLECT = (1.0, -1.0, -1.0, -1.0, 1.0)
F32 = jnp.float32
I32 = jnp.int32
MESH = pl.DeviceIdType.MESH

T_R = 0
T_S = 17
T_K = 34
T_U = 52
T_V = 68
T_H0 = 84
T_H1 = 87
T_H14 = 91
T_H15 = 95
T_D0, T_D15, T_DL, T_DR = 98, 99, 100, 101


def derivative_constants(slabs):
    n = slabs * ROWS
    side = np.full(n, 1.0 / 3.0)
    side[1] = side[n - 2] = 0.25
    side[0] = side[n - 1] = 0.0
    delta, eps = np.ones(n), np.ones(n)
    for k in range(n - 2, -1, -1):
        delta[k] = 1.0 - side[k] * side[k + 1] / delta[k + 1]
    for k in range(1, n):
        eps[k] = 1.0 - side[k] * side[k - 1] / eps[k - 1]
    r, s, e = -side / delta, -side / eps, 1.0 / (delta + eps - 1.0)

    def at(x, i):
        return x[i] if 0 <= i < n else 0.0

    table = np.zeros((slabs, 128))
    decay_l, decay_r = np.zeros(slabs), np.zeros(slabs)
    for p in range(slabs):
        g = p * ROWS
        row = table[p]
        kappa = {k: 25.0 / 36.0 * at(e, g + k) for k in range(-1, ROWS + 1)}
        for k in range(0, ROWS + 1):
            row[T_R + k] = at(r, g + k)
        for k in range(-1, ROWS):
            row[T_S + k + 1] = at(s, g + k)
        for k in range(-1, ROWS + 1):
            row[T_K + k + 1] = kappa[k]
        u = v = 1.0
        for k in range(ROWS):
            u = u * at(r, g + k) if k else 1.0
            row[T_U + k] = u
        for k in range(ROWS - 1, -1, -1):
            v = v * at(s, g + k) if k < ROWS - 1 else 1.0
            row[T_V + k] = v
        decay_l[p] = u * at(r, g + ROWS)
        decay_r[p] = v * at(s, g - 1)
        row[T_H0 : T_H0 + 3] = (0.0, kappa[0], 0.0)
        row[T_H1 : T_H1 + 4] = (-kappa[1], 0.0, kappa[1], 0.0)
        row[T_H14 : T_H14 + 4] = (0.0, -kappa[14], 0.0, kappa[14])
        row[T_H15 : T_H15 + 3] = (0.0, -kappa[15], 0.0)
        row[T_D0] = row[T_D15] = row[T_DR] = 1.0 / 12.0
        row[T_DL] = -1.0 / 12.0
        if p == 0:
            row[T_H0 : T_H0 + 3] = e[0] * np.array((-1.5, 2.0, -0.5))
            row[T_H1 : T_H1 + 4] = e[1] * np.array((-2.0 / 3.0, 1.0 / 48.0, 2.0 / 3.0, -1.0 / 48.0))
            row[T_D0] = row[T_DL] = 0.0
        if p == slabs - 1:
            row[T_H15 : T_H15 + 3] = e[n - 1] * np.array((0.5, -2.0, 1.5))
            row[T_H14 : T_H14 + 4] = e[n - 2] * np.array((1.0 / 48.0, -2.0 / 3.0, -1.0 / 48.0, 2.0 / 3.0))
            row[T_D15] = row[T_DR] = 0.0
    carry = np.zeros((2 * slabs, slabs))
    for p in range(slabs):
        w = 1.0
        for q in range(p - 1, -1, -1):
            carry[p, q] = w
            w *= decay_l[q]
        w = 1.0
        for q in range(p + 1, slabs):
            carry[slabs + p, q] = w
            w *= decay_r[q]
    return table.astype(np.float32), carry.astype(np.float32)


def kernel(
    slabs, cross, tiles,
    tab_hbm, lam_hbm, base_hbm, state_hbm, phi_hbm, cour_hbm, mask_hbm, gcell_hbm, gown_hbm, gimg_hbm, wts_hbm,
    fbuf, xrow, crow, arow, returns, ends, scale,
    tab, base_s, lam, base_v, state, phi, cour, mask, gcell, gown, gimg, wts,
    xbuf, win, stage, tabs, req, pick_out, pick_in, gmap, srow,
    coef_out, coef_in, fac, side_out, side_in, dat_out, dat_in, ret_out, ret_in, halo_out, halo_in,
    in_sem, send_sem, recv_sem,
):
    p = lax.axis_index("pipe")
    c = lax.axis_index("cross")
    yz, core = p // 2, p % 2
    planes = slabs // 2
    slot = c * 2 + core
    slots = cross * 2
    tp = tiles + 1
    magic = -(-65536 // tiles)
    solvers = -(-(VARS * tiles) // UNITS)
    is_solver = p < solvers
    before, after = lax.rem(p + slabs - 1, slabs), lax.rem(p + 1, slabs)

    def fetch(k, src, dst):
        copy = pltpu.make_async_copy(src, dst, in_sem.at[k])
        copy.start()
        return copy

    got_base = fetch(1, base_hbm, base_v)
    got_wts = fetch(3, wts_hbm, wts)
    got_state = [fetch(0, state_hbm, state)]
    got_base_s = fetch(2, base_hbm, base_s)
    barrier = pltpu.get_barrier_semaphore()

    def greet(i, _):
        pl.semaphore_signal(barrier, inc=1, device_id=(lax.rem(p + i, slabs), c), device_id_type=MESH)
        return 0

    lax.fori_loop(1, slabs, greet, 0)
    for dc in range(1, cross):
        for k in range(2):
            pl.semaphore_signal(
                barrier, inc=1, device_id=(yz * 2 + k, lax.rem(c + dc, cross)), device_id_type=MESH
            )

    got_rest = [
        fetch(4, mask_hbm, mask),
        fetch(5, phi_hbm, phi),
        fetch(6, cour_hbm, cour),
        fetch(7, gcell_hbm, gcell),
        fetch(8, gown_hbm, gown),
        fetch(9, gimg_hbm, gimg),
        fetch(10, tab_hbm.at[p], tab),
        fetch(11, lam_hbm, lam),
    ]

    def send(src, dst, sem, dev):
        pltpu.make_async_remote_copy(
            src_ref=src,
            dst_ref=dst,
            send_sem=send_sem.at[sem],
            recv_sem=recv_sem.at[sem],
            device_id=dev,
            device_id_type=MESH,
        ).start()

    def wait(sems, sem, ref, rows):
        part = ref.at[pl.ds(0, rows), :]
        pltpu.make_async_copy(part, part, sems.at[sem]).wait()

    def al(x):
        return pl.multiple_of(x, 8)

    lane = lax.broadcasted_iota(I32, (8, 128), 1)
    got_base.wait()
    got_wts.wait()
    spot = jnp.broadcast_to((base_v[...] & 127).astype(F32), (8, IMAGES)).T
    cols8 = wts[...].T
    for g in range(IMAGES // 8):
        here = spot[g * 8 : g * 8 + 8, 0:1].astype(I32)
        rel = (lane - here) & 127
        w = [jnp.broadcast_to(cols8[g * 8 : g * 8 + 8, k : k + 1], (8, 128)) for k in range(8)]
        for row in range(2):
            m = jnp.zeros((8, 128), F32)
            for k, off in enumerate((0, 1, 96, 97)):
                m = jnp.where(rel == off, w[row * 4 + k], m)
            win[pl.ds(row * IMAGES + g * 8, 8), :] = m

    for r in range(ROWS):
        xbuf[pl.ds((r * tp + tiles) * 8, 8), :] = jnp.zeros((8, 128), F32)
    for copy in got_state:
        copy.wait()
    for rt in range(2):
        for lt in range(tiles):
            for v in range(VARS):
                nat = state[v, pl.ds(rt * 8, 8), pl.ds(lt * 128, 128)]
                xbuf[pl.ds((rt * 8 * tp + lt) * 8 + v, 8, stride=tp * 8), :] = nat
    got_base_s.wait()
    blocks = xbuf.reshape(ROWS * tp, 8, 128)

    def merge(bit, a, b):
        low = ((lane >> bit) & 1) == 0
        return jnp.where(low, a, b) + pltpu.roll(jnp.where(low, b, a), 128 - (1 << bit), axis=1)

    def halves(bit, vals):
        n = len(vals) // 2
        return [merge(bit, vals[i], vals[i + n]) for i in range(n)]

    def image_group(g, _):
        m0 = win[pl.ds(al(g * 8), 8), :]
        m1 = win[pl.ds(al(IMAGES + g * 8), 8), :]
        vals = []
        for k in range(8):
            b = base_s[0, g * 8 + k]
            x = b >> 7
            r = (x * magic) >> 16
            off = x + r
            inside = lane >= (b & 127)
            z0 = jnp.where(inside, blocks[off], blocks[off + 1])
            z1 = jnp.where(inside, blocks[off + tp], blocks[off + tp + 1])
            stage[pl.ds(al(g * 64 + k * 8), 8), :] = z0 * m0[k : k + 1, :] + z1 * m1[k : k + 1, :]
        return 0

    lax.fori_loop(0, IMAGES // 8, image_group, 0, unroll=4)
    both = [[], []]
    for g in range(IMAGES // 8):
        vals = [stage[pl.ds(g * 64 + k * 8, 8), :] for k in range(8)]
        for bit in range(3):
            vals = halves(bit, vals)
        both[g // 16].append(vals[0])
    for bit in range(3, 7):
        both = [halves(bit, vals) for vals in both]
    sub = lax.broadcasted_iota(I32, (8, 128), 0)
    second = pltpu.roll(both[1][0], VARS, axis=0)
    tabs[pl.ds(al(yz * 16), 8), :] = jnp.where(sub < VARS, both[0][0], second)
    tabs[pl.ds(al(yz * 16 + 8), 8), :] = second

    for copy in got_rest:
        copy.wait()
    req[pl.ds(al(slot * 8), 8), :] = jnp.concatenate(
        [gown[...], gimg[...], jnp.zeros((6, GHOSTS), I32)], axis=0
    )

    pl.semaphore_wait(barrier, slabs - 1 + (cross - 1) * 2)

    def send_table(j, _):
        half = planes // 2
        d = lax.rem(yz + jnp.where(j < half, half + j, planes - 1 - j), planes)
        mine = pl.ds(al(yz * 16), 2 * VARS)
        send(tabs.at[mine, :], tabs.at[mine, :], 0, (d * 2 + core, c))
        return 0

    lax.fori_loop(0, planes - 1, send_table, 0)
    row_peers = [
        (yz * 2 + lax.rem(core + dk, 2), lax.rem(c + dc, cross))
        for dc in range(cross)
        for dk in range(2)
        if dc or dk
    ]
    for dev in row_peers:
        mine = pl.ds(al(slot * 8), 2)
        send(req.at[mine, :], req.at[mine, :], 1, dev)

    for rt in range(2):
        for lt in range(tiles):
            cols = pl.ds(lt * 128, 128)
            rows = pl.ds(rt * 8, 8)
            solid = mask[rows, cols] == 1
            place = (lt % 3) * 8 + lt // 3
            for v in range(VARS):
                fbuf[pl.ds((v * ROWS + rt * 8) * 24 + place, 8, stride=24), :] = jnp.where(
                    solid, 0.0, state[v, rows, cols]
                )
            crow[pl.ds(rt * 8 * 24 + place, 8, stride=24), :] = cour[rows, cols]
            arow[pl.ds(rt * 8 * 24 + place, 8, stride=24), :] = phi[rows, cols]

    cell = gcell[...]
    x = cell >> 7
    r = (x * magic) >> 16
    t = x - r * tiles
    t3 = (t * 21846) >> 16
    at_row = r * 24 + (t - t3 * 3) * 8 + t3
    ghost_no = (lax.broadcasted_iota(I32, (1, GHOSTS), 1) + 1).astype(F32)
    row_no = lax.broadcasted_iota(I32, (ROWS * 24, GHOSTS), 0)
    left = jnp.where(row_no == at_row, ghost_no, 0.0).astype(jnp.bfloat16)
    lane_no = lax.broadcasted_iota(I32, (128, GHOSTS), 0)
    right = jnp.where(lane_no == (cell & 127), 1.0, 0.0).astype(jnp.bfloat16)
    numbers = lax.dot_general(left, right, (((1,), (1,)), ((), ())), preferred_element_type=F32)
    gmap[...] = (numbers + 0.5).astype(I32) - 1

    def rowof(ref, i):
        return ref[pl.ds(i * 24, 24), :]

    def put(ref, i, val):
        ref[pl.ds(i * 24, 24), :] = val

    E, H, RD, WL, WR, C = 0, 16, 32, 48, 64, 80
    top = jnp.where(p == slabs - 1, 0.0, 1.0)
    h = rowof(arow, 0)
    m = jnp.ones_like(h)
    m_l = jnp.ones_like(h)
    faces = arow
    for k in range(1, ROWS):
        face = rowof(faces, k)
        if k == ROWS - 1:
            face = face * top
        rd = 1.0 / (h + face + m)
        e = face * rd
        hh = h * rd
        put(arow, 16 + E + k, e)
        put(arow, 16 + H + k, hh)
        put(arow, 16 + RD + k, rd)
        m_l = m_l + m * hh
        h = h * e
        m = 1.0 + m * e
    w_l = jnp.zeros_like(h)
    w_r = jnp.ones_like(h)
    cols = [jnp.zeros_like(h) for _ in range(4)]
    for k in range(ROWS - 1, 0, -1):
        e = rowof(arow, 16 + E + k)
        w_l = rowof(arow, 16 + H + k) + e * w_l
        w_r = e * w_r
        put(arow, 16 + WL + k, w_l)
        put(arow, 16 + WR + k, w_r)
        ck = rowof(crow, k)
        cl, cr = w_l * ck, w_r * ck
        u, v = tab[0, T_U + k], tab[0, T_V + k]
        cols = [cols[0] - u * cl, cols[1] - u * cr, cols[2] - v * cl, cols[3] - v * cr]
        if k == ROWS - 1:
            k1, k2 = -tab[0, T_DR] * cl, -tab[0, T_DR] * cr
    c0 = rowof(crow, 0)
    cols[0] = cols[0] - tab[0, T_U] * c0
    cols[2] = cols[2] - tab[0, T_V] * c0
    for k, val in enumerate((h, m_l, m - 1.0, *cols)):
        for b in range(3):
            coef_out[pl.ds(b * 8 + k, 8, stride=24), :] = val[b * 8 : b * 8 + 8, :]
    for k, val in enumerate((-tab[0, T_DL] * c0, k1, k2)):
        side_out[pl.ds(k * 24, 24), :] = val

    def first_tile(d):
        return (UNITS * d) // VARS

    def has_two(d):
        return jnp.logical_and(d < solvers, lax.rem(UNITS * d, VARS) > VARS - UNITS)

    n_two = sum((UNITS * d) % VARS > VARS - UNITS for d in range(solvers))

    def send_coef(i, _):
        d = lax.rem(p + i, slabs)

        @pl.when(d < solvers)
        def _():
            send(
                coef_out.at[pl.ds(al(first_tile(d) * 8), 8), :],
                coef_in.at[pl.ds(al(p * 16), 8), :],
                2,
                (d, c),
            )

        @pl.when(has_two(d))
        def _():
            send(
                coef_out.at[pl.ds(al(first_tile(d) * 8 + 8), 8), :],
                coef_in.at[pl.ds(al(p * 16 + 8), 8), :],
                8,
                (d, c),
            )

        return 0

    wait(recv_sem, 0, tabs, (planes - 1) * 2 * VARS)
    wait(recv_sem, 1, req, (slots - 1) * 2)
    owner = req[pl.ds(0, slots, stride=8), :]
    image = req[pl.ds(1, slots, stride=8), :]
    o_c = lax.rem(owner, cross)
    o_p = lax.div(owner, cross)
    held = jnp.logical_and(o_c == c, (o_p & 1) == core)
    which = jnp.where(held, (o_p >> 1) * 2 + (image >> 7), jnp.full_like(owner, -1))
    spot7 = jnp.zeros_like(image)
    for bit in range(7):
        spot7 = spot7 | (((image >> bit) & 1) << IMAGE_BITS[bit])
    tables = []
    for k in range(planes):
        first, second = tabs[pl.ds(k * 16, 8), :], tabs[pl.ds(k * 16 + 8, 8), :]
        back = 8 - VARS
        tables += [
            first,
            jnp.where(sub < back, pltpu.roll(first, back, axis=0), pltpu.roll(second, back, axis=0)),
        ]
    for n in range(slots):
        idx = jnp.broadcast_to(spot7[n : n + 1, :], (8, 128))
        wh = jnp.broadcast_to(which[n : n + 1, :], (8, 128))
        acc = jnp.zeros((8, 128), F32)
        for k in range(planes * 2):
            got = jnp.take_along_axis(tables[k], idx, axis=1, mode="promise_in_bounds")
            acc = jnp.where(wh == k, got, acc)
        pick_out[pl.ds(n * 8, 8), :] = acc

    for dev in row_peers:
        send(
            pick_out.at[pl.ds(al((dev[1] * 2 + lax.rem(dev[0], 2)) * 8), VARS), :],
            pick_in.at[pl.ds(al(slot * 8), VARS), :],
            3,
            dev,
        )
    pick_in[pl.ds(al(slot * 8), 8), :] = pick_out[pl.ds(al(slot * 8), 8), :]

    send(side_out.at[pl.ds(0, 24), :], side_in.at[pl.ds(0, 24), :], 9, (before, c))
    send(side_out.at[pl.ds(24, 48), :], side_in.at[pl.ds(24, 48), :], 10, (after, c))
    lax.fori_loop(1, slabs, send_coef, 0)

    @pl.when(is_solver)
    def _():
        coef_in[pl.ds(al(p * 16), 16), :] = coef_out[pl.ds(al(first_tile(p) * 8), 16), :]

    wait(recv_sem, 3, pick_in, (slots - 1) * VARS)
    ghost = pick_in[pl.ds(0, 8), :]
    for n in range(1, slots):
        ghost = ghost + pick_in[pl.ds(n * 8, 8), :]
    ghost = [jnp.broadcast_to(REFLECT[v] * ghost[v : v + 1, :], (8, 128)) for v in range(VARS)]

    def tv(i):
        return tab[0, i]

    wait(recv_sem, 9, side_in, 24)
    wait(recv_sem, 10, side_in, 48)

    def send_class(k):
        def one(i, _):
            d = 5 * lax.rem(p + i, tiles // 3) + k

            @pl.when(d != p)
            def _():
                send(
                    dat_out.at[pl.ds(al(d * 16), 16), :],
                    dat_in.at[pl.ds(al(p * 16), 16), :],
                    4,
                    (d, c),
                )

            return 0

        lax.fori_loop(0, tiles // 3, one, 0)

    for k in range(2 * ROWS):
        scale[pl.ds(k, 1), :] = jnp.full((1, 128), tv(T_U + k), F32)
    for k in range(2):
        scale[pl.ds(2 * ROWS + k, 1), :] = jnp.full((1, 128), tv(T_DL + k), F32)

    def local(b, _):
        def at(row):
            return pl.ds(al(row * 24 + b * 8), 8)

        def filled(i):
            gi = gmap[at(i), :]
            has = gi >= 0
            idx = jnp.maximum(gi, 0)
            out = []
            for v in range(VARS):
                got = jnp.take_along_axis(ghost[v], idx, axis=1, mode="promise_in_bounds")
                val = jnp.where(has, got, fbuf[at(v * ROWS + i), :])
                fbuf[at(v * ROWS + i), :] = val
                out.append(val)
            return out

        f = [filled(i) for i in range(ROWS)]
        for v in range(VARS):
            fv = [f[i][v] for i in range(ROWS)]
            up = tv(T_K) * fv[0]
            for i in range(ROWS):
                if i == 0:
                    hi = tv(T_H0) * fv[0] + tv(T_H0 + 1) * fv[1] + tv(T_H0 + 2) * fv[2]
                elif i == 1:
                    hi = sum(tv(T_H1 + k) * fv[k] for k in range(4))
                elif i == ROWS - 2:
                    hi = sum(tv(T_H14 + k) * fv[12 + k] for k in range(4))
                elif i == ROWS - 1:
                    hi = sum(tv(T_H15 + k) * fv[13 + k] for k in range(3))
                else:
                    hi = tv(T_K + 1 + i) * (fv[i + 1] - fv[i - 1])
                up = tv(T_R + i) * up + hi
                xrow[at(v * ROWS + i), :] = up
                srow[at(v * ROWS + i), :] = hi
            end = tv(T_K + 1 + ROWS) * fv[ROWS - 1]
            z_l = tv(T_R + ROWS) * up - end
            down = -end
            s_l = s_r = None
            for i in range(ROWS - 1, -1, -1):
                down = tv(T_S + 1 + i) * down
                xi = xrow[at(v * ROWS + i), :] + down
                if i == 0:
                    xi = xi + tv(T_D0) * fv[1]
                elif i == ROWS - 1:
                    xi = xi - tv(T_D15) * fv[ROWS - 2]
                else:
                    xi = xi + (1.0 / 12.0) * (fv[i + 1] - fv[i - 1])
                xrow[at(v * ROWS + i), :] = xi
                down = down + srow[at(v * ROWS + i), :]
                rhs = fv[i] - crow[at(i), :] * xi
                if i:
                    wl, wr = arow[at(16 + WL + i), :], arow[at(16 + WR + i), :]
                    s_l = wl * rhs if s_l is None else s_l + wl * rhs
                    s_r = wr * rhs if s_r is None else s_r + wr * rhs
                else:
                    s_l = s_l + rhs
            z_r = tv(T_S) * down + tv(T_K) * fv[0]
            s_r = s_r + side_in[at(0), :] * fv[ROWS - 1]
            s_b = side_in[at(1), :] * fv[0]
            s_l = s_l + side_in[at(2), :] * fv[0]
            w = 5 * b + v
            for k, val in enumerate((z_l, z_r, s_l, s_r, s_b)):
                dat_out[pl.ds((w // 3) * 16 + (w % 3) * 5 + k, 8, stride=80), :] = val
            halo_out[pl.ds(al(v * 24 + b * 8), 8), :] = fv[0]
            halo_out[pl.ds(al(120 + v * 24 + b * 8), 8), :] = fv[ROWS - 1]
        send_class(2 * b)

        @pl.when(b > 0)
        def _():
            send_class(2 * b - 1)

        return 0

    lax.fori_loop(0, 3, local, 0)

    @pl.when(is_solver)
    def _():
        wait(recv_sem, 2, coef_in, (slabs - 1) * 8)

        @pl.when(has_two(p))
        def _():
            wait(recv_sem, 8, coef_in, (slabs - 1) * 8)

        for j in range(2):

            def field(k):
                return coef_in[pl.ds(j * 8 + k, slabs, stride=16), :]

            gu = field(0)
            gl = pltpu.roll(gu, 1, axis=0)
            mm = field(1) + pltpu.roll(field(2), 1, axis=0)
            step, s = 0, 1
            while s < slabs:
                rd = 1.0 / (mm + gl + gu)
                pf = gl * pltpu.roll(rd, s, axis=0)
                tf = gu * pltpu.roll(rd, slabs - s, axis=0)
                at0 = ((j * 6 + step) * 2) * slabs
                fac[pl.ds(at0, slabs), :] = pf
                fac[pl.ds(at0 + slabs, slabs), :] = tf
                mm = mm + pf * pltpu.roll(mm, s, axis=0) + tf * pltpu.roll(mm, slabs - s, axis=0)
                gl = pf * pltpu.roll(gl, s, axis=0)
                gu = tf * pltpu.roll(gu, slabs - s, axis=0)
                step, s = step + 1, s * 2
            fac[pl.ds((j * 6 + 5) * 2 * slabs, slabs), :] = 1.0 / (mm + gl + gu)

    send(halo_out.at[pl.ds(0, 120), :], halo_in.at[pl.ds(0, 120), :], 5, (before, c))
    send(halo_out.at[pl.ds(120, 120), :], halo_in.at[pl.ds(120, 120), :], 6, (after, c))

    @pl.when(is_solver)
    def _():
        dat_in[pl.ds(al(p * 16), 16), :] = dat_out[pl.ds(al(p * 16), 16), :]
        wait(recv_sem, 4, dat_in, (slabs - 1) * 16)

        def data(u, k):
            return dat_in[pl.ds(u * 5 + k, slabs, stride=16), :]

        z_l = jnp.concatenate([data(u, 0) for u in range(UNITS)], axis=1)
        z_r = jnp.concatenate([data(u, 1) for u in range(UNITS)], axis=1)
        hi = lax.Precision.HIGHEST
        c_l = jnp.dot(lam[pl.ds(0, slabs), :], z_l, precision=hi, preferred_element_type=F32)
        c_r = jnp.dot(lam[pl.ds(slabs, slabs), :], z_r, precision=hi, preferred_element_type=F32)
        for u in range(UNITS):
            j = (UNITS * p + u) // VARS - first_tile(p)

            def field(k):
                return coef_in[pl.ds(j * 8 + k, slabs, stride=16), :]

            cl, cr = c_l[:, u * 128 : u * 128 + 128], c_r[:, u * 128 : u * 128 + 128]
            q = data(u, 3) + field(4) * cl + field(6) * cr
            d = data(u, 2) + field(3) * cl + field(5) * cr + pltpu.roll(data(u, 4), slabs - 1, axis=0)
            d = d + pltpu.roll(q, 1, axis=0)
            step, s = 0, 1
            while s < slabs:
                at0 = ((j * 6 + step) * 2) * slabs
                pf = fac[pl.ds(al(at0), slabs), :]
                tf = fac[pl.ds(al(at0 + slabs), slabs), :]
                d = d + pf * pltpu.roll(d, s, axis=0) + tf * pltpu.roll(d, slabs - s, axis=0)
                step, s = step + 1, s * 2
            x = d * fac[pl.ds(al((j * 6 + 5) * 2 * slabs), slabs), :]
            for k, val in enumerate((cl, cr, x, pltpu.roll(x, slabs - 1, axis=0))):
                ret_out[pl.ds(u * 4 + k, slabs, stride=16), :] = val

        def send_ret(i, _):
            d = lax.rem(p + i, slabs)
            send(ret_out.at[pl.ds(al(d * 16), 12), :], ret_in.at[pl.ds(al(p * 16), 12), :], 7, (d, c))
            return 0

        lax.fori_loop(1, slabs, send_ret, 0)
        ret_in[pl.ds(al(p * 16), 16), :] = ret_out[pl.ds(al(p * 16), 16), :]
        wait(recv_sem, 7, ret_in, (solvers - 1) * 12)

    @pl.when(jnp.logical_not(is_solver))
    def _():
        wait(recv_sem, 7, ret_in, solvers * 12)

    wait(recv_sem, 5, halo_in, 120)
    wait(recv_sem, 6, halo_in, 120)

    returns[...] = ret_in[...]
    ends[...] = halo_in[...]

    wait(send_sem, 0, tabs, (planes - 1) * 2 * VARS)
    wait(send_sem, 1, req, (slots - 1) * 2)
    wait(send_sem, 3, pick_in, (slots - 1) * VARS)
    wait(send_sem, 5, halo_in, 120)
    wait(send_sem, 6, halo_in, 120)
    wait(send_sem, 9, side_in, 24)
    wait(send_sem, 10, side_in, 48)

    @pl.when(is_solver)
    def _():
        wait(send_sem, 2, coef_in, (solvers - 1) * 8)
        wait(send_sem, 4, dat_in, (solvers - 1) * 16)
        wait(send_sem, 7, ret_out, (slabs - 1) * 12)

    @pl.when(jnp.logical_not(is_solver))
    def _():
        wait(send_sem, 2, coef_in, solvers * 8)
        wait(send_sem, 4, dat_in, solvers * 16)

    @pl.when(has_two(p))
    def _():
        wait(send_sem, 8, coef_in, (n_two - 1) * 8)

    @pl.when(jnp.logical_not(has_two(p)))
    def _():
        wait(send_sem, 8, coef_in, n_two * 8)


def finish(tiles, fbuf, xrow, crow, arow, returns, ends, scale, der, seg, x_out, y_out, srow, sem):
    E, H, RD = 16, 32, 48

    def one(v):
        def third(b, _):
            def at(row):
                return pl.ds(pl.multiple_of(row * 24 + b * 8, 8), 8)

            def natural(i):
                return pl.ds(((v * 2 + i // 8) * tiles + b) * 8 + i % 8, tiles // 3, stride=24)

            def const(k):
                return scale[pl.ds(k, 1), :]

            w = 5 * b + v

            def given(k):
                return returns[pl.ds((w // 3) * 16 + (w % 3) * 4 + k, 8, stride=80), :]

            left_c, right_c, t0, t1 = given(0), given(1), given(2), given(3)
            above = ends[at(v), :]
            below = ends[at(5 + v), :]
            run = None
            for i in range(ROWS):
                xi = xrow[at(v * ROWS + i), :] + const(i) * left_c + const(ROWS + i) * right_c
                if i == 0:
                    xi = xi + const(2 * ROWS) * below
                if i == ROWS - 1:
                    xi = xi + const(2 * ROWS + 1) * above
                x_out[natural(i), :] = xi[: tiles // 3]
                if i:
                    rhs = fbuf[at(v * ROWS + i), :] - crow[at(i), :] * xi
                    run = rhs if run is None else rhs + arow[at(E + i - 1), :] * run
                    srow[at(i), :] = arow[at(RD + i), :] * run + arow[at(H + i), :] * t0
            y = t1
            for i in range(ROWS - 1, 0, -1):
                y = srow[at(i), :] + arow[at(E + i), :] * y
                y_out[natural(i), :] = y[: tiles // 3]
            y_out[natural(0), :] = t0[: tiles // 3]
            return 0

        lax.fori_loop(0, 3, third, 0, unroll=3)

    rows = ROWS * tiles
    copies = []
    for v in range(VARS):
        one(v)
        part = pl.ds(v * rows, rows)
        for k, (src, dst) in enumerate(((x_out, der), (y_out, seg))):
            copies.append(pltpu.make_async_copy(src.at[part, :], dst.at[part, :], sem.at[k, v]))
            copies[-1].start()
    for copy in copies:
        copy.wait()


def solution(mesh):
    slabs, cross = mesh.shape["pipe"], mesh.shape["cross"]
    table, carry = derivative_constants(slabs)

    def local(state, face, courant, cell_mask, ghost_cell, ghost_owner, ghost_image, base, weight):
        pencils = state.shape[2]
        tiles = pencils // 128
        solvers = -(-(VARS * tiles) // UNITS)
        planes, slots = slabs // 2, cross * 2
        span = VARS * ROWS * 24

        def buf(rows, dtype=F32):
            return pltpu.VMEM((rows, 128), dtype)

        parts = pl.pallas_call(
            functools.partial(kernel, slabs, cross, tiles),
            out_shape=tuple(
                buf(n) for n in (span, span, ROWS * 24, ROWS * 24 * 6, max(640, solvers * 16), 240, 2 * ROWS + 8)
            ),
            in_specs=[pl.BlockSpec(memory_space=pl.ANY)] * 11,
            out_specs=(pl.BlockSpec(memory_space=pltpu.VMEM),) * 7,
            scratch_shapes=[
                pltpu.SMEM((1, 128), F32),
                pltpu.SMEM((1, IMAGES), I32),
                pltpu.VMEM((2 * slabs, slabs), F32),
                pltpu.VMEM((1, IMAGES), I32),
                pltpu.VMEM(state.shape, F32),
                pltpu.VMEM(face.shape, F32),
                pltpu.VMEM(face.shape, F32),
                pltpu.VMEM(face.shape, I32),
                pltpu.VMEM((1, GHOSTS), I32),
                pltpu.VMEM((1, GHOSTS), I32),
                pltpu.VMEM((1, GHOSTS), I32),
                pltpu.VMEM((8, IMAGES), F32),
                buf(ROWS * (tiles + 1) * 8),
                buf(2 * IMAGES),
                buf(IMAGES * 8),
                buf(planes * 16),
                buf(slots * 8, I32),
                buf(slots * 8),
                buf(slots * 8),
                buf(ROWS * 24, I32),
                buf(span),
                buf(192),
                buf(slabs * 16),
                buf(24 * slabs),
                buf(72),
                buf(72),
                buf(640),
                buf(slabs * 16),
                buf(slabs * 16),
                buf(max(640, solvers * 16)),
                buf(240),
                buf(240),
                pltpu.SemaphoreType.DMA((16,)),
                pltpu.SemaphoreType.DMA((11,)),
                pltpu.SemaphoreType.DMA((11,)),
            ],
            compiler_params=pltpu.CompilerParams(
                collective_id=0, has_side_effects=True, vmem_limit_bytes=59 * 1024 * 1024
            ),
        )(
            jnp.asarray(table).reshape(slabs, 1, 128), jnp.asarray(carry), base.reshape(1, -1),
            state, face, courant, cell_mask,
            ghost_cell.reshape(1, -1), ghost_owner.reshape(1, -1), ghost_image.reshape(1, -1), weight,
        )
        rows = VARS * ROWS * tiles
        results = pl.pallas_call(
            functools.partial(finish, tiles),
            out_shape=(jax.ShapeDtypeStruct((rows, 128), F32),) * 2,
            in_specs=[pl.BlockSpec(memory_space=pltpu.VMEM)] * 7,
            out_specs=(pl.BlockSpec(memory_space=pl.ANY),) * 2,
            scratch_shapes=[buf(rows), buf(rows), buf(ROWS * 24), pltpu.SemaphoreType.DMA((2, VARS))],
            compiler_params=pltpu.CompilerParams(vmem_limit_bytes=3 * 1024 * 1024),
        )(*parts)
        return tuple(
            x.reshape(VARS, 2, tiles, 8, 128).transpose(0, 1, 3, 2, 4).reshape(state.shape) for x in results
        )

    flat = P(("pipe", "cross"))
    slab = P("pipe", "cross")
    whole = P(None, "pipe", "cross")
    return jax.shard_map(
        local,
        mesh=mesh,
        in_specs=(whole, slab, slab, slab, flat, flat, flat, flat, P(None, ("pipe", "cross"))),
        out_specs=(whole, whole),
        check_vma=False,
    )
```

```python
import functools

import jax
import jax.numpy as jnp
import numpy as np
from jax import lax
from jax.experimental import pallas as pl
from jax.experimental.pallas import tpu as pltpu
from jax.sharding import PartitionSpec as P

VARS = 5
ROWS = 16
GHOSTS = 128
IMAGES = 256
UNITS = 3
IMAGE_BITS = (2, 1, 0, 6, 5, 4, 3)
REFLECT = (1.0, -1.0, -1.0, -1.0, 1.0)
F32 = jnp.float32
I32 = jnp.int32
MESH = pl.DeviceIdType.MESH

T_R = 0
T_S = 17
T_K = 34
T_U = 52
T_V = 68
T_H0 = 84
T_H1 = 87
T_H14 = 91
T_H15 = 95
T_D0, T_D15, T_DL, T_DR = 98, 99, 100, 101


def derivative_constants(slabs):
    n = slabs * ROWS
    side = np.full(n, 1.0 / 3.0)
    side[1] = side[n - 2] = 0.25
    side[0] = side[n - 1] = 0.0
    delta, eps = np.ones(n), np.ones(n)
    for k in range(n - 2, -1, -1):
        delta[k] = 1.0 - side[k] * side[k + 1] / delta[k + 1]
    for k in range(1, n):
        eps[k] = 1.0 - side[k] * side[k - 1] / eps[k - 1]
    r, s, e = -side / delta, -side / eps, 1.0 / (delta + eps - 1.0)

    def at(x, i):
        return x[i] if 0 <= i < n else 0.0

    table = np.zeros((slabs, 128))
    decay_l, decay_r = np.zeros(slabs), np.zeros(slabs)
    for p in range(slabs):
        g = p * ROWS
        row = table[p]
        kappa = {k: 25.0 / 36.0 * at(e, g + k) for k in range(-1, ROWS + 1)}
        for k in range(0, ROWS + 1):
            row[T_R + k] = at(r, g + k)
        for k in range(-1, ROWS):
            row[T_S + k + 1] = at(s, g + k)
        for k in range(-1, ROWS + 1):
            row[T_K + k + 1] = kappa[k]
        u = v = 1.0
        for k in range(ROWS):
            u = u * at(r, g + k) if k else 1.0
            row[T_U + k] = u
        for k in range(ROWS - 1, -1, -1):
            v = v * at(s, g + k) if k < ROWS - 1 else 1.0
            row[T_V + k] = v
        decay_l[p] = u * at(r, g + ROWS)
        decay_r[p] = v * at(s, g - 1)
        row[T_H0 : T_H0 + 3] = (0.0, kappa[0], 0.0)
        row[T_H1 : T_H1 + 4] = (-kappa[1], 0.0, kappa[1], 0.0)
        row[T_H14 : T_H14 + 4] = (0.0, -kappa[14], 0.0, kappa[14])
        row[T_H15 : T_H15 + 3] = (0.0, -kappa[15], 0.0)
        row[T_D0] = row[T_D15] = row[T_DR] = 1.0 / 12.0
        row[T_DL] = -1.0 / 12.0
        if p == 0:
            row[T_H0 : T_H0 + 3] = e[0] * np.array((-1.5, 2.0, -0.5))
            row[T_H1 : T_H1 + 4] = e[1] * np.array((-2.0 / 3.0, 1.0 / 48.0, 2.0 / 3.0, -1.0 / 48.0))
            row[T_D0] = row[T_DL] = 0.0
        if p == slabs - 1:
            row[T_H15 : T_H15 + 3] = e[n - 1] * np.array((0.5, -2.0, 1.5))
            row[T_H14 : T_H14 + 4] = e[n - 2] * np.array((1.0 / 48.0, -2.0 / 3.0, -1.0 / 48.0, 2.0 / 3.0))
            row[T_D15] = row[T_DR] = 0.0
    carry = np.zeros((2 * slabs, slabs))
    for p in range(slabs):
        w = 1.0
        for q in range(p - 1, -1, -1):
            carry[p, q] = w
            w *= decay_l[q]
        w = 1.0
        for q in range(p + 1, slabs):
            carry[slabs + p, q] = w
            w *= decay_r[q]
    return table.astype(np.float32), carry.astype(np.float32)


def kernel(
    slabs, cross, tiles,
    tab_hbm, lam_hbm, base_hbm, state_hbm, phi_hbm, cour_hbm, mask_hbm, gcell_hbm, gown_hbm, gimg_hbm, wts_hbm,
    fbuf, xrow, crow, arow, returns, ends, scale,
    tab, base_s, lam, base_v, state, phi, cour, mask, gcell, gown, gimg, wts,
    xbuf, win, stage, tabs, req, pick_out, pick_in, gmap, srow,
    coef_out, coef_in, fac, side_out, side_in, dat_out, dat_in, ret_out, ret_in, halo_out, halo_in,
    in_sem, send_sem, recv_sem,
):
    p = lax.axis_index("pipe")
    c = lax.axis_index("cross")
    yz, core = p // 2, p % 2
    planes = slabs // 2
    slot = c * 2 + core
    slots = cross * 2
    tp = tiles + 1
    magic = -(-65536 // tiles)
    solvers = -(-(VARS * tiles) // UNITS)
    is_solver = p < solvers
    before, after = lax.rem(p + slabs - 1, slabs), lax.rem(p + 1, slabs)

    def fetch(k, src, dst):
        copy = pltpu.make_async_copy(src, dst, in_sem.at[k])
        copy.start()
        return copy

    got_base = fetch(1, base_hbm, base_v)
    got_wts = fetch(3, wts_hbm, wts)
    got_state = [fetch(0, state_hbm, state)]
    got_base_s = fetch(2, base_hbm, base_s)
    barrier = pltpu.get_barrier_semaphore()

    def greet(i, _):
        pl.semaphore_signal(barrier, inc=1, device_id=(lax.rem(p + i, slabs), c), device_id_type=MESH)
        return 0

    lax.fori_loop(1, slabs, greet, 0, unroll=True)
    for dc in range(1, cross):
        for k in range(2):
            pl.semaphore_signal(
                barrier, inc=1, device_id=(yz * 2 + k, lax.rem(c + dc, cross)), device_id_type=MESH
            )

    got_rest = [
        fetch(4, mask_hbm, mask),
        fetch(5, phi_hbm, phi),
        fetch(6, cour_hbm, cour),
        fetch(7, gcell_hbm, gcell),
        fetch(8, gown_hbm, gown),
        fetch(9, gimg_hbm, gimg),
        fetch(10, tab_hbm.at[p], tab),
        fetch(11, lam_hbm, lam),
    ]

    def send(src, dst, sem, dev):
        pltpu.make_async_remote_copy(
            src_ref=src,
            dst_ref=dst,
            send_sem=send_sem.at[sem],
            recv_sem=recv_sem.at[sem],
            device_id=dev,
            device_id_type=MESH,
        ).start()

    def wait(sems, sem, ref, rows):
        part = ref.at[pl.ds(0, rows), :]
        pltpu.make_async_copy(part, part, sems.at[sem]).wait()

    def al(x):
        return pl.multiple_of(x, 8)

    lane = lax.broadcasted_iota(I32, (8, 128), 1)
    got_base.wait()
    got_wts.wait()
    spot = jnp.broadcast_to((base_v[...] & 127).astype(F32), (8, IMAGES)).T
    cols8 = wts[...].T
    for g in range(IMAGES // 8):
        here = spot[g * 8 : g * 8 + 8, 0:1].astype(I32)
        rel = (lane - here) & 127
        w = [jnp.broadcast_to(cols8[g * 8 : g * 8 + 8, k : k + 1], (8, 128)) for k in range(8)]
        for row in range(2):
            m = jnp.zeros((8, 128), F32)
            for k, off in enumerate((0, 1, 96, 97)):
                m = jnp.where(rel == off, w[row * 4 + k], m)
            win[pl.ds(row * IMAGES + g * 8, 8), :] = m

    for r in range(ROWS):
        xbuf[pl.ds((r * tp + tiles) * 8, 8), :] = jnp.zeros((8, 128), F32)
    for copy in got_state:
        copy.wait()
    for rt in range(2):
        for lt in range(tiles):
            for v in range(VARS):
                nat = state[v, pl.ds(rt * 8, 8), pl.ds(lt * 128, 128)]
                xbuf[pl.ds((rt * 8 * tp + lt) * 8 + v, 8, stride=tp * 8), :] = nat
    got_base_s.wait()
    blocks = xbuf.reshape(ROWS * tp, 8, 128)

    def merge(bit, a, b):
        low = ((lane >> bit) & 1) == 0
        return jnp.where(low, a, b) + pltpu.roll(jnp.where(low, b, a), 128 - (1 << bit), axis=1)

    def halves(bit, vals):
        n = len(vals) // 2
        return [merge(bit, vals[i], vals[i + n]) for i in range(n)]

    def image_group(g, _):
        m0 = win[pl.ds(al(g * 8), 8), :]
        m1 = win[pl.ds(al(IMAGES + g * 8), 8), :]
        vals = []
        for k in range(8):
            b = base_s[0, g * 8 + k]
            x = b >> 7
            r = (x * magic) >> 16
            off = x + r
            inside = lane >= (b & 127)
            z0 = jnp.where(inside, blocks[off], blocks[off + 1])
            z1 = jnp.where(inside, blocks[off + tp], blocks[off + tp + 1])
            stage[pl.ds(al(g * 64 + k * 8), 8), :] = z0 * m0[k : k + 1, :] + z1 * m1[k : k + 1, :]
        return 0

    lax.fori_loop(0, IMAGES // 8, image_group, 0, unroll=4)
    both = [[], []]
    for g in range(IMAGES // 8):
        vals = [stage[pl.ds(g * 64 + k * 8, 8), :] for k in range(8)]
        for bit in range(3):
            vals = halves(bit, vals)
        both[g // 16].append(vals[0])
    for bit in range(3, 7):
        both = [halves(bit, vals) for vals in both]
    sub = lax.broadcasted_iota(I32, (8, 128), 0)
    second = pltpu.roll(both[1][0], VARS, axis=0)
    tabs[pl.ds(al(yz * 16), 8), :] = jnp.where(sub < VARS, both[0][0], second)
    tabs[pl.ds(al(yz * 16 + 8), 8), :] = second

    for copy in got_rest:
        copy.wait()
    req[pl.ds(al(slot * 8), 8), :] = jnp.concatenate(
        [gown[...], gimg[...], jnp.zeros((6, GHOSTS), I32)], axis=0
    )

    pl.semaphore_wait(barrier, slabs - 1 + (cross - 1) * 2)

    def send_table(j, _):
        half = planes // 2
        d = lax.rem(yz + jnp.where(j < half, half + j, planes - 1 - j), planes)
        mine = pl.ds(al(yz * 16), 2 * VARS)
        send(tabs.at[mine, :], tabs.at[mine, :], 0, (d * 2 + core, c))
        return 0

    lax.fori_loop(0, planes - 1, send_table, 0, unroll=True)
    row_peers = [
        (yz * 2 + lax.rem(core + dk, 2), lax.rem(c + dc, cross))
        for dc in range(cross)
        for dk in range(2)
        if dc or dk
    ]
    for dev in row_peers:
        mine = pl.ds(al(slot * 8), 2)
        send(req.at[mine, :], req.at[mine, :], 1, dev)

    for rt in range(2):
        for lt in range(tiles):
            cols = pl.ds(lt * 128, 128)
            rows = pl.ds(rt * 8, 8)
            solid = mask[rows, cols] == 1
            place = (lt % 3) * 8 + lt // 3
            for v in range(VARS):
                fbuf[pl.ds((v * ROWS + rt * 8) * 24 + place, 8, stride=24), :] = jnp.where(
                    solid, 0.0, state[v, rows, cols]
                )
            crow[pl.ds(rt * 8 * 24 + place, 8, stride=24), :] = cour[rows, cols]
            arow[pl.ds(rt * 8 * 24 + place, 8, stride=24), :] = phi[rows, cols]

    cell = gcell[...]
    x = cell >> 7
    r = (x * magic) >> 16
    t = x - r * tiles
    t3 = (t * 21846) >> 16
    at_row = r * 24 + (t - t3 * 3) * 8 + t3
    ghost_no = (lax.broadcasted_iota(I32, (1, GHOSTS), 1) + 1).astype(F32)
    row_no = lax.broadcasted_iota(I32, (ROWS * 24, GHOSTS), 0)
    left = jnp.where(row_no == at_row, ghost_no, 0.0).astype(jnp.bfloat16)
    lane_no = lax.broadcasted_iota(I32, (128, GHOSTS), 0)
    right = jnp.where(lane_no == (cell & 127), 1.0, 0.0).astype(jnp.bfloat16)
    numbers = lax.dot_general(left, right, (((1,), (1,)), ((), ())), preferred_element_type=F32)
    gmap[...] = (numbers + 0.5).astype(I32) - 1

    def rowof(ref, i):
        return ref[pl.ds(i * 24, 24), :]

    def put(ref, i, val):
        ref[pl.ds(i * 24, 24), :] = val

    E, H, RD, WL, WR, C = 0, 16, 32, 48, 64, 80
    top = jnp.where(p == slabs - 1, 0.0, 1.0)
    h = rowof(arow, 0)
    m = jnp.ones_like(h)
    m_l = jnp.ones_like(h)
    faces = arow
    for k in range(1, ROWS):
        face = rowof(faces, k)
        if k == ROWS - 1:
            face = face * top
        rd = 1.0 / (h + face + m)
        e = face * rd
        hh = h * rd
        put(arow, 16 + E + k, e)
        put(arow, 16 + H + k, hh)
        put(arow, 16 + RD + k, rd)
        m_l = m_l + m * hh
        h = h * e
        m = 1.0 + m * e
    w_l = jnp.zeros_like(h)
    w_r = jnp.ones_like(h)
    cols = [jnp.zeros_like(h) for _ in range(4)]
    for k in range(ROWS - 1, 0, -1):
        e = rowof(arow, 16 + E + k)
        w_l = rowof(arow, 16 + H + k) + e * w_l
        w_r = e * w_r
        put(arow, 16 + WL + k, w_l)
        put(arow, 16 + WR + k, w_r)
        ck = rowof(crow, k)
        cl, cr = w_l * ck, w_r * ck
        u, v = tab[0, T_U + k], tab[0, T_V + k]
        cols = [cols[0] - u * cl, cols[1] - u * cr, cols[2] - v * cl, cols[3] - v * cr]
        if k == ROWS - 1:
            k1, k2 = -tab[0, T_DR] * cl, -tab[0, T_DR] * cr
    c0 = rowof(crow, 0)
    cols[0] = cols[0] - tab[0, T_U] * c0
    cols[2] = cols[2] - tab[0, T_V] * c0
    for k, val in enumerate((h, m_l, m - 1.0, *cols)):
        for b in range(3):
            coef_out[pl.ds(b * 8 + k, 8, stride=24), :] = val[b * 8 : b * 8 + 8, :]
    for k, val in enumerate((-tab[0, T_DL] * c0, k1, k2)):
        side_out[pl.ds(k * 24, 24), :] = val

    def first_tile(d):
        return (UNITS * d) // VARS

    def has_two(d):
        return jnp.logical_and(d < solvers, lax.rem(UNITS * d, VARS) > VARS - UNITS)

    n_two = sum((UNITS * d) % VARS > VARS - UNITS for d in range(solvers))

    def send_coef(i, _):
        d = lax.rem(p + i, slabs)

        @pl.when(d < solvers)
        def _():
            send(
                coef_out.at[pl.ds(al(first_tile(d) * 8), 8), :],
                coef_in.at[pl.ds(al(p * 16), 8), :],
                2,
                (d, c),
            )

        @pl.when(has_two(d))
        def _():
            send(
                coef_out.at[pl.ds(al(first_tile(d) * 8 + 8), 8), :],
                coef_in.at[pl.ds(al(p * 16 + 8), 8), :],
                8,
                (d, c),
            )

        return 0

    wait(recv_sem, 0, tabs, (planes - 1) * 2 * VARS)
    wait(recv_sem, 1, req, (slots - 1) * 2)
    owner = req[pl.ds(0, slots, stride=8), :]
    image = req[pl.ds(1, slots, stride=8), :]
    o_c = lax.rem(owner, cross)
    o_p = lax.div(owner, cross)
    held = jnp.logical_and(o_c == c, (o_p & 1) == core)
    which = jnp.where(held, (o_p >> 1) * 2 + (image >> 7), jnp.full_like(owner, -1))
    spot7 = jnp.zeros_like(image)
    for bit in range(7):
        spot7 = spot7 | (((image >> bit) & 1) << IMAGE_BITS[bit])
    tables = []
    for k in range(planes):
        first, second = tabs[pl.ds(k * 16, 8), :], tabs[pl.ds(k * 16 + 8, 8), :]
        back = 8 - VARS
        tables += [
            first,
            jnp.where(sub < back, pltpu.roll(first, back, axis=0), pltpu.roll(second, back, axis=0)),
        ]
    for n in range(slots):
        idx = jnp.broadcast_to(spot7[n : n + 1, :], (8, 128))
        wh = jnp.broadcast_to(which[n : n + 1, :], (8, 128))
        acc = jnp.zeros((8, 128), F32)
        for k in range(planes * 2):
            got = jnp.take_along_axis(tables[k], idx, axis=1, mode="promise_in_bounds")
            acc = jnp.where(wh == k, got, acc)
        pick_out[pl.ds(n * 8, 8), :] = acc

    for dev in row_peers:
        send(
            pick_out.at[pl.ds(al((dev[1] * 2 + lax.rem(dev[0], 2)) * 8), VARS), :],
            pick_in.at[pl.ds(al(slot * 8), VARS), :],
            3,
            dev,
        )
    pick_in[pl.ds(al(slot * 8), 8), :] = pick_out[pl.ds(al(slot * 8), 8), :]

    send(side_out.at[pl.ds(0, 24), :], side_in.at[pl.ds(0, 24), :], 9, (before, c))
    send(side_out.at[pl.ds(24, 48), :], side_in.at[pl.ds(24, 48), :], 10, (after, c))
    lax.fori_loop(1, slabs, send_coef, 0)

    @pl.when(is_solver)
    def _():
        coef_in[pl.ds(al(p * 16), 16), :] = coef_out[pl.ds(al(first_tile(p) * 8), 16), :]

    wait(recv_sem, 3, pick_in, (slots - 1) * VARS)
    ghost = pick_in[pl.ds(0, 8), :]
    for n in range(1, slots):
        ghost = ghost + pick_in[pl.ds(n * 8, 8), :]
    ghost = [jnp.broadcast_to(REFLECT[v] * ghost[v : v + 1, :], (8, 128)) for v in range(VARS)]

    def tv(i):
        return tab[0, i]

    wait(recv_sem, 9, side_in, 24)
    wait(recv_sem, 10, side_in, 48)

    def send_class(k):
        def one(i, _):
            d = 5 * lax.rem(p + i, tiles // 3) + k

            @pl.when(d != p)
            def _():
                send(
                    dat_out.at[pl.ds(al(d * 16), 16), :],
                    dat_in.at[pl.ds(al(p * 16), 16), :],
                    4,
                    (d, c),
                )

            return 0

        lax.fori_loop(0, tiles // 3, one, 0, unroll=True)

    for k in range(2 * ROWS):
        scale[pl.ds(k, 1), :] = jnp.full((1, 128), tv(T_U + k), F32)
    for k in range(2):
        scale[pl.ds(2 * ROWS + k, 1), :] = jnp.full((1, 128), tv(T_DL + k), F32)

    def local(b, _):
        def at(row):
            return pl.ds(al(row * 24 + b * 8), 8)

        def filled(i):
            gi = gmap[at(i), :]
            has = gi >= 0
            idx = jnp.maximum(gi, 0)
            out = []
            for v in range(VARS):
                got = jnp.take_along_axis(ghost[v], idx, axis=1, mode="promise_in_bounds")
                val = jnp.where(has, got, fbuf[at(v * ROWS + i), :])
                fbuf[at(v * ROWS + i), :] = val
                out.append(val)
            return out

        f = [filled(i) for i in range(ROWS)]
        for v in range(VARS):
            fv = [f[i][v] for i in range(ROWS)]
            up = tv(T_K) * fv[0]
            for i in range(ROWS):
                if i == 0:
                    hi = tv(T_H0) * fv[0] + tv(T_H0 + 1) * fv[1] + tv(T_H0 + 2) * fv[2]
                elif i == 1:
                    hi = sum(tv(T_H1 + k) * fv[k] for k in range(4))
                elif i == ROWS - 2:
                    hi = sum(tv(T_H14 + k) * fv[12 + k] for k in range(4))
                elif i == ROWS - 1:
                    hi = sum(tv(T_H15 + k) * fv[13 + k] for k in range(3))
                else:
                    hi = tv(T_K + 1 + i) * (fv[i + 1] - fv[i - 1])
                up = tv(T_R + i) * up + hi
                xrow[at(v * ROWS + i), :] = up
                srow[at(v * ROWS + i), :] = hi
            end = tv(T_K + 1 + ROWS) * fv[ROWS - 1]
            z_l = tv(T_R + ROWS) * up - end
            down = -end
            s_l = s_r = None
            for i in range(ROWS - 1, -1, -1):
                down = tv(T_S + 1 + i) * down
                xi = xrow[at(v * ROWS + i), :] + down
                if i == 0:
                    xi = xi + tv(T_D0) * fv[1]
                elif i == ROWS - 1:
                    xi = xi - tv(T_D15) * fv[ROWS - 2]
                else:
                    xi = xi + (1.0 / 12.0) * (fv[i + 1] - fv[i - 1])
                xrow[at(v * ROWS + i), :] = xi
                down = down + srow[at(v * ROWS + i), :]
                rhs = fv[i] - crow[at(i), :] * xi
                if i:
                    wl, wr = arow[at(16 + WL + i), :], arow[at(16 + WR + i), :]
                    s_l = wl * rhs if s_l is None else s_l + wl * rhs
                    s_r = wr * rhs if s_r is None else s_r + wr * rhs
                else:
                    s_l = s_l + rhs
            z_r = tv(T_S) * down + tv(T_K) * fv[0]
            s_r = s_r + side_in[at(0), :] * fv[ROWS - 1]
            s_b = side_in[at(1), :] * fv[0]
            s_l = s_l + side_in[at(2), :] * fv[0]
            w = 5 * b + v
            for k, val in enumerate((z_l, z_r, s_l, s_r, s_b)):
                dat_out[pl.ds((w // 3) * 16 + (w % 3) * 5 + k, 8, stride=80), :] = val
            halo_out[pl.ds(al(v * 24 + b * 8), 8), :] = fv[0]
            halo_out[pl.ds(al(120 + v * 24 + b * 8), 8), :] = fv[ROWS - 1]
        send_class(2 * b)

        @pl.when(b > 0)
        def _():
            send_class(2 * b - 1)

        return 0

    lax.fori_loop(0, 3, local, 0, unroll=3)

    @pl.when(is_solver)
    def _():
        wait(recv_sem, 2, coef_in, (slabs - 1) * 8)

        @pl.when(has_two(p))
        def _():
            wait(recv_sem, 8, coef_in, (slabs - 1) * 8)

        for j in range(2):

            def field(k):
                return coef_in[pl.ds(j * 8 + k, slabs, stride=16), :]

            gu = field(0)
            gl = pltpu.roll(gu, 1, axis=0)
            mm = field(1) + pltpu.roll(field(2), 1, axis=0)
            step, s = 0, 1
            while s < slabs:
                rd = 1.0 / (mm + gl + gu)
                pf = gl * pltpu.roll(rd, s, axis=0)
                tf = gu * pltpu.roll(rd, slabs - s, axis=0)
                at0 = ((j * 6 + step) * 2) * slabs
                fac[pl.ds(at0, slabs), :] = pf
                fac[pl.ds(at0 + slabs, slabs), :] = tf
                mm = mm + pf * pltpu.roll(mm, s, axis=0) + tf * pltpu.roll(mm, slabs - s, axis=0)
                gl = pf * pltpu.roll(gl, s, axis=0)
                gu = tf * pltpu.roll(gu, slabs - s, axis=0)
                step, s = step + 1, s * 2
            fac[pl.ds((j * 6 + 5) * 2 * slabs, slabs), :] = 1.0 / (mm + gl + gu)

    send(halo_out.at[pl.ds(0, 120), :], halo_in.at[pl.ds(0, 120), :], 5, (before, c))
    send(halo_out.at[pl.ds(120, 120), :], halo_in.at[pl.ds(120, 120), :], 6, (after, c))

    @pl.when(is_solver)
    def _():
        dat_in[pl.ds(al(p * 16), 16), :] = dat_out[pl.ds(al(p * 16), 16), :]
        wait(recv_sem, 4, dat_in, (slabs - 1) * 16)

        def data(u, k):
            return dat_in[pl.ds(u * 5 + k, slabs, stride=16), :]

        z_l = jnp.concatenate([data(u, 0) for u in range(UNITS)], axis=1)
        z_r = jnp.concatenate([data(u, 1) for u in range(UNITS)], axis=1)
        hi = lax.Precision.HIGHEST
        c_l = jnp.dot(lam[pl.ds(0, slabs), :], z_l, precision=hi, preferred_element_type=F32)
        c_r = jnp.dot(lam[pl.ds(slabs, slabs), :], z_r, precision=hi, preferred_element_type=F32)
        for u in range(UNITS):
            j = (UNITS * p + u) // VARS - first_tile(p)

            def field(k):
                return coef_in[pl.ds(j * 8 + k, slabs, stride=16), :]

            cl, cr = c_l[:, u * 128 : u * 128 + 128], c_r[:, u * 128 : u * 128 + 128]
            q = data(u, 3) + field(4) * cl + field(6) * cr
            d = data(u, 2) + field(3) * cl + field(5) * cr + pltpu.roll(data(u, 4), slabs - 1, axis=0)
            d = d + pltpu.roll(q, 1, axis=0)
            step, s = 0, 1
            while s < slabs:
                at0 = ((j * 6 + step) * 2) * slabs
                pf = fac[pl.ds(al(at0), slabs), :]
                tf = fac[pl.ds(al(at0 + slabs), slabs), :]
                d = d + pf * pltpu.roll(d, s, axis=0) + tf * pltpu.roll(d, slabs - s, axis=0)
                step, s = step + 1, s * 2
            x = d * fac[pl.ds(al((j * 6 + 5) * 2 * slabs), slabs), :]
            for k, val in enumerate((cl, cr, x, pltpu.roll(x, slabs - 1, axis=0))):
                ret_out[pl.ds(u * 4 + k, slabs, stride=16), :] = val

        def send_ret(i, _):
            d = lax.rem(p + i, slabs)
            send(ret_out.at[pl.ds(al(d * 16), 12), :], ret_in.at[pl.ds(al(p * 16), 12), :], 7, (d, c))
            return 0

        lax.fori_loop(1, slabs, send_ret, 0, unroll=4)
        ret_in[pl.ds(al(p * 16), 16), :] = ret_out[pl.ds(al(p * 16), 16), :]
        wait(recv_sem, 7, ret_in, (solvers - 1) * 12)

    @pl.when(jnp.logical_not(is_solver))
    def _():
        wait(recv_sem, 7, ret_in, solvers * 12)

    wait(recv_sem, 5, halo_in, 120)
    wait(recv_sem, 6, halo_in, 120)

    returns[...] = ret_in[...]
    ends[...] = halo_in[...]

    wait(send_sem, 0, tabs, (planes - 1) * 2 * VARS)
    wait(send_sem, 1, req, (slots - 1) * 2)
    wait(send_sem, 3, pick_in, (slots - 1) * VARS)
    wait(send_sem, 5, halo_in, 120)
    wait(send_sem, 6, halo_in, 120)
    wait(send_sem, 9, side_in, 24)
    wait(send_sem, 10, side_in, 48)

    @pl.when(is_solver)
    def _():
        wait(send_sem, 2, coef_in, (solvers - 1) * 8)
        wait(send_sem, 4, dat_in, (solvers - 1) * 16)
        wait(send_sem, 7, ret_out, (slabs - 1) * 12)

    @pl.when(jnp.logical_not(is_solver))
    def _():
        wait(send_sem, 2, coef_in, solvers * 8)
        wait(send_sem, 4, dat_in, solvers * 16)

    @pl.when(has_two(p))
    def _():
        wait(send_sem, 8, coef_in, (n_two - 1) * 8)

    @pl.when(jnp.logical_not(has_two(p)))
    def _():
        wait(send_sem, 8, coef_in, n_two * 8)


def finish(tiles, fbuf, xrow, crow, arow, returns, ends, scale, der, seg, x_out, y_out, srow, sem):
    E, H, RD = 16, 32, 48

    def one(v):
        def third(b, _):
            def at(row):
                return pl.ds(pl.multiple_of(row * 24 + b * 8, 8), 8)

            def natural(i):
                return pl.ds(((v * 2 + i // 8) * tiles + b) * 8 + i % 8, tiles // 3, stride=24)

            def const(k):
                return scale[pl.ds(k, 1), :]

            w = 5 * b + v

            def given(k):
                return returns[pl.ds((w // 3) * 16 + (w % 3) * 4 + k, 8, stride=80), :]

            left_c, right_c, t0, t1 = given(0), given(1), given(2), given(3)
            above = ends[at(v), :]
            below = ends[at(5 + v), :]
            run = None
            for i in range(ROWS):
                xi = xrow[at(v * ROWS + i), :] + const(i) * left_c + const(ROWS + i) * right_c
                if i == 0:
                    xi = xi + const(2 * ROWS) * below
                if i == ROWS - 1:
                    xi = xi + const(2 * ROWS + 1) * above
                x_out[natural(i), :] = xi[: tiles // 3]
                if i:
                    rhs = fbuf[at(v * ROWS + i), :] - crow[at(i), :] * xi
                    run = rhs if run is None else rhs + arow[at(E + i - 1), :] * run
                    srow[at(i), :] = arow[at(RD + i), :] * run + arow[at(H + i), :] * t0
            y = t1
            for i in range(ROWS - 1, 0, -1):
                y = srow[at(i), :] + arow[at(E + i), :] * y
                y_out[natural(i), :] = y[: tiles // 3]
            y_out[natural(0), :] = t0[: tiles // 3]
            return 0

        lax.fori_loop(0, 3, third, 0, unroll=3)

    rows = ROWS * tiles
    copies = []
    for v in range(VARS):
        one(v)
        part = pl.ds(v * rows, rows)
        for k, (src, dst) in enumerate(((x_out, der), (y_out, seg))):
            copies.append(pltpu.make_async_copy(src.at[part, :], dst.at[part, :], sem.at[k, v]))
            copies[-1].start()
    for copy in copies:
        copy.wait()


def solution(mesh):
    slabs, cross = mesh.shape["pipe"], mesh.shape["cross"]
    table, carry = derivative_constants(slabs)

    def local(state, face, courant, cell_mask, ghost_cell, ghost_owner, ghost_image, base, weight):
        pencils = state.shape[2]
        tiles = pencils // 128
        solvers = -(-(VARS * tiles) // UNITS)
        planes, slots = slabs // 2, cross * 2
        span = VARS * ROWS * 24

        def buf(rows, dtype=F32):
            return pltpu.VMEM((rows, 128), dtype)

        parts = pl.pallas_call(
            functools.partial(kernel, slabs, cross, tiles),
            out_shape=tuple(
                buf(n) for n in (span, span, ROWS * 24, ROWS * 24 * 6, max(640, solvers * 16), 240, 2 * ROWS + 8)
            ),
            in_specs=[pl.BlockSpec(memory_space=pl.ANY)] * 11,
            out_specs=(pl.BlockSpec(memory_space=pltpu.VMEM),) * 7,
            scratch_shapes=[
                pltpu.SMEM((1, 128), F32),
                pltpu.SMEM((1, IMAGES), I32),
                pltpu.VMEM((2 * slabs, slabs), F32),
                pltpu.VMEM((1, IMAGES), I32),
                pltpu.VMEM(state.shape, F32),
                pltpu.VMEM(face.shape, F32),
                pltpu.VMEM(face.shape, F32),
                pltpu.VMEM(face.shape, I32),
                pltpu.VMEM((1, GHOSTS), I32),
                pltpu.VMEM((1, GHOSTS), I32),
                pltpu.VMEM((1, GHOSTS), I32),
                pltpu.VMEM((8, IMAGES), F32),
                buf(ROWS * (tiles + 1) * 8),
                buf(2 * IMAGES),
                buf(IMAGES * 8),
                buf(planes * 16),
                buf(slots * 8, I32),
                buf(slots * 8),
                buf(slots * 8),
                buf(ROWS * 24, I32),
                buf(span),
                buf(192),
                buf(slabs * 16),
                buf(24 * slabs),
                buf(72),
                buf(72),
                buf(640),
                buf(slabs * 16),
                buf(slabs * 16),
                buf(max(640, solvers * 16)),
                buf(240),
                buf(240),
                pltpu.SemaphoreType.DMA((16,)),
                pltpu.SemaphoreType.DMA((11,)),
                pltpu.SemaphoreType.DMA((11,)),
            ],
            compiler_params=pltpu.CompilerParams(
                collective_id=0, has_side_effects=True, vmem_limit_bytes=59 * 1024 * 1024
            ),
        )(
            jnp.asarray(table).reshape(slabs, 1, 128), jnp.asarray(carry), base.reshape(1, -1),
            state, face, courant, cell_mask,
            ghost_cell.reshape(1, -1), ghost_owner.reshape(1, -1), ghost_image.reshape(1, -1), weight,
        )
        rows = VARS * ROWS * tiles
        results = pl.pallas_call(
            functools.partial(finish, tiles),
            out_shape=(jax.ShapeDtypeStruct((rows, 128), F32),) * 2,
            in_specs=[pl.BlockSpec(memory_space=pltpu.VMEM)] * 7,
            out_specs=(pl.BlockSpec(memory_space=pl.ANY),) * 2,
            scratch_shapes=[buf(rows), buf(rows), buf(ROWS * 24), pltpu.SemaphoreType.DMA((2, VARS))],
            compiler_params=pltpu.CompilerParams(vmem_limit_bytes=3 * 1024 * 1024),
        )(*parts)
        return tuple(
            x.reshape(VARS, 2, tiles, 8, 128).transpose(0, 1, 3, 2, 4).reshape(state.shape) for x in results
        )

    flat = P(("pipe", "cross"))
    slab = P("pipe", "cross")
    whole = P(None, "pipe", "cross")
    return jax.shard_map(
        local,
        mesh=mesh,
        in_specs=(whole, slab, slab, slab, flat, flat, flat, flat, P(None, ("pipe", "cross"))),
        out_specs=(whole, whole),
        check_vma=False,
    )
```

```python
import functools

import jax
import jax.numpy as jnp
import numpy as np
from jax import lax
from jax.experimental import pallas as pl
from jax.experimental.pallas import tpu as pltpu
from jax.sharding import PartitionSpec as P

VARS = 5
ROWS = 16
GHOSTS = 128
IMAGES = 256
UNITS = 3
IMAGE_BITS = (2, 1, 0, 6, 5, 4, 3)
REFLECT = (1.0, -1.0, -1.0, -1.0, 1.0)
F32 = jnp.float32
I32 = jnp.int32
MESH = pl.DeviceIdType.MESH

T_R = 0
T_S = 17
T_K = 34
T_U = 52
T_V = 68
T_H0 = 84
T_H1 = 87
T_H14 = 91
T_H15 = 95
T_D0, T_D15, T_DL, T_DR = 98, 99, 100, 101


def derivative_constants(slabs):
    n = slabs * ROWS
    side = np.full(n, 1.0 / 3.0)
    side[1] = side[n - 2] = 0.25
    side[0] = side[n - 1] = 0.0
    delta, eps = np.ones(n), np.ones(n)
    for k in range(n - 2, -1, -1):
        delta[k] = 1.0 - side[k] * side[k + 1] / delta[k + 1]
    for k in range(1, n):
        eps[k] = 1.0 - side[k] * side[k - 1] / eps[k - 1]
    r, s, e = -side / delta, -side / eps, 1.0 / (delta + eps - 1.0)

    def at(x, i):
        return x[i] if 0 <= i < n else 0.0

    table = np.zeros((slabs, 128))
    decay_l, decay_r = np.zeros(slabs), np.zeros(slabs)
    for p in range(slabs):
        g = p * ROWS
        row = table[p]
        kappa = {k: 25.0 / 36.0 * at(e, g + k) for k in range(-1, ROWS + 1)}
        for k in range(0, ROWS + 1):
            row[T_R + k] = at(r, g + k)
        for k in range(-1, ROWS):
            row[T_S + k + 1] = at(s, g + k)
        for k in range(-1, ROWS + 1):
            row[T_K + k + 1] = kappa[k]
        u = v = 1.0
        for k in range(ROWS):
            u = u * at(r, g + k) if k else 1.0
            row[T_U + k] = u
        for k in range(ROWS - 1, -1, -1):
            v = v * at(s, g + k) if k < ROWS - 1 else 1.0
            row[T_V + k] = v
        decay_l[p] = u * at(r, g + ROWS)
        decay_r[p] = v * at(s, g - 1)
        row[T_H0 : T_H0 + 3] = (0.0, kappa[0], 0.0)
        row[T_H1 : T_H1 + 4] = (-kappa[1], 0.0, kappa[1], 0.0)
        row[T_H14 : T_H14 + 4] = (0.0, -kappa[14], 0.0, kappa[14])
        row[T_H15 : T_H15 + 3] = (0.0, -kappa[15], 0.0)
        row[T_D0] = row[T_D15] = row[T_DR] = 1.0 / 12.0
        row[T_DL] = -1.0 / 12.0
        if p == 0:
            row[T_H0 : T_H0 + 3] = e[0] * np.array((-1.5, 2.0, -0.5))
            row[T_H1 : T_H1 + 4] = e[1] * np.array((-2.0 / 3.0, 1.0 / 48.0, 2.0 / 3.0, -1.0 / 48.0))
            row[T_D0] = row[T_DL] = 0.0
        if p == slabs - 1:
            row[T_H15 : T_H15 + 3] = e[n - 1] * np.array((0.5, -2.0, 1.5))
            row[T_H14 : T_H14 + 4] = e[n - 2] * np.array((1.0 / 48.0, -2.0 / 3.0, -1.0 / 48.0, 2.0 / 3.0))
            row[T_D15] = row[T_DR] = 0.0
    carry = np.zeros((2 * slabs, slabs))
    for p in range(slabs):
        w = 1.0
        for q in range(p - 1, -1, -1):
            carry[p, q] = w
            w *= decay_l[q]
        w = 1.0
        for q in range(p + 1, slabs):
            carry[slabs + p, q] = w
            w *= decay_r[q]
    return table.astype(np.float32), carry.astype(np.float32)


def kernel(
    slabs, cross, tiles,
    tab_hbm, lam_hbm, base_hbm, state_hbm, phi_hbm, cour_hbm, mask_hbm, gcell_hbm, gown_hbm, gimg_hbm, wts_hbm,
    fbuf, xrow, crow, arow, returns, ends, scale,
    tab, base_s, lam, base_v, state, phi, cour, mask, gcell, gown, gimg, wts,
    xbuf, win, stage, tabs, req, pick_out, pick_in, gmap, srow,
    coef_out, coef_in, fac, side_out, side_in, dat_out, dat_in, ret_out, ret_in, halo_out, halo_in,
    in_sem, send_sem, recv_sem,
):
    p = lax.axis_index("pipe")
    c = lax.axis_index("cross")
    yz, core = p // 2, p % 2
    planes = slabs // 2
    slot = c * 2 + core
    slots = cross * 2
    tp = tiles + 1
    magic = -(-65536 // tiles)
    solvers = -(-(VARS * tiles) // UNITS)
    is_solver = p < solvers
    before, after = lax.rem(p + slabs - 1, slabs), lax.rem(p + 1, slabs)

    def fetch(k, src, dst):
        copy = pltpu.make_async_copy(src, dst, in_sem.at[k])
        copy.start()
        return copy

    got_base = fetch(1, base_hbm, base_v)
    got_wts = fetch(3, wts_hbm, wts)
    got_state = [fetch(0, state_hbm, state)]
    got_base_s = fetch(2, base_hbm, base_s)
    barrier = pltpu.get_barrier_semaphore()

    def greet(i, _):
        pl.semaphore_signal(barrier, inc=1, device_id=(lax.rem(p + i, slabs), c), device_id_type=MESH)
        return 0

    lax.fori_loop(1, slabs, greet, 0, unroll=True)
    for dc in range(1, cross):
        for k in range(2):
            pl.semaphore_signal(
                barrier, inc=1, device_id=(yz * 2 + k, lax.rem(c + dc, cross)), device_id_type=MESH
            )

    got_rest = [
        fetch(4, mask_hbm, mask),
        fetch(5, phi_hbm, phi),
        fetch(6, cour_hbm, cour),
        fetch(7, gcell_hbm, gcell),
        fetch(8, gown_hbm, gown),
        fetch(9, gimg_hbm, gimg),
        fetch(10, tab_hbm.at[p], tab),
        fetch(11, lam_hbm, lam),
    ]

    def send(src, dst, sem, dev):
        pltpu.make_async_remote_copy(
            src_ref=src,
            dst_ref=dst,
            send_sem=send_sem.at[sem],
            recv_sem=recv_sem.at[sem],
            device_id=dev,
            device_id_type=MESH,
        ).start()

    def wait(sems, sem, ref, rows):
        part = ref.at[pl.ds(0, rows), :]
        pltpu.make_async_copy(part, part, sems.at[sem]).wait()

    def al(x):
        return pl.multiple_of(x, 8)

    lane = lax.broadcasted_iota(I32, (8, 128), 1)
    got_base.wait()
    got_wts.wait()
    spot = jnp.broadcast_to((base_v[...] & 127).astype(F32), (8, IMAGES)).T
    cols8 = wts[...].T
    for g in range(IMAGES // 8):
        here = spot[g * 8 : g * 8 + 8, 0:1].astype(I32)
        rel = (lane - here) & 127
        w = [jnp.broadcast_to(cols8[g * 8 : g * 8 + 8, k : k + 1], (8, 128)) for k in range(8)]
        for row in range(2):
            m = jnp.zeros((8, 128), F32)
            for k, off in enumerate((0, 1, 96, 97)):
                m = jnp.where(rel == off, w[row * 4 + k], m)
            win[pl.ds(row * IMAGES + g * 8, 8), :] = m

    for r in range(ROWS):
        xbuf[pl.ds((r * tp + tiles) * 8, 8), :] = jnp.zeros((8, 128), F32)
    for copy in got_state:
        copy.wait()
    for rt in range(2):
        for lt in range(tiles):
            for v in range(VARS):
                nat = state[v, pl.ds(rt * 8, 8), pl.ds(lt * 128, 128)]
                xbuf[pl.ds((rt * 8 * tp + lt) * 8 + v, 8, stride=tp * 8), :] = nat
    got_base_s.wait()
    blocks = xbuf.reshape(ROWS * tp, 8, 128)

    def merge(bit, a, b):
        low = ((lane >> bit) & 1) == 0
        return jnp.where(low, a, b) + pltpu.roll(jnp.where(low, b, a), 128 - (1 << bit), axis=1)

    def halves(bit, vals):
        n = len(vals) // 2
        return [merge(bit, vals[i], vals[i + n]) for i in range(n)]

    def image_group(g, _):
        m0 = win[pl.ds(al(g * 8), 8), :]
        m1 = win[pl.ds(al(IMAGES + g * 8), 8), :]
        vals = []
        for k in range(8):
            b = base_s[0, g * 8 + k]
            x = b >> 7
            r = (x * magic) >> 16
            off = x + r
            inside = lane >= (b & 127)
            z0 = jnp.where(inside, blocks[off], blocks[off + 1])
            z1 = jnp.where(inside, blocks[off + tp], blocks[off + tp + 1])
            stage[pl.ds(al(g * 64 + k * 8), 8), :] = z0 * m0[k : k + 1, :] + z1 * m1[k : k + 1, :]
        return 0

    lax.fori_loop(0, IMAGES // 8, image_group, 0, unroll=4)
    both = [[], []]
    for g in range(IMAGES // 8):
        vals = [stage[pl.ds(g * 64 + k * 8, 8), :] for k in range(8)]
        for bit in range(3):
            vals = halves(bit, vals)
        both[g // 16].append(vals[0])
    for bit in range(3, 7):
        both = [halves(bit, vals) for vals in both]
    sub = lax.broadcasted_iota(I32, (8, 128), 0)
    second = pltpu.roll(both[1][0], VARS, axis=0)
    tabs[pl.ds(al(yz * 16), 8), :] = jnp.where(sub < VARS, both[0][0], second)
    tabs[pl.ds(al(yz * 16 + 8), 8), :] = second

    for copy in got_rest:
        copy.wait()
    req[pl.ds(al(slot * 8), 8), :] = jnp.concatenate(
        [gown[...], gimg[...], jnp.zeros((6, GHOSTS), I32)], axis=0
    )

    pl.semaphore_wait(barrier, slabs - 1 + (cross - 1) * 2)

    def send_table(j, _):
        half = planes // 2
        d = lax.rem(yz + jnp.where(j < half, half + j, planes - 1 - j), planes)
        mine = pl.ds(al(yz * 16), 2 * VARS)
        send(tabs.at[mine, :], tabs.at[mine, :], 0, (d * 2 + core, c))
        return 0

    lax.fori_loop(0, planes - 1, send_table, 0, unroll=True)
    row_peers = [
        (yz * 2 + lax.rem(core + dk, 2), lax.rem(c + dc, cross))
        for dc in range(cross)
        for dk in range(2)
        if dc or dk
    ]
    for dev in row_peers:
        mine = pl.ds(al(slot * 8), 2)
        send(req.at[mine, :], req.at[mine, :], 1, dev)

    for rt in range(2):
        for lt in range(tiles):
            cols = pl.ds(lt * 128, 128)
            rows = pl.ds(rt * 8, 8)
            solid = mask[rows, cols] == 1
            place = (lt % 3) * 8 + lt // 3
            for v in range(VARS):
                fbuf[pl.ds((v * ROWS + rt * 8) * 24 + place, 8, stride=24), :] = jnp.where(
                    solid, 0.0, state[v, rows, cols]
                )
            crow[pl.ds(rt * 8 * 24 + place, 8, stride=24), :] = cour[rows, cols]
            arow[pl.ds(rt * 8 * 24 + place, 8, stride=24), :] = phi[rows, cols]

    cell = gcell[...]
    x = cell >> 7
    r = (x * magic) >> 16
    t = x - r * tiles
    t3 = (t * 21846) >> 16
    at_row = r * 24 + (t - t3 * 3) * 8 + t3
    ghost_no = (lax.broadcasted_iota(I32, (1, GHOSTS), 1) + 1).astype(F32)
    row_no = lax.broadcasted_iota(I32, (ROWS * 24, GHOSTS), 0)
    left = jnp.where(row_no == at_row, ghost_no, 0.0).astype(jnp.bfloat16)
    lane_no = lax.broadcasted_iota(I32, (128, GHOSTS), 0)
    right = jnp.where(lane_no == (cell & 127), 1.0, 0.0).astype(jnp.bfloat16)
    numbers = lax.dot_general(left, right, (((1,), (1,)), ((), ())), preferred_element_type=F32)
    gmap[...] = (numbers + 0.5).astype(I32) - 1

    def rowof(ref, i):
        return ref[pl.ds(i * 24, 24), :]

    def put(ref, i, val):
        ref[pl.ds(i * 24, 24), :] = val

    E, H, RD, WL, WR, C = 0, 16, 32, 48, 64, 80
    top = jnp.where(p == slabs - 1, 0.0, 1.0)
    h = rowof(arow, 0)
    m = jnp.ones_like(h)
    m_l = jnp.ones_like(h)
    faces = arow
    for k in range(1, ROWS):
        face = rowof(faces, k)
        if k == ROWS - 1:
            face = face * top
        rd = 1.0 / (h + face + m)
        e = face * rd
        hh = h * rd
        put(arow, 16 + E + k, e)
        put(arow, 16 + H + k, hh)
        put(arow, 16 + RD + k, rd)
        m_l = m_l + m * hh
        h = h * e
        m = 1.0 + m * e
    w_l = jnp.zeros_like(h)
    w_r = jnp.ones_like(h)
    cols = [jnp.zeros_like(h) for _ in range(4)]
    for k in range(ROWS - 1, 0, -1):
        e = rowof(arow, 16 + E + k)
        w_l = rowof(arow, 16 + H + k) + e * w_l
        w_r = e * w_r
        put(arow, 16 + WL + k, w_l)
        put(arow, 16 + WR + k, w_r)
        ck = rowof(crow, k)
        cl, cr = w_l * ck, w_r * ck
        u, v = tab[0, T_U + k], tab[0, T_V + k]
        cols = [cols[0] - u * cl, cols[1] - u * cr, cols[2] - v * cl, cols[3] - v * cr]
        if k == ROWS - 1:
            k1, k2 = -tab[0, T_DR] * cl, -tab[0, T_DR] * cr
    c0 = rowof(crow, 0)
    cols[0] = cols[0] - tab[0, T_U] * c0
    cols[2] = cols[2] - tab[0, T_V] * c0
    for k, val in enumerate((h, m_l, m - 1.0, *cols)):
        for b in range(3):
            coef_out[pl.ds(b * 8 + k, 8, stride=24), :] = val[b * 8 : b * 8 + 8, :]
    for k, val in enumerate((-tab[0, T_DL] * c0, k1, k2)):
        side_out[pl.ds(k * 24, 24), :] = val

    def first_tile(d):
        return (UNITS * d) // VARS

    def has_two(d):
        return jnp.logical_and(d < solvers, lax.rem(UNITS * d, VARS) > VARS - UNITS)

    n_two = sum((UNITS * d) % VARS > VARS - UNITS for d in range(solvers))

    def send_coef(i, _):
        d = lax.rem(p + i, slabs)

        @pl.when(d < solvers)
        def _():
            send(
                coef_out.at[pl.ds(al(first_tile(d) * 8), 8), :],
                coef_in.at[pl.ds(al(p * 16), 8), :],
                2,
                (d, c),
            )

        @pl.when(has_two(d))
        def _():
            send(
                coef_out.at[pl.ds(al(first_tile(d) * 8 + 8), 8), :],
                coef_in.at[pl.ds(al(p * 16 + 8), 8), :],
                8,
                (d, c),
            )

        return 0

    wait(recv_sem, 0, tabs, (planes - 1) * 2 * VARS)
    wait(recv_sem, 1, req, (slots - 1) * 2)
    owner = req[pl.ds(0, slots, stride=8), :]
    image = req[pl.ds(1, slots, stride=8), :]
    o_c = lax.rem(owner, cross)
    o_p = lax.div(owner, cross)
    held = jnp.logical_and(o_c == c, (o_p & 1) == core)
    which = jnp.where(held, (o_p >> 1) * 2 + (image >> 7), jnp.full_like(owner, -1))
    spot7 = jnp.zeros_like(image)
    for bit in range(7):
        spot7 = spot7 | (((image >> bit) & 1) << IMAGE_BITS[bit])
    tables = []
    for k in range(planes):
        first, second = tabs[pl.ds(k * 16, 8), :], tabs[pl.ds(k * 16 + 8, 8), :]
        back = 8 - VARS
        tables += [
            first,
            jnp.where(sub < back, pltpu.roll(first, back, axis=0), pltpu.roll(second, back, axis=0)),
        ]
    for n in range(slots):
        idx = jnp.broadcast_to(spot7[n : n + 1, :], (8, 128))
        wh = jnp.broadcast_to(which[n : n + 1, :], (8, 128))
        acc = jnp.zeros((8, 128), F32)
        for k in range(planes * 2):
            got = jnp.take_along_axis(tables[k], idx, axis=1, mode="promise_in_bounds")
            acc = jnp.where(wh == k, got, acc)
        pick_out[pl.ds(n * 8, 8), :] = acc

    for dev in row_peers:
        send(
            pick_out.at[pl.ds(al((dev[1] * 2 + lax.rem(dev[0], 2)) * 8), VARS), :],
            pick_in.at[pl.ds(al(slot * 8), VARS), :],
            3,
            dev,
        )
    pick_in[pl.ds(al(slot * 8), 8), :] = pick_out[pl.ds(al(slot * 8), 8), :]

    send(side_out.at[pl.ds(0, 24), :], side_in.at[pl.ds(0, 24), :], 9, (before, c))
    send(side_out.at[pl.ds(24, 48), :], side_in.at[pl.ds(24, 48), :], 10, (after, c))
    lax.fori_loop(1, slabs, send_coef, 0)

    @pl.when(is_solver)
    def _():
        coef_in[pl.ds(al(p * 16), 16), :] = coef_out[pl.ds(al(first_tile(p) * 8), 16), :]

    wait(recv_sem, 3, pick_in, (slots - 1) * VARS)
    ghost = pick_in[pl.ds(0, 8), :]
    for n in range(1, slots):
        ghost = ghost + pick_in[pl.ds(n * 8, 8), :]
    ghost = [jnp.broadcast_to(REFLECT[v] * ghost[v : v + 1, :], (8, 128)) for v in range(VARS)]

    def tv(i):
        return tab[0, i]

    wait(recv_sem, 9, side_in, 24)
    wait(recv_sem, 10, side_in, 48)

    def send_class(k):
        def one(i, _):
            d = 5 * lax.rem(p + i, tiles // 3) + k

            @pl.when(d != p)
            def _():
                send(
                    dat_out.at[pl.ds(al(d * 16), 16), :],
                    dat_in.at[pl.ds(al(p * 16), 16), :],
                    4,
                    (d, c),
                )

            return 0

        lax.fori_loop(0, tiles // 3, one, 0, unroll=True)

    for k in range(2 * ROWS):
        scale[pl.ds(k, 1), :] = jnp.full((1, 128), tv(T_U + k), F32)
    for k in range(2):
        scale[pl.ds(2 * ROWS + k, 1), :] = jnp.full((1, 128), tv(T_DL + k), F32)

    def local(b, _):
        def at(row):
            return pl.ds(al(row * 24 + b * 8), 8)

        def filled(i):
            gi = gmap[at(i), :]
            has = gi >= 0
            idx = jnp.maximum(gi, 0)
            out = []
            for v in range(VARS):
                got = jnp.take_along_axis(ghost[v], idx, axis=1, mode="promise_in_bounds")
                val = jnp.where(has, got, fbuf[at(v * ROWS + i), :])
                fbuf[at(v * ROWS + i), :] = val
                out.append(val)
            return out

        f = [filled(i) for i in range(ROWS)]
        for v in range(VARS):
            fv = [f[i][v] for i in range(ROWS)]
            up = tv(T_K) * fv[0]
            for i in range(ROWS):
                if i == 0:
                    hi = tv(T_H0) * fv[0] + tv(T_H0 + 1) * fv[1] + tv(T_H0 + 2) * fv[2]
                elif i == 1:
                    hi = sum(tv(T_H1 + k) * fv[k] for k in range(4))
                elif i == ROWS - 2:
                    hi = sum(tv(T_H14 + k) * fv[12 + k] for k in range(4))
                elif i == ROWS - 1:
                    hi = sum(tv(T_H15 + k) * fv[13 + k] for k in range(3))
                else:
                    hi = tv(T_K + 1 + i) * (fv[i + 1] - fv[i - 1])
                up = tv(T_R + i) * up + hi
                xrow[at(v * ROWS + i), :] = up
                srow[at(v * ROWS + i), :] = hi
            end = tv(T_K + 1 + ROWS) * fv[ROWS - 1]
            z_l = tv(T_R + ROWS) * up - end
            down = -end
            s_l = s_r = None
            for i in range(ROWS - 1, -1, -1):
                down = tv(T_S + 1 + i) * down
                xi = xrow[at(v * ROWS + i), :] + down
                if i == 0:
                    xi = xi + tv(T_D0) * fv[1]
                elif i == ROWS - 1:
                    xi = xi - tv(T_D15) * fv[ROWS - 2]
                else:
                    xi = xi + (1.0 / 12.0) * (fv[i + 1] - fv[i - 1])
                xrow[at(v * ROWS + i), :] = xi
                down = down + srow[at(v * ROWS + i), :]
                rhs = fv[i] - crow[at(i), :] * xi
                if i:
                    wl, wr = arow[at(16 + WL + i), :], arow[at(16 + WR + i), :]
                    s_l = wl * rhs if s_l is None else s_l + wl * rhs
                    s_r = wr * rhs if s_r is None else s_r + wr * rhs
                else:
                    s_l = s_l + rhs
            z_r = tv(T_S) * down + tv(T_K) * fv[0]
            s_r = s_r + side_in[at(0), :] * fv[ROWS - 1]
            s_b = side_in[at(1), :] * fv[0]
            s_l = s_l + side_in[at(2), :] * fv[0]
            w = 5 * b + v
            for k, val in enumerate((z_l, z_r, s_l, s_r, s_b)):
                dat_out[pl.ds((w // 3) * 16 + (w % 3) * 5 + k, 8, stride=80), :] = val
            halo_out[pl.ds(al(v * 24 + b * 8), 8), :] = fv[0]
            halo_out[pl.ds(al(120 + v * 24 + b * 8), 8), :] = fv[ROWS - 1]
        send_class(2 * b)

        @pl.when(b > 0)
        def _():
            send_class(2 * b - 1)

        return 0

    lax.fori_loop(0, 3, local, 0, unroll=3)

    @pl.when(is_solver)
    def _():
        wait(recv_sem, 2, coef_in, (slabs - 1) * 8)

        @pl.when(has_two(p))
        def _():
            wait(recv_sem, 8, coef_in, (slabs - 1) * 8)

        for j in range(2):

            def field(k):
                return coef_in[pl.ds(j * 8 + k, slabs, stride=16), :]

            gu = field(0)
            gl = pltpu.roll(gu, 1, axis=0)
            mm = field(1) + pltpu.roll(field(2), 1, axis=0)
            step, s = 0, 1
            while s < slabs:
                rd = 1.0 / (mm + gl + gu)
                pf = gl * pltpu.roll(rd, s, axis=0)
                tf = gu * pltpu.roll(rd, slabs - s, axis=0)
                at0 = ((j * 6 + step) * 2) * slabs
                fac[pl.ds(at0, slabs), :] = pf
                fac[pl.ds(at0 + slabs, slabs), :] = tf
                mm = mm + pf * pltpu.roll(mm, s, axis=0) + tf * pltpu.roll(mm, slabs - s, axis=0)
                gl = pf * pltpu.roll(gl, s, axis=0)
                gu = tf * pltpu.roll(gu, slabs - s, axis=0)
                step, s = step + 1, s * 2
            fac[pl.ds((j * 6 + 5) * 2 * slabs, slabs), :] = 1.0 / (mm + gl + gu)

    send(halo_out.at[pl.ds(0, 120), :], halo_in.at[pl.ds(0, 120), :], 5, (before, c))
    send(halo_out.at[pl.ds(120, 120), :], halo_in.at[pl.ds(120, 120), :], 6, (after, c))

    @pl.when(is_solver)
    def _():
        dat_in[pl.ds(al(p * 16), 16), :] = dat_out[pl.ds(al(p * 16), 16), :]
        wait(recv_sem, 4, dat_in, (slabs - 1) * 16)

        def data(u, k):
            return dat_in[pl.ds(u * 5 + k, slabs, stride=16), :]

        z_l = jnp.concatenate([data(u, 0) for u in range(UNITS)], axis=1)
        z_r = jnp.concatenate([data(u, 1) for u in range(UNITS)], axis=1)
        hi = lax.Precision.HIGHEST
        c_l = jnp.dot(lam[pl.ds(0, slabs), :], z_l, precision=hi, preferred_element_type=F32)
        c_r = jnp.dot(lam[pl.ds(slabs, slabs), :], z_r, precision=hi, preferred_element_type=F32)
        for u in range(UNITS):
            j = (UNITS * p + u) // VARS - first_tile(p)

            def field(k):
                return coef_in[pl.ds(j * 8 + k, slabs, stride=16), :]

            cl, cr = c_l[:, u * 128 : u * 128 + 128], c_r[:, u * 128 : u * 128 + 128]
            q = data(u, 3) + field(4) * cl + field(6) * cr
            d = data(u, 2) + field(3) * cl + field(5) * cr + pltpu.roll(data(u, 4), slabs - 1, axis=0)
            d = d + pltpu.roll(q, 1, axis=0)
            step, s = 0, 1
            while s < slabs:
                at0 = ((j * 6 + step) * 2) * slabs
                pf = fac[pl.ds(al(at0), slabs), :]
                tf = fac[pl.ds(al(at0 + slabs), slabs), :]
                d = d + pf * pltpu.roll(d, s, axis=0) + tf * pltpu.roll(d, slabs - s, axis=0)
                step, s = step + 1, s * 2
            x = d * fac[pl.ds(al((j * 6 + 5) * 2 * slabs), slabs), :]
            for k, val in enumerate((cl, cr, x, pltpu.roll(x, slabs - 1, axis=0))):
                ret_out[pl.ds(u * 4 + k, slabs, stride=16), :] = val

        def send_ret(i, _):
            d = lax.rem(p + i, slabs)
            send(ret_out.at[pl.ds(al(d * 16), 12), :], ret_in.at[pl.ds(al(p * 16), 12), :], 7, (d, c))
            return 0

        lax.fori_loop(1, slabs, send_ret, 0, unroll=True)
        ret_in[pl.ds(al(p * 16), 16), :] = ret_out[pl.ds(al(p * 16), 16), :]
        wait(recv_sem, 7, ret_in, (solvers - 1) * 12)

    @pl.when(jnp.logical_not(is_solver))
    def _():
        wait(recv_sem, 7, ret_in, solvers * 12)

    wait(recv_sem, 5, halo_in, 120)
    wait(recv_sem, 6, halo_in, 120)

    returns[...] = ret_in[...]
    ends[...] = halo_in[...]

    wait(send_sem, 0, tabs, (planes - 1) * 2 * VARS)
    wait(send_sem, 1, req, (slots - 1) * 2)
    wait(send_sem, 3, pick_in, (slots - 1) * VARS)
    wait(send_sem, 5, halo_in, 120)
    wait(send_sem, 6, halo_in, 120)
    wait(send_sem, 9, side_in, 24)
    wait(send_sem, 10, side_in, 48)

    @pl.when(is_solver)
    def _():
        wait(send_sem, 2, coef_in, (solvers - 1) * 8)
        wait(send_sem, 4, dat_in, (solvers - 1) * 16)
        wait(send_sem, 7, ret_out, (slabs - 1) * 12)

    @pl.when(jnp.logical_not(is_solver))
    def _():
        wait(send_sem, 2, coef_in, solvers * 8)
        wait(send_sem, 4, dat_in, solvers * 16)

    @pl.when(has_two(p))
    def _():
        wait(send_sem, 8, coef_in, (n_two - 1) * 8)

    @pl.when(jnp.logical_not(has_two(p)))
    def _():
        wait(send_sem, 8, coef_in, n_two * 8)


def finish(tiles, fbuf, xrow, crow, arow, returns, ends, scale, der, seg, x_out, y_out, srow, sem):
    E, H, RD = 16, 32, 48

    def one(v):
        def third(b, _):
            def at(row):
                return pl.ds(pl.multiple_of(row * 24 + b * 8, 8), 8)

            def natural(i):
                return pl.ds(((v * 2 + i // 8) * tiles + b) * 8 + i % 8, tiles // 3, stride=24)

            def const(k):
                return scale[pl.ds(k, 1), :]

            w = 5 * b + v

            def given(k):
                return returns[pl.ds((w // 3) * 16 + (w % 3) * 4 + k, 8, stride=80), :]

            left_c, right_c, t0, t1 = given(0), given(1), given(2), given(3)
            above = ends[at(v), :]
            below = ends[at(5 + v), :]
            run = None
            for i in range(ROWS):
                xi = xrow[at(v * ROWS + i), :] + const(i) * left_c + const(ROWS + i) * right_c
                if i == 0:
                    xi = xi + const(2 * ROWS) * below
                if i == ROWS - 1:
                    xi = xi + const(2 * ROWS + 1) * above
                x_out[natural(i), :] = xi[: tiles // 3]
                if i:
                    rhs = fbuf[at(v * ROWS + i), :] - crow[at(i), :] * xi
                    run = rhs if run is None else rhs + arow[at(E + i - 1), :] * run
                    srow[at(i), :] = arow[at(RD + i), :] * run + arow[at(H + i), :] * t0
            y = t1
            for i in range(ROWS - 1, 0, -1):
                y = srow[at(i), :] + arow[at(E + i), :] * y
                y_out[natural(i), :] = y[: tiles // 3]
            y_out[natural(0), :] = t0[: tiles // 3]
            return 0

        lax.fori_loop(0, 3, third, 0, unroll=3)

    rows = ROWS * tiles
    copies = []
    for v in range(VARS):
        one(v)
        part = pl.ds(v * rows, rows)
        for k, (src, dst) in enumerate(((x_out, der), (y_out, seg))):
            copies.append(pltpu.make_async_copy(src.at[part, :], dst.at[part, :], sem.at[k, v]))
            copies[-1].start()
    for copy in copies:
        copy.wait()


def solution(mesh):
    slabs, cross = mesh.shape["pipe"], mesh.shape["cross"]
    table, carry = derivative_constants(slabs)

    def local(state, face, courant, cell_mask, ghost_cell, ghost_owner, ghost_image, base, weight):
        pencils = state.shape[2]
        tiles = pencils // 128
        solvers = -(-(VARS * tiles) // UNITS)
        planes, slots = slabs // 2, cross * 2
        span = VARS * ROWS * 24

        def buf(rows, dtype=F32):
            return pltpu.VMEM((rows, 128), dtype)

        parts = pl.pallas_call(
            functools.partial(kernel, slabs, cross, tiles),
            out_shape=tuple(
                buf(n) for n in (span, span, ROWS * 24, ROWS * 24 * 6, max(640, solvers * 16), 240, 2 * ROWS + 8)
            ),
            in_specs=[pl.BlockSpec(memory_space=pl.ANY)] * 11,
            out_specs=(pl.BlockSpec(memory_space=pltpu.VMEM),) * 7,
            scratch_shapes=[
                pltpu.SMEM((1, 128), F32),
                pltpu.SMEM((1, IMAGES), I32),
                pltpu.VMEM((2 * slabs, slabs), F32),
                pltpu.VMEM((1, IMAGES), I32),
                pltpu.VMEM(state.shape, F32),
                pltpu.VMEM(face.shape, F32),
                pltpu.VMEM(face.shape, F32),
                pltpu.VMEM(face.shape, I32),
                pltpu.VMEM((1, GHOSTS), I32),
                pltpu.VMEM((1, GHOSTS), I32),
                pltpu.VMEM((1, GHOSTS), I32),
                pltpu.VMEM((8, IMAGES), F32),
                buf(ROWS * (tiles + 1) * 8),
                buf(2 * IMAGES),
                buf(IMAGES * 8),
                buf(planes * 16),
                buf(slots * 8, I32),
                buf(slots * 8),
                buf(slots * 8),
                buf(ROWS * 24, I32),
                buf(span),
                buf(192),
                buf(slabs * 16),
                buf(24 * slabs),
                buf(72),
                buf(72),
                buf(640),
                buf(slabs * 16),
                buf(slabs * 16),
                buf(max(640, solvers * 16)),
                buf(240),
                buf(240),
                pltpu.SemaphoreType.DMA((16,)),
                pltpu.SemaphoreType.DMA((11,)),
                pltpu.SemaphoreType.DMA((11,)),
            ],
            compiler_params=pltpu.CompilerParams(
                collective_id=0, has_side_effects=True, vmem_limit_bytes=59 * 1024 * 1024
            ),
        )(
            jnp.asarray(table).reshape(slabs, 1, 128), jnp.asarray(carry), base.reshape(1, -1),
            state, face, courant, cell_mask,
            ghost_cell.reshape(1, -1), ghost_owner.reshape(1, -1), ghost_image.reshape(1, -1), weight,
        )
        rows = VARS * ROWS * tiles
        results = pl.pallas_call(
            functools.partial(finish, tiles),
            out_shape=(jax.ShapeDtypeStruct((rows, 128), F32),) * 2,
            in_specs=[pl.BlockSpec(memory_space=pltpu.VMEM)] * 7,
            out_specs=(pl.BlockSpec(memory_space=pl.ANY),) * 2,
            scratch_shapes=[buf(rows), buf(rows), buf(ROWS * 24), pltpu.SemaphoreType.DMA((2, VARS))],
            compiler_params=pltpu.CompilerParams(vmem_limit_bytes=3 * 1024 * 1024),
        )(*parts)
        return tuple(
            x.reshape(VARS, 2, tiles, 8, 128).transpose(0, 1, 3, 2, 4).reshape(state.shape) for x in results
        )

    flat = P(("pipe", "cross"))
    slab = P("pipe", "cross")
    whole = P(None, "pipe", "cross")
    return jax.shard_map(
        local,
        mesh=mesh,
        in_specs=(whole, slab, slab, slab, flat, flat, flat, flat, P(None, ("pipe", "cross"))),
        out_specs=(whole, whole),
        check_vma=False,
    )
```
